128 devices in a mesh: group: 4 (over y), dev: 32 (over z, x, core).
Axes of the slice: x: 4, y: 4, z: 4, core: 2. Of those that a mesh axis runs over, the one named last changes fastest.
Arguments:
- atom_rows: float32 [4, 262144], P(None, ('group', 'dev')), may hold values from -0.5 to 0.5
- atom_owner: int32 [262144], P(('group', 'dev')), may hold values from 0 to 127, as said below
- atom_cell: int32 [262144], P(('group', 'dev')), may hold values from 0 to 1023
- need_cells: int32 [128, 128, 72], P(('group', 'dev')), may hold values from -1 to 1023, as said below
- list_entry: int32 [16, 131072], P(None, ('group', 'dev')), may hold values from 0 to 10239, as said below
- list_class: int32 [16, 131072], P(None, ('group', 'dev')), may hold values from 0 to 7
- basis_freq: float32 [121, 3], replicated, may hold values from -4 to 4
- basis_phase: float32 [121], replicated, may hold values from -3.140625 to 3.140625
- near_ops: float32 [8, 121, 121], replicated, may hold values from -0.125 to 0.125
- up_ops: float32 [8, 121, 121], replicated, may hold values from -0.046875 to 0.046875
- far_in: float32 [31, 121, 121], replicated, may hold values from -0.09375 to 0.09375
- far_out: float32 [3, 121, 121], replicated, may hold values from -0.046875 to 0.046875
- down_ops: float32 [8, 121, 121], replicated, may hold values from -0.5 to 0.5
Outputs:
- local_field: float32 [121, 131072], P(None, ('group', 'dev'))
- potential: float32 [327680], P(('group', 'dev'))
The draws below stay inside these ranges and needn't reach their ends.
Inputs may be any that keep to these rules, and one draw needn't show every extreme that they name: `atom_owner`: an atom that changes device moves at most 2 positions along the curve. Of one device's rows, those sent to lower devices come first, the farther before the nearer, and those sent to higher devices come last, the nearer before the farther; the rest stay. At most 128 rows of one device name one other device, and for every offset some device sends exactly 128. `need_cells`: -1 marks an unused slot, and the used slots of a row come first. The cells asked of one device are consecutive cell numbers modulo 1024. No device asks itself; devices next to it on the curve (|s - t| = 1) are asked for exactly 72 cells, those two positions away for exactly 18, all others for 9 to 18. `list_entry`: each entry of a cell of device t is a column below 1024 or a column 1024 + s * 72 + j with need_cells[t, s, j] >= 0, and every such requested column appears in some entry of device t.
All inputs are finite; a program needn't handle non-finite values.
Results may differ from the reference program's by a relative error of at most 0.0003.
Values sent between devices are 32-bit elements; how exact they have to be, the bound alone decides.
No kernel may reach another device: no remote copies, remote signals or barrier semaphores. Data moves between devices by JAX's collectives and lax.ppermute only.
A program may use at most 64 MiB of HBM per device.

```python
from functools import partial
import jax
import jax.numpy as jnp
from jax import lax

K = 121
CELLS_DEV = 1024
ATOM_DEV = 2048
SLOT = 72
LIST = 16
OPS = 8
REACH = 2
OCT = 8
CAP = 128
NCELLS = 131072
ATOMS = 262144
MEMBERS_FAR = 31
GROUPS_FAR = 3
N_GROUP = 4
N_DEV = 32


def request_plan(key):
    device_total = NCELLS // CELLS_DEV
    count_key, base_key = jax.random.split(key)
    lower_count = max(1, SLOT // 8)
    upper_count = max(lower_count, SLOT // 4)
    rows_at = jnp.arange(device_total, dtype=jnp.int32)
    apart_by = jnp.abs(rows_at[None, :] - rows_at[:, None])
    spread = jax.random.randint(count_key, (device_total, device_total), lower_count, upper_count + 1, dtype=jnp.int32)
    counts = jnp.where(apart_by == 1, SLOT, jnp.where(apart_by == 2, upper_count, spread))
    counts = jnp.where(apart_by == 0, 0, counts)
    first_cell = jax.random.randint(base_key, (device_total, device_total), 0, CELLS_DEV, dtype=jnp.int32)
    return (counts, first_cell)


def draw_need_cells(key, part):
    counts, first_cell = request_plan(key)
    slot_ids = jnp.arange(SLOT, dtype=jnp.int32)
    cells = (first_cell[:, :, None] + slot_ids[None, None, :]) % CELLS_DEV
    return jnp.where(slot_ids[None, None, :] < counts[:, :, None], cells, -1).astype(jnp.int32)


def draw_list_entry(key, part):
    counts, first_cell = request_plan(key)
    key = jax.random.fold_in(key, 11)
    device_total = NCELLS // CELLS_DEV
    width = device_total * SLOT
    entry_total = LIST * CELLS_DEV
    slot_ids = jnp.arange(SLOT, dtype=jnp.int32)
    in_use = (slot_ids[None, None, :] < counts[:, :, None]).reshape(device_total, width)
    order = jnp.argsort(1 - in_use.astype(jnp.int32), axis=1).astype(jnp.int32)
    used_total = jnp.sum(in_use.astype(jnp.int32), axis=1)
    own_key, remote_key, share_key, shuffle_key = jax.random.split(key, 4)
    own_pick = jax.random.randint(own_key, (device_total, entry_total), 0, CELLS_DEV, dtype=jnp.int32)
    remote_pick = jax.random.randint(remote_key, (device_total, entry_total), 0, used_total[:, None], dtype=jnp.int32)
    go_remote = jax.random.randint(share_key, (device_total, entry_total), 0, 4, dtype=jnp.int32) == 0
    entry_ids = jnp.arange(entry_total, dtype=jnp.int32)
    forced = entry_ids[None, :] < used_total[:, None]
    position = jnp.where(forced, jnp.minimum(entry_ids, width - 1)[None, :], remote_pick)
    remote_column = CELLS_DEV + jnp.take_along_axis(order, position, axis=1)
    values = jnp.where(forced | go_remote, remote_column, own_pick)
    shuffles = jax.vmap(lambda one_key: jax.random.permutation(one_key, entry_total))(jax.random.split(shuffle_key, device_total))
    mixed = jnp.take_along_axis(values, shuffles.astype(jnp.int32), axis=1)
    return jnp.transpose(mixed.reshape(device_total, LIST, CELLS_DEV), (1, 0, 2)).reshape(LIST, NCELLS).astype(jnp.int32)


def draw_atom_owner(key, part):
    key = jax.random.fold_in(key, 3)
    device_total = ATOMS // ATOM_DEV
    step_list = jnp.array([step_by for step_by in range(-REACH, REACH + 1) if step_by != 0], jnp.int32)
    count_key, pick_key = jax.random.split(key)
    rows_at = jnp.arange(device_total, dtype=jnp.int32)[:, None]
    target = rows_at + step_list[None, :]
    inside = (target >= 0) & (target < device_total)
    counts = jax.random.randint(count_key, (device_total, 2 * REACH), 0, CAP + 1, dtype=jnp.int32)
    low_end = jnp.maximum(0, -step_list)
    high_end = device_total - jnp.maximum(0, step_list)
    picks = jax.random.randint(pick_key, (2 * REACH,), low_end, high_end, dtype=jnp.int32)
    counts = jnp.where(rows_at == picks[None, :], CAP, counts)
    counts = jnp.where(inside, counts, 0)
    lower_bounds = jnp.cumsum(counts[:, :REACH], axis=1)
    upper_bounds = jnp.cumsum(counts[:, REACH:][:, ::-1], axis=1)
    row_ids = jnp.arange(ATOM_DEV, dtype=jnp.int32)
    lower_index = jnp.sum((row_ids[None, :, None] >= lower_bounds[:, None, :]).astype(jnp.int32), axis=2)
    from_end = ATOM_DEV - 1 - row_ids
    upper_index = jnp.sum((from_end[None, :, None] >= upper_bounds[:, None, :]).astype(jnp.int32), axis=2)
    shift_to = jnp.where(lower_index < REACH, lower_index - REACH, jnp.where(upper_index < REACH, REACH - upper_index, 0))
    return (rows_at + shift_to).reshape(ATOMS).astype(jnp.int32)


def touch_ends(drawn, stream_key, least, high):
    place = [jax.random.randint(jax.random.fold_in(stream_key, axis), (), 0, length) for axis, length in enumerate(drawn.shape)]
    widest = drawn.shape.index(max(drawn.shape))
    next_to = place[:widest] + [(place[widest] + 1) % drawn.shape[widest]] + place[widest + 1:]
    return drawn.at[tuple(place)].set(least).at[tuple(next_to)].set(high)


def block_levels(stream_key, shape, cuts, smallest, top_value):
    loudness, own = 1.0, jax.random.fold_in(stream_key, 6)
    for dim, blocks in cuts:
        heights = jnp.exp(jax.random.uniform(jax.random.fold_in(own, dim), (blocks,), jnp.float32, smallest / len(cuts), top_value / len(cuts)))
        loudness = loudness * jnp.repeat(heights, shape[dim] // blocks).reshape([-1 if axis == dim else 1 for axis in range(len(shape))])
    return loudness


def gaussian(stream_key, extent, scale, limit, kind=jnp.bfloat16):
    return jnp.clip(scale * jax.random.normal(stream_key, extent, jnp.float32), -limit, limit).astype(kind)


def setup_inputs(seed: int = 0) -> dict:
    seeds = jax.random.split(jax.random.key(seed), 14)
    atom_rows = jnp.clip(jax.random.uniform(seeds[0], (4, ATOMS), jnp.float32, -0.5, 0.5) * block_levels(seeds[0], (4, ATOMS), ((1, 128),), -0.4, 0.0), -0.5, 0.5)
    atom_owner = draw_atom_owner(jax.random.fold_in(seeds[13], 71), 0)
    atom_cell = touch_ends(jax.random.randint(seeds[2], (ATOMS,), 0, CELLS_DEV), jax.random.fold_in(seeds[2], 1), 0, CELLS_DEV - 1).astype(jnp.int32)
    need_cells = draw_need_cells(jax.random.fold_in(seeds[13], 71), 0)
    list_entry = draw_list_entry(jax.random.fold_in(seeds[13], 71), 0)
    list_class = touch_ends(jax.random.randint(seeds[5], (LIST, NCELLS), 0, OPS), jax.random.fold_in(seeds[5], 1), 0, OPS - 1).astype(jnp.int32)
    basis_freq = jnp.clip(jax.random.uniform(seeds[6], (K, 3), jnp.float32, -4.0, 4.0), -4.0, 4.0)
    basis_phase = jnp.clip(jax.random.uniform(seeds[7], (K,), jnp.float32, -3.140625, 3.140625), -3.140625, 3.140625)
    near_ops = gaussian(seeds[8], (OPS, K, K), (K * LIST) ** -0.5, 0.125, jnp.float32)
    up_ops = gaussian(seeds[9], (OCT, K, K), (K * CELLS_DEV // OCT) ** -0.5, 0.046875, jnp.float32)
    far_in = gaussian(seeds[10], (MEMBERS_FAR, K, K), (K * N_DEV) ** -0.5, 0.09375, jnp.float32)
    far_out = gaussian(seeds[11], (GROUPS_FAR, K, K), (K * N_DEV * N_GROUP) ** -0.5, 0.046875, jnp.float32)
    down_ops = gaussian(seeds[12], (OCT, K, K), K ** -0.5, 0.5, jnp.float32)
    return dict(atom_rows=atom_rows, atom_owner=atom_owner, atom_cell=atom_cell, need_cells=need_cells, list_entry=list_entry, list_class=list_class, basis_freq=basis_freq, basis_phase=basis_phase, near_ops=near_ops, up_ops=up_ops, far_in=far_in, far_out=far_out, down_ops=down_ops)


soften = 0.25
highest = lax.Precision.HIGHEST

def move_steps():
    return [step_by for step_by in range(-REACH, REACH + 1) if step_by != 0]

def outgoing(payload, offsets, step_by):
    chosen = (offsets == step_by).astype(jnp.int32)
    ranking = jnp.cumsum(chosen) - chosen
    where_to = jnp.where(chosen > 0, ranking, CAP).astype(jnp.int32)
    buffer = jnp.zeros((payload.shape[0], CAP + 1), jnp.float32).at[:, where_to].set(payload)
    return buffer[:, :CAP]

def shift_rows(outbound, step_by):
    blank = jnp.zeros_like(outbound[:abs(step_by)])
    if step_by > 0:
        return jnp.concatenate([blank, outbound[:-step_by]], axis=0)
    return jnp.concatenate([outbound[-step_by:], blank], axis=0)

def slot_basis(arrived_dev, basis_freq, basis_phase):
    return jnp.cos(jnp.dot(basis_freq, arrived_dev[0:3], precision=highest) + basis_phase[:, None])

def cell_index(arrived_dev):
    return jnp.where(arrived_dev[4] > 0.5, arrived_dev[4] - 1.0, float(CELLS_DEV)).astype(jnp.int32)

def pole_sums(arrived_dev, basis_vals, cell_ids):
    weighted = basis_vals * arrived_dev[3][None, :]
    summed = jax.ops.segment_sum(weighted.T, cell_ids, num_segments=CELLS_DEV + 1)
    return summed[:CELLS_DEV].T

def near_potential(arrived_dev):
    slot_count = arrived_dev.shape[1]
    block_rows = slot_count // max(1, slot_count // 512)

    def one_block(offset):
        picked = lax.dynamic_slice_in_dim(arrived_dev, offset, block_rows, 1)
        squared = jnp.zeros((block_rows, slot_count), jnp.float32)
        for axis_id in range(3):
            spacing = picked[axis_id][:, None] - arrived_dev[axis_id][None, :]
            squared = squared + spacing * spacing
        same_cell = picked[4][:, None] == arrived_dev[4][None, :]
        itself = (offset + jnp.arange(block_rows, dtype=jnp.int32))[:, None] == jnp.arange(slot_count, dtype=jnp.int32)[None, :]
        weights = jnp.where(same_cell & ~itself, arrived_dev[3][None, :] / jnp.sqrt(squared + soften), 0.0)
        return lax.optimization_barrier(jnp.sum(weights, axis=1))
    starts = jnp.arange(slot_count // block_rows, dtype=jnp.int32) * block_rows
    return lax.map(one_block, starts).reshape(-1)

def near_apply(source_table, entry_dev, class_dev, near_ops):
    coef_count = source_table.shape[0]
    gathered = jnp.take(source_table, entry_dev.reshape(-1), axis=1).reshape(coef_count, entry_dev.shape[0], entry_dev.shape[1])
    class_hot = (class_dev[None, :, :] == jnp.arange(near_ops.shape[0], dtype=jnp.int32)[:, None, None]).astype(jnp.float32)
    by_class = jnp.einsum('klc,olc->okc', gathered, class_hot, precision=highest)
    return jnp.einsum('okj,ojc->kc', near_ops, by_class, precision=highest)

def coarse_of(multipole, up_ops):
    grouped = lax.optimization_barrier(jnp.sum(multipole.reshape(multipole.shape[0], -1, OCT), axis=1))
    return jnp.einsum('okj,jo->k', up_ops, grouped, precision=highest)

def distance_table(member_count):
    member_ids = jnp.arange(member_count, dtype=jnp.int32)
    apart_by = jnp.abs(member_ids[:, None] - member_ids[None, :]) - 1
    return (apart_by[:, :, None] == jnp.arange(member_count - 1, dtype=jnp.int32)[None, None, :]).astype(jnp.float32)

def far_fields(coarse_all, far_in, far_out):
    groups = coarse_all.shape[0]
    members = coarse_all.shape[1]
    turned = jnp.einsum('okj,gbj->gbok', far_in, coarse_all, precision=highest)
    inner_field = jnp.einsum('abo,gbok->gak', distance_table(members), turned, precision=highest)
    group_sums = lax.optimization_barrier(jnp.sum(coarse_all, axis=1))
    outer_terms = jnp.einsum('okj,bj->bok', far_out, group_sums, precision=highest)
    outer_field = jnp.einsum('abo,bok->ak', distance_table(groups), outer_terms, precision=highest)
    return inner_field + outer_field[:, None, :]

def reference(atom_rows, atom_owner, atom_cell, need_cells, list_entry, list_class, basis_freq, basis_phase, near_ops, up_ops, far_in, far_out, down_ops):
    devices = N_GROUP * N_DEV
    own_ids = jnp.arange(devices, dtype=jnp.int32)
    offsets = atom_owner.reshape(devices, ATOM_DEV) - own_ids[:, None]
    payload = jnp.concatenate([atom_rows, (atom_cell + 1).astype(jnp.float32)[None, :]], axis=0)
    payload = jnp.transpose(payload.reshape(5, devices, ATOM_DEV), (1, 0, 2))
    pieces = [jnp.where((offsets == 0)[:, None, :], payload, 0.0)]
    for step_by in move_steps():
        outbound = jax.vmap(partial(outgoing, step_by=step_by))(payload, offsets)
        pieces.append(shift_rows(outbound, step_by))
    per_device = jnp.concatenate(pieces, axis=2)

    def multipole_of(arrived_dev):
        basis_vals = slot_basis(arrived_dev, basis_freq, basis_phase)
        return pole_sums(arrived_dev, basis_vals, cell_index(arrived_dev))
    multipoles = lax.map(multipole_of, per_device)
    flat_poles = jnp.transpose(multipoles, (1, 0, 2)).reshape(K, devices * CELLS_DEV)

    def coarse_one(multipole):
        return coarse_of(multipole, up_ops)
    coarse = lax.map(coarse_one, multipoles)
    far_all = far_fields(coarse.reshape(N_GROUP, N_DEV, K), far_in, far_out).reshape(devices, K)
    entries = jnp.transpose(list_entry.reshape(LIST, devices, CELLS_DEV), (1, 0, 2))
    classes = jnp.transpose(list_class.reshape(LIST, devices, CELLS_DEV), (1, 0, 2))

    def finish(inputs):
        arrived_dev, own_poles, requests, entry_dev, class_dev, far_vec = inputs
        in_use = requests >= 0
        wanted = jnp.where(in_use, own_ids[:, None] * CELLS_DEV + requests, 0).astype(jnp.int32)
        fetched = jnp.take(flat_poles, wanted.reshape(-1), axis=1).reshape(K, devices, SLOT)
        received = jnp.where(in_use[None, :, :], fetched, 0.0).reshape(K, devices * SLOT)
        source_table = jnp.concatenate([own_poles, received], axis=1)
        near_field = near_apply(source_table, entry_dev, class_dev, near_ops)
        down_terms = jnp.einsum('okj,j->ko', down_ops, far_vec, precision=highest)
        local_dev = near_field + jnp.tile(down_terms, (1, CELLS_DEV // OCT))
        basis_vals = slot_basis(arrived_dev, basis_freq, basis_phase)
        local_pad = jnp.concatenate([local_dev, jnp.zeros((K, 1), jnp.float32)], axis=1)
        local_at = jnp.take(local_pad, cell_index(arrived_dev), axis=1)
        far_part = lax.optimization_barrier(jnp.sum(local_at * basis_vals, axis=0)) * K ** (-0.5)
        return (local_dev, far_part + near_potential(arrived_dev))
    locals_all, potentials = lax.map(finish, (per_device, multipoles, need_cells, entries, classes, far_all))
    local_field = jnp.transpose(locals_all, (1, 0, 2)).reshape(K, devices * CELLS_DEV)
    return (local_field, potentials.reshape(-1))
```

```python
import math

import jax
import jax.numpy as jnp
from jax import lax
from jax.experimental import pallas as pl
from jax.experimental.pallas import tpu as pltpu
from jax.sharding import PartitionSpec as P

COEF = 121
LANES = 128
CELLS = 1024
STAY = 2048
CAP = 128
ARRIVE = 4 * CAP
SLOTS = STAY + ARRIVE
LIST = 16
OPS = 8
SLOT = 72
SHORT = 18
BLOCK = SHORT + 1
DEVICES = 128
MEMBERS = 32
GROUPS = 4
EXTRA = 56
FAR_ROWS = DEVICES * BLOCK
REMOTE = FAR_ROWS + 2 * EXTRA
WRAP = CELLS + 80
AXES = ("group", "dev")
MIB = 2**20
f32, bf16, i32 = jnp.float32, jnp.bfloat16, jnp.int32
SIN = [(-1) ** n * (2 * math.pi) ** (2 * n + 1) / math.factorial(2 * n + 1) for n in range(6)]

NT = (((1,), (1,)), ((), ()))
NN = (((1,), (0,)), ((), ()))


def shift(value, by):
    pairs = [(i, i + by) for i in range(DEVICES) if 0 <= i + by < DEVICES]
    return lax.ppermute(value, AXES, pairs)


def split(value):
    high = value.astype(bf16)
    return high, (value - high.astype(f32)).astype(bf16)


def basis_of(waves, atoms):
    turns = waves[:, 3:4] + waves[:, 0:1] * atoms[0:1, :]
    turns = turns + waves[:, 1:2] * atoms[1:2, :]
    turns = turns + waves[:, 2:3] * atoms[2:3, :]
    turns = turns - jnp.floor(turns + 0.5)
    base = 0.25 - jnp.abs(turns)
    square = base * base
    total = jnp.full_like(square, SIN[5])
    for factor in SIN[4::-1]:
        total = total * square + factor
    return base * total


def cell_hot(cell_row):
    ids = lax.broadcasted_iota(i32, (CELLS, cell_row.shape[1]), 0) + 1
    return jnp.where(ids == cell_row, 1.0, 0.0).astype(bf16)


def poles(basis, charge, hot):
    high, low = split(basis * charge)
    both = lax.dot_general(hot, jnp.concatenate([high, low], axis=0), NT, preferred_element_type=f32)
    return both[:, :LANES] + both[:, LANES:]


def pack_kernel(me_ref, owner_ref, rows_ref, cell_ref, m2_ref, m1_ref, p1_ref, p2_ref, buf):
    gap = owner_ref[...] - me_ref[0]

    def count(by):
        return jnp.sum(jnp.where(gap == by, 1.0, 0.0)).astype(i32)

    buf[...] = jnp.zeros_like(buf)
    for at, lo in ((0, 0), (256, STAY - 256)):
        buf[0:4, at : at + 256] = rows_ref[:, lo : lo + 256]
        buf[4:5, at : at + 256] = (cell_ref[:, lo : lo + 256] + 1).astype(f32)
    lane = lax.broadcasted_iota(i32, (8, CAP), 1)
    low2, low1, up1, up2 = count(-2), count(-1), count(1), count(2)
    m2_ref[...] = jnp.where(lane < low2, buf[:, :CAP], 0.0)
    ahead = pltpu.roll(buf[:, :256], lax.rem(256 - low2, 256), 1)
    m1_ref[...] = jnp.where(lane < low1, ahead[:, :CAP], 0.0)
    behind = pltpu.roll(buf[:, 256:], lax.rem(up1 + up2, 256), 1)
    p1_ref[...] = jnp.where(lane < up1, behind[:, :CAP], 0.0)
    last = pltpu.roll(buf[:, 256:], lax.rem(up2, 256), 1)
    p2_ref[...] = jnp.where(lane < up2, last[:, :CAP], 0.0)


def order_kernel(me_ref, entry_ref, class_ref, own_ref, far_ref, count_ref):
    entry, kind = entry_ref[...], class_ref[...]
    own_ref[...] = jnp.where(entry < CELLS, kind * CELLS + entry, OPS * CELLS)
    asked = jnp.maximum(entry - CELLS, 0)
    source = jnp.floor((asked.astype(f32) + 0.5) * (1.0 / SLOT)).astype(i32)
    slot = asked - source * SLOT
    side = jnp.where(source < me_ref[0], FAR_ROWS, FAR_ROWS + EXTRA)
    row = jnp.where(slot < SHORT, source * BLOCK + slot, side + slot - SHORT)
    key = jnp.where(entry < CELLS, -1, kind * REMOTE + row)
    keys = [key[l] for l in range(LIST)]
    used = keys[0] * 0
    for one in keys:
        used = used + jnp.where(one >= 0, 1, 0)
    step = 1
    while step < LIST:
        gap = step
        while gap >= 1:
            for base in range(gap % step, LIST - gap, 2 * gap):
                for i in range(min(gap, LIST - base - gap)):
                    a, b = base + i, base + i + gap
                    if a // (2 * step) == b // (2 * step):
                        keys[a], keys[b] = jnp.maximum(keys[a], keys[b]), jnp.minimum(keys[a], keys[b])
            gap //= 2
        step *= 2
    for l in range(LIST):
        far_ref[l] = jnp.where(keys[l] < 0, OPS * REMOTE, keys[l])
    count_ref[...] = jnp.max(used, axis=0, keepdims=True)


def stay_kernel(me_ref, owner_ref, rows_ref, cell_ref, waves_ref, atoms_ref, basis_ref, pole_ref):
    stays = owner_ref[...] == me_ref[0]
    atoms_ref[...] = jnp.zeros_like(atoms_ref)
    atoms_ref[0:4, :] = jnp.where(stays, rows_ref[...], 0.0)
    atoms_ref[4:5, :] = jnp.where(stays, (cell_ref[...] + 1).astype(f32), 0.0)
    width = 512
    for lo in range(0, STAY, width):
        atoms = atoms_ref[:, lo : lo + width]
        basis = basis_of(waves_ref[...], atoms)
        basis_ref[:, lo : lo + width] = basis
        part = poles(basis, atoms[3:4, :], cell_hot(atoms[4:5, :].astype(i32)))
        pole_ref[...] = part if lo == 0 else pole_ref[...] + part


def merge_kernel(
    me_ref, first_ref, m2_ref, m1_ref, p1_ref, p2_ref, waves_ref, stay_ref, up_ref,
    send_ref, low_ref, high_ref, pole_ref, basis_ref, atoms_ref, ring, turned,
):
    for at, ref in enumerate((m2_ref, m1_ref, p1_ref, p2_ref)):
        atoms_ref[:, at * CAP : (at + 1) * CAP] = ref[...]
    atoms = atoms_ref[...]
    basis = basis_of(waves_ref[...], atoms)
    basis_ref[...] = basis
    pole = stay_ref[...] + poles(basis, atoms[3:4, :], cell_hot(atoms[4:5, :].astype(i32)))
    pole_ref[...] = pole
    ring[0:CELLS, :] = pole
    ring[CELLS:WRAP, :] = pole[0 : WRAP - CELLS, :]
    grouped = jnp.sum(pole.reshape(CELLS // 8, 8, LANES), axis=0)
    raised = up_ref[...].reshape(COEF, OPS, COEF) * grouped[None, :, :COEF]
    turned[...] = jnp.zeros_like(turned)
    turned[0:COEF, 0:COEF] = jnp.sum(raised, axis=1)
    coarse = jnp.sum(turned[...].T, axis=0, keepdims=True)

    def one(t, _):
        start = jnp.maximum(first_ref[t], 0)
        send_ref[pl.ds(t * BLOCK, SHORT), :] = ring[pl.ds(start, SHORT), :]
        send_ref[pl.ds(t * BLOCK + SHORT, 1), :] = coarse
        return 0

    lax.fori_loop(0, DEVICES, one, 0, unroll=4)
    me = me_ref[0]
    below = jnp.maximum(first_ref[jnp.maximum(me - 1, 0)], 0)
    above = jnp.maximum(first_ref[jnp.minimum(me + 1, DEVICES - 1)], 0)
    low_ref[...] = ring[pl.ds(below + SHORT, EXTRA), :]
    high_ref[...] = ring[pl.ds(above + SHORT, EXTRA), :]


def load_ops(ops_ref, both, low):
    both[...] = jnp.zeros_like(both)
    low[...] = jnp.zeros_like(low)
    for o in range(OPS):
        one_high, one_low = split(ops_ref[pl.ds(o, COEF, stride=OPS), :])
        both[o * LANES : o * LANES + COEF, 0:COEF] = one_high
        both[o * LANES : o * LANES + COEF, LANES : LANES + COEF] = one_high
        low[o * LANES : o * LANES + COEF, 0:COEF] = one_low


def premultiply(rows, both, low):
    high, rest = split(rows)
    out = lax.dot_general(jnp.concatenate([high, rest], axis=1), both[...], NT, preferred_element_type=f32)
    return out + lax.dot_general(high, low[...], NT, preferred_element_type=f32)


def mid_kernel(own_ref, stay_ref, new_ref, pole_ref, ops_ref, sum_ref, pair_ref, table, both, low, cols, atoms_ref):
    atoms_ref[:, 0:STAY] = stay_ref[...]
    atoms_ref[:, STAY:] = new_ref[...]
    load_ops(ops_ref, both, low)
    width = 128

    def apply(i, _):
        lo = pl.multiple_of(i * width, width)
        out = premultiply(pole_ref[pl.ds(lo, width), :], both, low)
        for o in range(OPS):
            table[pl.ds(o * CELLS + lo, width), :] = out[:, o * LANES : (o + 1) * LANES]
        return 0

    lax.fori_loop(0, CELLS // width, apply, 0)
    table[OPS * CELLS :, :] = jnp.zeros((8, LANES), f32)

    def gather(g, _):
        for r in range(8):
            total = None
            for l in range(LIST):
                row = table[pl.ds(own_ref[l * CELLS + r * LANES + g], 1), :]
                total = row if total is None else total + row
            sum_ref[pl.ds(r * LANES + g, 1), :] = total
        return 0

    lax.fori_loop(0, LANES, gather, 0)

    for lo in range(0, SLOTS, LANES):
        cols[lo : lo + LANES, :] = atoms_ref[:, lo : lo + LANES].T
    pair_ref[...] = jnp.zeros_like(pair_ref)
    wide = 512
    for lo in range(0, SLOTS, wide):
        across = atoms_ref[:, lo : lo + wide]

        def pairs(i, total):
            down = cols[pl.ds(pl.multiple_of(i * 8, 8), 8), :]
            gap = down[:, 0:1] - across[0:1, :]
            far = gap * gap + 0.25
            gap = down[:, 1:2] - across[1:2, :]
            far = far + gap * gap
            gap = down[:, 2:3] - across[2:3, :]
            far = far + gap * gap
            charge = jnp.where(down[:, 4:5] == across[4:5, :], down[:, 3:4], 0.0)
            return total + charge * lax.rsqrt(far)

        total = lax.fori_loop(0, SLOTS // 8, pairs, jnp.zeros((8, wide), f32), unroll=8)
        itself = across[3:4, :] * lax.rsqrt(jnp.full((1, wide), 0.25, f32))
        pair_ref[:, lo : lo + wide] = jnp.sum(total, axis=0, keepdims=True) - itself


def last_kernel(
    me_ref, index_ref, count_ref, far_ref, below_ref, above_ref, ops_ref, sum_ref, inner_ref, outer_ref, down_ref,
    stay_ref, new_ref, stay_basis_ref, new_basis_ref, pair_ref, local_ref, pot_ref,
    table, both, low, rows, coarse,
):
    load_ops(ops_ref, both, low)

    def apply(rows_in, at):
        out = premultiply(rows_in, both, low)
        for o in range(OPS):
            table[pl.ds(o * REMOTE + at, rows_in.shape[0]), :] = out[:, o * LANES : (o + 1) * LANES]

    width = 128

    def step(i, _):
        lo = pl.multiple_of(i * width, width)
        apply(far_ref[pl.ds(lo, width), :], lo)
        return 0

    lax.fori_loop(0, FAR_ROWS // width, step, 0)
    apply(below_ref[...], FAR_ROWS)
    apply(above_ref[...], FAR_ROWS + EXTRA)
    table[OPS * REMOTE :, :] = jnp.zeros((8, LANES), f32)

    coarse[...] = far_ref[pl.ds(SHORT, DEVICES, stride=BLOCK), :]
    me = me_ref[0]
    group, member = me // MEMBERS, lax.rem(me, MEMBERS)
    who = lax.broadcasted_iota(i32, (40, DEVICES), 1)
    which = lax.broadcasted_iota(i32, (40, DEVICES), 0)
    its_group, its_member = who // MEMBERS, lax.rem(who, MEMBERS)
    near = (its_group == group) & (jnp.abs(its_member - member) - 1 == which) & (which < MEMBERS)
    away = (jnp.abs(its_group - group) - 1 == which - MEMBERS) & (which >= MEMBERS)
    chosen = jnp.where(near | away, 1.0, 0.0)
    sums = lax.dot_general(chosen, coarse[...], NN, precision=lax.Precision.HIGHEST, preferred_element_type=f32)
    field = jnp.sum(inner_ref[...] * sums[None, 0 : MEMBERS - 1, 0:COEF], axis=1)
    for o in range(GROUPS - 1):
        field = field + outer_ref[o] * sums[MEMBERS + o : MEMBERS + o + 1, 0:COEF]
    field = jnp.broadcast_to(jnp.sum(field, axis=1, keepdims=True), (COEF, LANES))
    child = lax.rem(lax.broadcasted_iota(i32, (COEF, LANES), 1), OPS)
    pattern = jnp.zeros((COEF, LANES), f32)
    for o in range(OPS):
        one = lax.dot_general(
            down_ref[pl.ds(o, COEF, stride=OPS), :], field, NN,
            precision=lax.Precision.HIGHEST, preferred_element_type=f32,
        )
        pattern = jnp.where(child == o, one, pattern)

    def gather(g, _):
        def more(l, totals):
            return tuple(
                totals[r] + table[pl.ds(index_ref[l * CELLS + r * LANES + g], 1), :] for r in range(8)
            )

        start = tuple(sum_ref[pl.ds(r * LANES + g, 1), :] for r in range(8))
        totals = lax.fori_loop(0, count_ref[g], more, start)
        for r in range(8):
            rows[pl.ds(r * LANES + g, 1), :] = totals[r]
        return 0

    lax.fori_loop(0, LANES, gather, 0)

    for lo in range(0, CELLS, LANES):
        local_ref[:, lo : lo + LANES] = rows[lo : lo + LANES, :].T[0:COEF, :] + pattern
    local = local_ref[...]
    high, rest = split(local)
    high = jnp.concatenate([high, jnp.zeros((LANES - COEF, CELLS), bf16)], axis=0)
    rest = jnp.concatenate([rest, jnp.zeros((LANES - COEF, CELLS), bf16)], axis=0)
    stacked = jnp.concatenate([high, rest], axis=0)
    wide = 512
    for lo in range(0, SLOTS, wide):
        if lo < STAY:
            cells, basis = stay_ref[4:5, lo : lo + wide], stay_basis_ref[:, lo : lo + wide]
        else:
            cells, basis = new_ref[4:5, :], new_basis_ref[...]
        at = lax.dot_general(stacked, cell_hot(cells.astype(i32)), NN, preferred_element_type=f32)
        read = jnp.sum((at[:LANES] + at[LANES:]) * basis, axis=0, keepdims=True)
        pot_ref[:, lo : lo + wide] = read * COEF**-0.5 + pair_ref[:, lo : lo + wide]


VM = pl.BlockSpec(memory_space=pltpu.VMEM)
SM = pl.BlockSpec(memory_space=pltpu.SMEM)


def call(kernel, name, ins, outs, scratch, limit, flops, *operands):
    cost = pl.CostEstimate(flops=flops, bytes_accessed=4 * MIB, transcendentals=0)
    return pl.pallas_call(
        kernel,
        name=name,
        in_specs=ins,
        out_specs=[VM] * len(outs),
        out_shape=[jax.ShapeDtypeStruct(shape, kind) for shape, kind in outs],
        scratch_shapes=scratch,
        cost_estimate=cost,
        compiler_params=pltpu.CompilerParams(vmem_limit_bytes=limit * MIB),
    )(*operands)


def on_device(
    atom_rows,
    atom_owner,
    atom_cell,
    need_cells,
    list_entry,
    list_class,
    basis_freq,
    basis_phase,
    near_ops,
    up_ops,
    far_in,
    far_out,
    down_ops,
):
    me = (lax.axis_index("group") * MEMBERS + lax.axis_index("dev")).reshape(1).astype(i32)
    first = lax.all_to_all(need_cells[0, :, 0].reshape(DEVICES, 1, 1), AXES, split_axis=0, concat_axis=0, tiled=True)
    first = first.reshape(DEVICES)
    waves = jnp.concatenate([basis_freq, basis_phase[:, None]], axis=1) * (0.5 / math.pi)
    waves = jnp.pad(waves, ((0, LANES - COEF), (0, 4)))
    owner_row, cell_row = atom_owner.reshape(1, STAY), atom_cell.reshape(1, STAY)
    by_row = [ops.transpose(1, 0, 2).reshape(COEF * OPS, COEF) for ops in (near_ops, up_ops, down_ops)]

    piece = ((8, CAP), f32)
    outbound = call(
        pack_kernel, "pack", [SM, VM, VM, VM], [piece] * 4, [pltpu.VMEM((8, 512), f32)], 16, 10**6,
        me, atom_owner.reshape(STAY // LANES, LANES), atom_rows, cell_row,
    )
    pieces = [shift(out, by) for out, by in zip(outbound, (-2, -1, 1, 2))]

    shape3 = (LIST, CELLS // LANES, LANES)
    own_index, far_index, counts = call(
        order_kernel, "order", [SM, VM, VM], [(shape3, i32), (shape3, i32), ((1, LANES), i32)], [], 16, 10**6,
        me, list_entry.reshape(shape3), list_class.reshape(shape3),
    )
    stay_atoms, stay_basis, stay_pole = call(
        stay_kernel, "stay", [SM, VM, VM, VM, VM],
        [((8, STAY), f32), ((LANES, STAY), f32), ((CELLS, LANES), f32)], [], 32, 4 * 10**9,
        me, owner_row, atom_rows, cell_row, waves,
    )
    send, low, high, pole, new_basis, new_atoms = call(
        merge_kernel, "merge", [SM, SM, VM, VM, VM, VM, VM, VM, VM],
        [((FAR_ROWS, LANES), f32), ((EXTRA, LANES), f32), ((EXTRA, LANES), f32), ((CELLS, LANES), f32),
         ((LANES, ARRIVE), f32), ((8, ARRIVE), f32)],
        [pltpu.VMEM((WRAP, LANES), f32), pltpu.VMEM((LANES, LANES), f32)], 32, 2 * 10**9,
        me, first, *pieces, waves, stay_pole, by_row[1],
    )
    below, above = shift(high, 1), shift(low, -1)
    far_rows = lax.all_to_all(send.reshape(DEVICES, 1, BLOCK * LANES), AXES, split_axis=0, concat_axis=0, tiled=True)
    far_rows = far_rows.reshape(FAR_ROWS, LANES)
    split_ops = [pltpu.VMEM((OPS * LANES, 2 * LANES), bf16), pltpu.VMEM((OPS * LANES, LANES), bf16)]
    own_sum, pair = call(
        mid_kernel, "mid", [SM, VM, VM, VM, VM], [((CELLS, LANES), f32), ((1, SLOTS), f32)],
        [pltpu.VMEM((OPS * CELLS + 8, LANES), f32), *split_ops, pltpu.VMEM((SLOTS, 8), f32), pltpu.VMEM((8, SLOTS), f32)],
        32, 20 * 10**9,
        own_index.reshape(-1), stay_atoms, new_atoms, pole, by_row[0],
    )
    local, pot = call(
        last_kernel, "last", [SM, SM, SM] + [VM] * 13, [((COEF, CELLS), f32), ((1, SLOTS), f32)],
        [pltpu.VMEM((OPS * REMOTE + 8, LANES), f32), *split_ops, pltpu.VMEM((CELLS, LANES), f32),
         pltpu.VMEM((DEVICES, LANES), f32)],
        40, 8 * 10**9,
        me, far_index.reshape(-1), counts.reshape(-1), far_rows, below, above, by_row[0], own_sum,
        far_in.transpose(1, 0, 2), far_out, by_row[2], stay_atoms, new_atoms, stay_basis, new_basis, pair,
    )
    return local, pot.reshape(SLOTS)


def solution(mesh):
    in_specs = (
        P(None, AXES),
        P(AXES),
        P(AXES),
        P(AXES, None, None),
        P(None, AXES),
        P(None, AXES),
        P(),
        P(),
        P(),
        P(),
        P(),
        P(),
        P(),
    )
    out_specs = (P(None, AXES), P(AXES))
    return jax.shard_map(on_device, mesh=mesh, in_specs=in_specs, out_specs=out_specs, check_vma=False)
```

```python
import math

import jax
import jax.numpy as jnp
from jax import lax
from jax.experimental import pallas as pl
from jax.experimental.pallas import tpu as pltpu
from jax.sharding import PartitionSpec as P

COEF = 121
LANES = 128
CELLS = 1024
STAY = 2048
CAP = 128
ARRIVE = 4 * CAP
SLOTS = STAY + ARRIVE
LIST = 16
OPS = 8
SLOT = 72
SHORT = 18
BLOCK = SHORT + 1
DEVICES = 128
MEMBERS = 32
GROUPS = 4
PIECE = 6
EXTRA = 56
FAR_ROWS = DEVICES * BLOCK
REMOTE = FAR_ROWS + 2 * EXTRA
WRAP = CELLS + 80
AXES = ("group", "dev")
MIB = 2**20
f32, bf16, i32 = jnp.float32, jnp.bfloat16, jnp.int32
SIN = [(-1) ** n * (2 * math.pi) ** (2 * n + 1) / math.factorial(2 * n + 1) for n in range(6)]

NT = (((1,), (1,)), ((), ()))
NN = (((1,), (0,)), ((), ()))


def shift(value, by):
    pairs = [(i, i + by) for i in range(DEVICES) if 0 <= i + by < DEVICES]
    return lax.ppermute(value, AXES, pairs)


def split(value):
    high = value.astype(bf16)
    return high, (value - high.astype(f32)).astype(bf16)


def basis_of(waves, atoms):
    turns = waves[:, 3:4] + waves[:, 0:1] * atoms[0:1, :]
    turns = turns + waves[:, 1:2] * atoms[1:2, :]
    turns = turns + waves[:, 2:3] * atoms[2:3, :]
    turns = turns - jnp.floor(turns + 0.5)
    base = 0.25 - jnp.abs(turns)
    square = base * base
    total = jnp.full_like(square, SIN[5])
    for factor in SIN[4::-1]:
        total = total * square + factor
    return base * total


def cell_hot(cell_row):
    ids = lax.broadcasted_iota(i32, (CELLS, cell_row.shape[1]), 0) + 1
    return jnp.where(ids == cell_row, 1.0, 0.0).astype(bf16)


def poles(basis, charge, hot):
    high, low = split(basis * charge)
    both = lax.dot_general(hot, jnp.concatenate([high, low], axis=0), NT, preferred_element_type=f32)
    return both[:, :LANES] + both[:, LANES:]


def load(sems, *pairs):
    copies = [pltpu.make_async_copy(src, dst, sems.at[i]) for i, (src, dst) in enumerate(pairs)]
    for copy in copies:
        copy.start()
    return copies


def waves_of(freq_ref, phase_ref, flat):
    flat[...] = jnp.zeros_like(flat)
    flat[0:3, 0:COEF] = freq_ref[...] * (0.5 / math.pi)
    flat[3:4, 0:COEF] = phase_ref[...] * (0.5 / math.pi)
    return flat[...].T


def pack_kernel(me_ref, need_hbm, owner_hbm, rows_hbm, cell_hbm, out_ref, need, owner, rows, cell, buf, sems):
    copies = load(
        sems, (owner_hbm, owner), (rows_hbm, rows), (cell_hbm, cell), (need_hbm.at[0, pl.ds(0, 8), :], need)
    )
    out_ref[...] = jnp.zeros_like(out_ref)
    buf[...] = jnp.zeros_like(buf)
    for copy in copies:
        copy.wait()
    me = me_ref[0]
    gap = owner[...] - me

    def count(by):
        return jnp.sum(jnp.where(gap == by, 1.0, 0.0)).astype(i32)

    for at, lo in ((0, 0), (256, STAY - 256)):
        buf[0:4, at : at + 256] = rows[:, lo : lo + 256]
        buf[4:5, at : at + 256] = (cell[:, lo : lo + 256] + 1).astype(f32)
    lane = lax.broadcasted_iota(i32, (8, CAP), 1)
    low2, low1, up1, up2 = count(-2), count(-1), count(1), count(2)
    first = jnp.broadcast_to(need[0:1, :].astype(f32), (LANES, LANES)).T
    out_ref[pl.ds(5, DEVICES, stride=PIECE), :] = first
    ahead = pltpu.roll(buf[:, :256], lax.rem(256 - low2, 256), 1)
    behind = pltpu.roll(buf[:, 256:], lax.rem(up1 + up2, 256), 1)
    last = pltpu.roll(buf[:, 256:], lax.rem(up2, 256), 1)
    for by, count_by, piece in (
        (-2, low2, buf[:, :CAP]), (-1, low1, ahead[:, :CAP]), (1, up1, behind[:, :CAP]), (2, up2, last[:, :CAP])
    ):
        to = me + by

        @pl.when((to >= 0) & (to < DEVICES))
        def _(to=to, count_by=count_by, piece=piece):
            out_ref[pl.ds(to * PIECE, 5), :] = jnp.where(lane < count_by, piece, 0.0)[0:5, :]


def order(me, entry, kind, own_ref, far_ref, count_ref):
    own_ref[...] = jnp.where(entry < CELLS, kind * CELLS + entry, OPS * CELLS)
    asked = jnp.maximum(entry - CELLS, 0)
    source = jnp.floor((asked.astype(f32) + 0.5) * (1.0 / SLOT)).astype(i32)
    slot = asked - source * SLOT
    side = jnp.where(source < me, FAR_ROWS, FAR_ROWS + EXTRA)
    row = jnp.where(slot < SHORT, source * BLOCK + slot, side + slot - SHORT)
    key = jnp.where(entry < CELLS, -1, kind * REMOTE + row)
    keys = [key[l] for l in range(LIST)]
    used = keys[0] * 0
    for one in keys:
        used = used + jnp.where(one >= 0, 1, 0)
    step = 1
    while step < LIST:
        gap = step
        while gap >= 1:
            for base in range(gap % step, LIST - gap, 2 * gap):
                for i in range(min(gap, LIST - base - gap)):
                    a, b = base + i, base + i + gap
                    if a // (2 * step) == b // (2 * step):
                        keys[a], keys[b] = jnp.maximum(keys[a], keys[b]), jnp.minimum(keys[a], keys[b])
            gap //= 2
        step *= 2
    for l in range(LIST):
        far_ref[l] = jnp.where(keys[l] < 0, OPS * REMOTE, keys[l])
    count_ref[...] = jnp.max(used, axis=0, keepdims=True)


def early_kernel(
    me_ref, owner_hbm, rows_hbm, cell_hbm, freq_hbm, phase_hbm, entry_hbm, class_hbm,
    atoms_hbm, basis_hbm, pole_hbm, own_hbm, far_hbm, count_hbm,
    owner, rows, cell, freq, phase, entry, kind, entry3, kind3, flat, atoms_ref, basis_ref, pole_ref,
    own_ref, far_ref, count_ref, sems, out_sems,
):
    copies = load(
        sems, (owner_hbm, owner), (rows_hbm, rows), (cell_hbm, cell), (freq_hbm, freq), (phase_hbm, phase),
        (entry_hbm, entry), (class_hbm, kind),
    )
    atoms_ref[...] = jnp.zeros_like(atoms_ref)
    for copy in copies[:5]:
        copy.wait()
    stays = owner[...] == me_ref[0]
    atoms_ref[0:4, :] = jnp.where(stays, rows[...], 0.0)
    atoms_ref[4:5, :] = jnp.where(stays, (cell[...] + 1).astype(f32), 0.0)
    waves = waves_of(freq, phase, flat)
    width = 512
    for lo in range(0, STAY, width):
        atoms = atoms_ref[:, lo : lo + width]
        basis = basis_of(waves, atoms)
        basis_ref[:, lo : lo + width] = basis
        part = poles(basis, atoms[3:4, :], cell_hot(atoms[4:5, :].astype(i32)))
        pole_ref[...] = part if lo == 0 else pole_ref[...] + part
    outs = load(out_sems, (atoms_ref, atoms_hbm), (basis_ref, basis_hbm), (pole_ref, pole_hbm))
    for copy in copies[5:]:
        copy.wait()
    for l in range(LIST):
        for r in range(CELLS // LANES):
            entry3[l, r : r + 1, :] = entry[l : l + 1, r * LANES : (r + 1) * LANES]
            kind3[l, r : r + 1, :] = kind[l : l + 1, r * LANES : (r + 1) * LANES]
    order(me_ref[0], entry3[...], kind3[...], own_ref, far_ref, count_ref)
    more = [
        pltpu.make_async_copy(src, dst, out_sems.at[3 + i])
        for i, (src, dst) in enumerate(((own_ref, own_hbm), (far_ref, far_hbm), (count_ref, count_hbm)))
    ]
    for copy in more:
        copy.start()
    for copy in outs + more:
        copy.wait()


def merge_kernel(
    me_ref, got_ref, freq_hbm, phase_hbm, stay_hbm, up_hbm,
    send_ref, low_ref, high_ref, pole_hbm, basis_hbm, atoms_hbm,
    freq, phase, stay, up, flat, atoms_ref, basis_ref, pole_ref, ring, turned, ids, first_ref, sems, out_sems,
):
    copies = load(sems, (freq_hbm, freq), (phase_hbm, phase), (stay_hbm, stay), (up_hbm, up))
    me = me_ref[0]
    row = lax.broadcasted_iota(i32, (DEVICES, LANES), 0)
    lane = lax.broadcasted_iota(i32, (DEVICES, LANES), 1)
    asked = jnp.where(row == lane, got_ref[pl.ds(5, DEVICES, stride=PIECE), :], 0.0)
    ids[...] = jnp.maximum(jnp.sum(asked, axis=0, keepdims=True).astype(i32), 0)
    to_scalars = pltpu.make_async_copy(ids, first_ref, sems.at[4])
    to_scalars.start()
    atoms_ref[...] = jnp.zeros_like(atoms_ref)
    for at, by in enumerate((-2, -1, 1, 2)):
        source = me - by

        @pl.when((source >= 0) & (source < DEVICES))
        def _(at=at, source=source):
            atoms_ref[0:5, at * CAP : (at + 1) * CAP] = got_ref[pl.ds(source * PIECE, 5), :]

    copies[0].wait()
    copies[1].wait()
    atoms = atoms_ref[...]
    basis = basis_of(waves_of(freq, phase, flat), atoms)
    basis_ref[...] = basis
    both = poles(basis, atoms[3:4, :], cell_hot(atoms[4:5, :].astype(i32)))
    copies[2].wait()
    pole = stay[...] + both
    pole_ref[...] = pole
    outs = load(out_sems, (atoms_ref, atoms_hbm), (basis_ref, basis_hbm), (pole_ref, pole_hbm))
    ring[0:CELLS, :] = pole
    ring[CELLS:WRAP, :] = pole[0 : WRAP - CELLS, :]
    grouped = jnp.sum(pole.reshape(CELLS // 8, 8, LANES), axis=0)
    copies[3].wait()
    raised = up[...].reshape(COEF, OPS, COEF) * grouped[None, :, :COEF]
    turned[...] = jnp.zeros_like(turned)
    turned[0:COEF, 0:COEF] = jnp.sum(raised, axis=1)
    coarse = jnp.sum(turned[...].T, axis=0, keepdims=True)
    to_scalars.wait()

    def one(t, _):
        send_ref[pl.ds(t * BLOCK, SHORT), :] = ring[pl.ds(first_ref[0, t], SHORT), :]
        send_ref[pl.ds(t * BLOCK + SHORT, 1), :] = coarse
        return 0

    lax.fori_loop(0, DEVICES, one, 0, unroll=8)
    low_ref[...] = ring[pl.ds(first_ref[0, jnp.maximum(me - 1, 0)] + SHORT, EXTRA), :]
    high_ref[...] = ring[pl.ds(first_ref[0, jnp.minimum(me + 1, DEVICES - 1)] + SHORT, EXTRA), :]
    for copy in outs:
        copy.wait()


def load_ops(ops_ref, both):
    both[...] = jnp.zeros_like(both)
    for o in range(OPS):
        high, low = split(ops_ref[pl.ds(o, COEF, stride=OPS), :])
        for at, part in enumerate((high, high, low)):
            both[o * LANES : o * LANES + COEF, at * LANES : at * LANES + COEF] = part


def premultiply(rows, both, table, at, pitch):
    high, low = split(rows)
    out = lax.dot_general(jnp.concatenate([high, low, high], axis=1), both[...], NT, preferred_element_type=f32)
    for o in range(OPS):
        table[pl.ds(o * pitch + at, rows.shape[0]), :] = out[:, o * LANES : (o + 1) * LANES]


def index_of(index_ref, l, r, g):
    return index_ref.at[pl.ds(l * CELLS + r * LANES, LANES)][g]


def features(atoms_ref, left, right):
    def parts(value, count):
        out = []
        for _ in range(count):
            out.append(value.astype(bf16).astype(f32))
            value = value - out[-1]
        return out

    left[...] = jnp.zeros_like(left)
    right[...] = jnp.zeros_like(right)
    square = None
    for d in range(3):
        value = atoms_ref[d : d + 1, :]
        square = value * value if square is None else square + value * value
        for i, (a, b) in enumerate((a, b) for a in parts(value, 2) for b in parts(value, 2)):
            left[4 * d + i : 4 * d + i + 1, :] = a
            right[4 * d + i : 4 * d + i + 1, :] = -2.0 * b
    ones = jnp.ones_like(square)
    for i, part in enumerate(parts(square, 3)):
        left[12 + i : 13 + i, :] = part
        right[12 + i : 13 + i, :] = ones
    for i, part in enumerate(parts(square + 0.25, 3)):
        left[15 + i : 16 + i, :] = ones
        right[15 + i : 16 + i, :] = part


def pair_sums(atoms_ref, pair_ref, left, right, left_cols, cols, cells, far):
    features(atoms_ref, left, right)
    for lo in range(0, SLOTS, LANES):
        cols[lo : lo + LANES, :] = atoms_ref[:, lo : lo + LANES].T
        left_cols[lo : lo + LANES, :] = left[:, lo : lo + LANES].T
    cells[...] = jnp.broadcast_to(atoms_ref[4:5, :], (8, SLOTS))
    chunk = far.shape[0]

    def block(c, total):
        at = pl.multiple_of(c * chunk, chunk)
        far[...] = lax.dot_general(
            left_cols[pl.ds(at, chunk), :].astype(bf16), right[...].astype(bf16), NN, preferred_element_type=f32
        )

        def tile(i, total):
            down = cols[pl.ds(pl.multiple_of(at + i * 8, 8), 8), :]
            charge = jnp.where(down[:, 4:5] == cells[...], down[:, 3:4], 0.0)
            return total + charge * lax.rsqrt(far[pl.ds(pl.multiple_of(i * 8, 8), 8), :])

        return lax.fori_loop(0, chunk // 8, tile, total)

    total = lax.fori_loop(0, SLOTS // chunk, block, jnp.zeros((8, SLOTS), f32))
    itself = atoms_ref[3:4, :] * lax.rsqrt(jnp.full((1, SLOTS), 0.25, f32))
    pair_ref[...] = jnp.sum(total, axis=0, keepdims=True) - itself


def mid_kernel(
    own_ref, stay_hbm, new_hbm, pole_hbm, ops_hbm, sum_hbm, pair_hbm,
    table, both, ops, pole, atoms_ref, sum_ref, pair_ref, left, right, left_cols, cols, cells, far, sems, out_sems,
):
    copies = load(
        sems, (ops_hbm, ops), (pole_hbm, pole), (stay_hbm, atoms_ref.at[:, pl.ds(0, STAY)]),
        (new_hbm, atoms_ref.at[:, pl.ds(STAY, ARRIVE)]),
    )
    copies[0].wait()
    load_ops(ops, both)
    table[OPS * CELLS :, :] = jnp.zeros((8, LANES), f32)
    copies[1].wait()
    width = CELLS // 2
    for lo in range(0, CELLS, width):
        premultiply(pole[lo : lo + width, :], both, table, lo, CELLS)

    def gather(g, _):
        for r in range(8):
            total = None
            for l in range(LIST):
                row = table[pl.ds(index_of(own_ref, l, r, g), 1), :]
                total = row if total is None else total + row
            sum_ref[pl.ds(r * LANES + g, 1), :] = total
        return 0

    lax.fori_loop(0, LANES, gather, 0)
    sums_out = pltpu.make_async_copy(sum_ref, sum_hbm, out_sems.at[0])
    sums_out.start()
    copies[2].wait()
    copies[3].wait()
    pair_sums(atoms_ref, pair_ref, left, right, left_cols, cols, cells, far)
    pairs_out = pltpu.make_async_copy(pair_ref, pair_hbm, out_sems.at[1])
    pairs_out.start()
    sums_out.wait()
    pairs_out.wait()


def last_kernel(
    me_ref, index_ref, count_ref, far_ref, below_ref, above_ref, ops_hbm, sum_hbm, inner_hbm, outer_hbm, down_hbm,
    stay_hbm, new_hbm, stay_basis_hbm, new_basis_hbm, pair_hbm, local_ref, pot_ref,
    table, both, rows, coarse, ops, inner, outer, down, atoms_ref, basis_ref, pair, sems,
):
    copies = load(
        sems, (ops_hbm, ops), (sum_hbm, rows), (inner_hbm, inner), (outer_hbm, outer), (down_hbm, down),
        (stay_hbm, atoms_ref.at[:, pl.ds(0, STAY)]), (new_hbm, atoms_ref.at[:, pl.ds(STAY, ARRIVE)]),
        (stay_basis_hbm, basis_ref.at[:, pl.ds(0, STAY)]), (new_basis_hbm, basis_ref.at[:, pl.ds(STAY, ARRIVE)]),
        (pair_hbm, pair),
    )
    copies[0].wait()
    load_ops(ops, both)
    width = FAR_ROWS // 4
    for lo in range(0, FAR_ROWS, width):
        premultiply(far_ref[lo : lo + width, :], both, table, lo, REMOTE)
    premultiply(below_ref[...], both, table, FAR_ROWS, REMOTE)
    premultiply(above_ref[...], both, table, FAR_ROWS + EXTRA, REMOTE)
    table[OPS * REMOTE :, :] = jnp.zeros((8, LANES), f32)

    coarse[...] = far_ref[pl.ds(SHORT, DEVICES, stride=BLOCK), :]
    me = me_ref[0]
    group, member = me // MEMBERS, lax.rem(me, MEMBERS)
    who = lax.broadcasted_iota(i32, (40, DEVICES), 1)
    which = lax.broadcasted_iota(i32, (40, DEVICES), 0)
    its_group, its_member = who // MEMBERS, lax.rem(who, MEMBERS)
    near = (its_group == group) & (jnp.abs(its_member - member) - 1 == which) & (which < MEMBERS)
    away = (jnp.abs(its_group - group) - 1 == which - MEMBERS) & (which >= MEMBERS)
    chosen = jnp.where(near | away, 1.0, 0.0)
    sums = lax.dot_general(chosen, coarse[...], NN, precision=lax.Precision.HIGHEST, preferred_element_type=f32)
    for copy in copies[1:5]:
        copy.wait()
    field = jnp.sum(inner[...] * sums[None, 0 : MEMBERS - 1, 0:COEF], axis=1)
    for o in range(GROUPS - 1):
        field = field + outer[o] * sums[MEMBERS + o : MEMBERS + o + 1, 0:COEF]
    field = jnp.broadcast_to(jnp.sum(field, axis=1, keepdims=True), (COEF, LANES))
    child = lax.rem(lax.broadcasted_iota(i32, (COEF, LANES), 1), OPS)
    pattern = jnp.zeros((COEF, LANES), f32)
    for o in range(OPS):
        one = lax.dot_general(
            down[pl.ds(o, COEF, stride=OPS), :], field, NN,
            precision=lax.Precision.HIGHEST, preferred_element_type=f32,
        )
        pattern = jnp.where(child == o, one, pattern)

    def gather(g, _):
        def steps(count):
            totals = []
            for r in range(8):
                total = rows[pl.ds(r * LANES + g, 1), :]
                for l in range(count):
                    total = total + table[pl.ds(index_of(index_ref, l, r, g), 1), :]
                totals.append(total)
            return tuple(totals)

        used = count_ref[g]

        def tree(low, high):
            if low == high:
                return steps(2 * low)
            middle = (low + high) // 2
            return lax.cond(used <= 2 * middle, lambda: tree(low, middle), lambda: tree(middle + 1, high))

        totals = tree(1, LIST // 2)
        for r in range(8):
            rows[pl.ds(r * LANES + g, 1), :] = totals[r]
        return 0

    lax.fori_loop(0, LANES, gather, 0)

    for lo in range(0, CELLS, LANES):
        local_ref[:, lo : lo + LANES] = rows[lo : lo + LANES, :].T[0:COEF, :] + pattern
    local = local_ref[...]
    high, rest = split(local)
    high = jnp.concatenate([high, jnp.zeros((LANES - COEF, CELLS), bf16)], axis=0)
    rest = jnp.concatenate([rest, jnp.zeros((LANES - COEF, CELLS), bf16)], axis=0)
    stacked = jnp.concatenate([high, rest], axis=0)
    for copy in copies[5:]:
        copy.wait()
    wide = 512
    for lo in range(0, SLOTS, wide):
        cells, basis = atoms_ref[4:5, lo : lo + wide], basis_ref[:, lo : lo + wide]
        at = lax.dot_general(stacked, cell_hot(cells.astype(i32)), NN, preferred_element_type=f32)
        read = jnp.sum((at[:LANES] + at[LANES:]) * basis, axis=0, keepdims=True)
        pot_ref[:, lo : lo + wide] = read * COEF**-0.5 + pair[:, lo : lo + wide]


VM = pl.BlockSpec(memory_space=pltpu.VMEM)
SM = pl.BlockSpec(memory_space=pltpu.SMEM)
HB = pl.BlockSpec(memory_space=pltpu.HBM)


def call(kernel, name, ins, outs, scratch, copies, flops, *operands):
    cost = pl.CostEstimate(flops=flops, bytes_accessed=4 * MIB, transcendentals=0)
    return pl.pallas_call(
        kernel,
        name=name,
        in_specs=ins,
        out_specs=[spec for spec, _, _ in outs],
        out_shape=[jax.ShapeDtypeStruct(shape, kind) for _, shape, kind in outs],
        scratch_shapes=[pltpu.VMEM(shape, kind) if isinstance(shape, tuple) else shape for shape, kind in scratch]
        + [pltpu.SemaphoreType.DMA((count,)) for count in copies],
        cost_estimate=cost,
        compiler_params=pltpu.CompilerParams(vmem_limit_bytes=48 * MIB),
    )(*operands)


def on_device(
    atom_rows,
    atom_owner,
    atom_cell,
    need_cells,
    list_entry,
    list_class,
    basis_freq,
    basis_phase,
    near_ops,
    up_ops,
    far_in,
    far_out,
    down_ops,
):
    me = (lax.axis_index("group") * MEMBERS + lax.axis_index("dev")).reshape(1).astype(i32)
    freq, phase = basis_freq.T, basis_phase.reshape(1, COEF)
    waves = [((3, COEF), f32), ((1, COEF), f32)]
    owner_row, cell_row = atom_owner.reshape(1, STAY), atom_cell.reshape(1, STAY)
    by_row = [ops.transpose(1, 0, 2).reshape(COEF * OPS, COEF) for ops in (near_ops, up_ops, down_ops)]
    ops_shape = ((COEF * OPS, COEF), f32)
    mine = [((1, STAY), i32), ((4, STAY), f32), ((1, STAY), i32)]

    (outbound,) = call(
        pack_kernel, "pack", [SM, HB, HB, HB, HB], [(VM, (DEVICES * PIECE, LANES), f32)],
        [((8, LANES), i32), ((STAY // LANES, LANES), i32), *mine[1:], ((8, 512), f32)], [4], 10**6,
        me, need_cells.transpose(0, 2, 1), atom_owner.reshape(STAY // LANES, LANES), atom_rows, cell_row,
    )
    got = lax.all_to_all(outbound.reshape(DEVICES, 1, PIECE * LANES), AXES, split_axis=0, concat_axis=0, tiled=True)
    got = got.reshape(DEVICES * PIECE, LANES)

    shape3 = (LIST, CELLS // LANES, LANES)
    stay_outs = [((8, STAY), f32), ((LANES, STAY), f32), ((CELLS, LANES), f32), (shape3, i32), (shape3, i32), ((1, LANES), i32)]
    stay_atoms, stay_basis, stay_pole, own_index, far_index, counts = call(
        early_kernel, "early", [SM] + [HB] * 7, [(HB, *out) for out in stay_outs],
        [*mine, *waves, *[((LIST, CELLS), i32)] * 2, *[(shape3, i32)] * 2, ((8, LANES), f32), *stay_outs], [7, 6], 4 * 10**9,
        me, owner_row, atom_rows, cell_row, freq, phase, list_entry, list_class,
    )
    merge_outs = [((CELLS, LANES), f32), ((LANES, ARRIVE), f32), ((8, ARRIVE), f32)]
    send, low, high, pole, new_basis, new_atoms = call(
        merge_kernel, "merge", [SM, VM, HB, HB, HB, HB],
        [(VM, (FAR_ROWS, LANES), f32), (VM, (EXTRA, LANES), f32), (VM, (EXTRA, LANES), f32), *[(HB, *out) for out in merge_outs]],
        [*waves, ((CELLS, LANES), f32), ops_shape, ((8, LANES), f32), *merge_outs[::-1],
         ((WRAP, LANES), f32), ((LANES, LANES), f32), ((1, LANES), i32), (pltpu.SMEM((1, LANES), i32), None)],
        [5, 3], 2 * 10**9,
        me, got, freq, phase, stay_pole, by_row[1],
    )
    below, above = shift(high, 1), shift(low, -1)
    far_rows = lax.all_to_all(send.reshape(DEVICES, 1, BLOCK * LANES), AXES, split_axis=0, concat_axis=0, tiled=True)
    far_rows = far_rows.reshape(FAR_ROWS, LANES)
    mid_outs = [((CELLS, LANES), f32), ((1, SLOTS), f32)]
    own_sum, pair = call(
        mid_kernel, "mid", [SM, HB, HB, HB, HB], [(HB, *out) for out in mid_outs],
        [((OPS * CELLS + 8, LANES), f32), ((OPS * LANES, 3 * LANES), bf16), ops_shape, ((CELLS, LANES), f32), ((8, SLOTS), f32),
         *mid_outs, ((32, SLOTS), f32), ((32, SLOTS), f32), ((SLOTS, 32), f32), ((SLOTS, 8), f32), ((8, SLOTS), f32),
         ((256, SLOTS), f32)],
        [4, 2], 20 * 10**9,
        own_index.reshape(-1), stay_atoms, new_atoms, pole, by_row[0],
    )
    local, pot = call(
        last_kernel, "last", [SM, SM, SM, VM, VM, VM] + [HB] * 10, [(VM, (COEF, CELLS), f32), (VM, (1, SLOTS), f32)],
        [((OPS * REMOTE + 8, LANES), f32), ((OPS * LANES, 3 * LANES), bf16), ((CELLS, LANES), f32), ((DEVICES, LANES), f32), ops_shape,
         ((COEF, MEMBERS - 1, COEF), f32), ((GROUPS - 1, COEF, COEF), f32), ops_shape, ((8, SLOTS), f32), ((LANES, SLOTS), f32),
         ((1, SLOTS), f32)],
        [10], 8 * 10**9,
        me, far_index.reshape(-1), counts.reshape(-1), far_rows, below, above, by_row[0], own_sum,
        far_in.transpose(1, 0, 2), far_out, by_row[2], stay_atoms, new_atoms, stay_basis, new_basis, pair,
    )
    return local, pot.reshape(SLOTS)


def solution(mesh):
    in_specs = (
        P(None, AXES),
        P(AXES),
        P(AXES),
        P(AXES, None, None),
        P(None, AXES),
        P(None, AXES),
        P(),
        P(),
        P(),
        P(),
        P(),
        P(),
        P(),
    )
    out_specs = (P(None, AXES), P(AXES))
    return jax.shard_map(on_device, mesh=mesh, in_specs=in_specs, out_specs=out_specs, check_vma=False)
```

```python
import math

import jax
import jax.numpy as jnp
from jax import lax
from jax.experimental import pallas as pl
from jax.experimental.pallas import tpu as pltpu
from jax.sharding import PartitionSpec as P

COEF = 121
LANES = 128
CELLS = 1024
STAY = 2048
CAP = 128
ARRIVE = 4 * CAP
SLOTS = STAY + ARRIVE
LIST = 16
OPS = 8
SLOT = 72
SHORT = 18
BLOCK = SHORT + 1
DEVICES = 128
MEMBERS = 32
GROUPS = 4
PIECE = 6
EXTRA = 56
FAR_ROWS = DEVICES * BLOCK
REMOTE = FAR_ROWS + 2 * EXTRA
WRAP = CELLS + 80
TALL, WIDE = 128, 512
AXES = ("group", "dev")
MIB = 2**20
f32, bf16, i32 = jnp.float32, jnp.bfloat16, jnp.int32
SIN = [(-1) ** n * (2 * math.pi) ** (2 * n + 1) / math.factorial(2 * n + 1) for n in range(6)]

NT = (((1,), (1,)), ((), ()))
NN = (((1,), (0,)), ((), ()))


def shift(value, by):
    pairs = [(i, i + by) for i in range(DEVICES) if 0 <= i + by < DEVICES]
    return lax.ppermute(value, AXES, pairs)


def split(value):
    high = value.astype(bf16)
    return high, (value - high.astype(f32)).astype(bf16)


def basis_of(waves, atoms):
    turns = waves[:, 3:4] + waves[:, 0:1] * atoms[0:1, :]
    turns = turns + waves[:, 1:2] * atoms[1:2, :]
    turns = turns + waves[:, 2:3] * atoms[2:3, :]
    turns = turns - jnp.floor(turns + 0.5)
    base = 0.25 - jnp.abs(turns)
    square = base * base
    total = jnp.full_like(square, SIN[5])
    for factor in SIN[4::-1]:
        total = total * square + factor
    return base * total


def cell_hot(cell_row):
    ids = lax.broadcasted_iota(i32, (CELLS, cell_row.shape[1]), 0) + 1
    return jnp.where(ids == cell_row, 1.0, 0.0).astype(bf16)


def poles(basis, charge, hot):
    high, low = split(basis * charge)
    both = lax.dot_general(hot, jnp.concatenate([high, low], axis=0), NT, preferred_element_type=f32)
    return both[:, :LANES] + both[:, LANES:]


def load(sems, *pairs):
    copies = [pltpu.make_async_copy(src, dst, sems.at[i]) for i, (src, dst) in enumerate(pairs)]
    for copy in copies:
        copy.start()
    return copies


def waves_of(freq_ref, phase_ref, flat):
    flat[...] = jnp.zeros_like(flat)
    flat[0:3, 0:COEF] = freq_ref[...] * (0.5 / math.pi)
    flat[3:4, 0:COEF] = phase_ref[...] * (0.5 / math.pi)
    return flat[...].T


def pack_kernel(me_ref, need_hbm, owner_hbm, rows_hbm, cell_hbm, out_ref, need, owner, rows, cell, buf, sems):
    copies = load(
        sems, (owner_hbm, owner), (rows_hbm, rows), (cell_hbm, cell), (need_hbm.at[0, pl.ds(0, 8), :], need)
    )
    out_ref[...] = jnp.zeros_like(out_ref)
    buf[...] = jnp.zeros_like(buf)
    for copy in copies:
        copy.wait()
    me = me_ref[0]
    gap = owner[...] - me

    def count(by):
        return jnp.sum(jnp.where(gap == by, 1.0, 0.0)).astype(i32)

    for at, lo in ((0, 0), (256, STAY - 256)):
        buf[0:4, at : at + 256] = rows[:, lo : lo + 256]
        buf[4:5, at : at + 256] = (cell[:, lo : lo + 256] + 1).astype(f32)
    lane = lax.broadcasted_iota(i32, (8, CAP), 1)
    low2, low1, up1, up2 = count(-2), count(-1), count(1), count(2)
    first = jnp.broadcast_to(need[0:1, :].astype(f32), (LANES, LANES)).T
    out_ref[pl.ds(5, DEVICES, stride=PIECE), :] = first
    ahead = pltpu.roll(buf[:, :256], lax.rem(256 - low2, 256), 1)
    behind = pltpu.roll(buf[:, 256:], lax.rem(up1 + up2, 256), 1)
    last = pltpu.roll(buf[:, 256:], lax.rem(up2, 256), 1)
    for by, count_by, piece in (
        (-2, low2, buf[:, :CAP]), (-1, low1, ahead[:, :CAP]), (1, up1, behind[:, :CAP]), (2, up2, last[:, :CAP])
    ):
        to = me + by

        @pl.when((to >= 0) & (to < DEVICES))
        def _(to=to, count_by=count_by, piece=piece):
            out_ref[pl.ds(to * PIECE, 5), :] = jnp.where(lane < count_by, piece, 0.0)[0:5, :]


def order(me, entry, kind, own_ref, far_ref, count_ref):
    own_ref[...] = jnp.where(entry < CELLS, kind * CELLS + entry, OPS * CELLS)
    asked = jnp.maximum(entry - CELLS, 0)
    source = jnp.floor((asked.astype(f32) + 0.5) * (1.0 / SLOT)).astype(i32)
    slot = asked - source * SLOT
    side = jnp.where(source < me, FAR_ROWS, FAR_ROWS + EXTRA)
    row = jnp.where(slot < SHORT, source * BLOCK + slot, side + slot - SHORT)
    key = jnp.where(entry < CELLS, -1, kind * REMOTE + row)
    keys = [key[l] for l in range(LIST)]
    used = keys[0] * 0
    for one in keys:
        used = used + jnp.where(one >= 0, 1, 0)
    step = 1
    while step < LIST:
        gap = step
        while gap >= 1:
            for base in range(gap % step, LIST - gap, 2 * gap):
                for i in range(min(gap, LIST - base - gap)):
                    a, b = base + i, base + i + gap
                    if a // (2 * step) == b // (2 * step):
                        keys[a], keys[b] = jnp.maximum(keys[a], keys[b]), jnp.minimum(keys[a], keys[b])
            gap //= 2
        step *= 2
    for l in range(LIST):
        far_ref[l] = jnp.where(keys[l] < 0, OPS * REMOTE, keys[l])
    count_ref[...] = jnp.max(used, axis=0, keepdims=True)


def early_kernel(
    me_ref, owner_hbm, rows_hbm, cell_hbm, freq_hbm, phase_hbm, entry_hbm, class_hbm,
    atoms_hbm, basis_hbm, pole_hbm, own_hbm, far_hbm, count_hbm,
    owner, rows, cell, freq, phase, entry, kind, entry3, kind3, flat, atoms_ref, basis_ref, pole_ref,
    own_ref, far_ref, count_ref, sems, out_sems,
):
    copies = load(
        sems, (owner_hbm, owner), (rows_hbm, rows), (cell_hbm, cell), (freq_hbm, freq), (phase_hbm, phase),
        (entry_hbm, entry), (class_hbm, kind),
    )
    atoms_ref[...] = jnp.zeros_like(atoms_ref)
    for copy in copies[:5]:
        copy.wait()
    stays = owner[...] == me_ref[0]
    atoms_ref[0:4, :] = jnp.where(stays, rows[...], 0.0)
    atoms_ref[4:5, :] = jnp.where(stays, (cell[...] + 1).astype(f32), 0.0)
    waves = waves_of(freq, phase, flat)
    width = 512
    for lo in range(0, STAY, width):
        atoms = atoms_ref[:, lo : lo + width]
        basis = basis_of(waves, atoms)
        basis_ref[:, lo : lo + width] = basis
        part = poles(basis, atoms[3:4, :], cell_hot(atoms[4:5, :].astype(i32)))
        pole_ref[...] = part if lo == 0 else pole_ref[...] + part
    outs = load(out_sems, (atoms_ref, atoms_hbm), (basis_ref, basis_hbm), (pole_ref, pole_hbm))
    for copy in copies[5:]:
        copy.wait()
    for l in range(LIST):
        for r in range(CELLS // LANES):
            entry3[l, r : r + 1, :] = entry[l : l + 1, r * LANES : (r + 1) * LANES]
            kind3[l, r : r + 1, :] = kind[l : l + 1, r * LANES : (r + 1) * LANES]
    order(me_ref[0], entry3[...], kind3[...], own_ref, far_ref, count_ref)
    more = [
        pltpu.make_async_copy(src, dst, out_sems.at[3 + i])
        for i, (src, dst) in enumerate(((own_ref, own_hbm), (far_ref, far_hbm), (count_ref, count_hbm)))
    ]
    for copy in more:
        copy.start()
    for copy in outs + more:
        copy.wait()


def merge_kernel(
    me_ref, got_ref, freq_hbm, phase_hbm, stay_hbm, up_hbm,
    send_ref, low_ref, high_ref, pole_hbm, basis_hbm, atoms_hbm,
    freq, phase, stay, up, flat, atoms_ref, basis_ref, pole_ref, ring, turned, ids, first_ref, sems, out_sems,
):
    copies = load(sems, (freq_hbm, freq), (phase_hbm, phase), (stay_hbm, stay), (up_hbm, up))
    me = me_ref[0]
    row = lax.broadcasted_iota(i32, (DEVICES, LANES), 0)
    lane = lax.broadcasted_iota(i32, (DEVICES, LANES), 1)
    asked = jnp.where(row == lane, got_ref[pl.ds(5, DEVICES, stride=PIECE), :], 0.0)
    ids[...] = jnp.maximum(jnp.sum(asked, axis=0, keepdims=True).astype(i32), 0)
    to_scalars = pltpu.make_async_copy(ids, first_ref, sems.at[4])
    to_scalars.start()
    atoms_ref[...] = jnp.zeros_like(atoms_ref)
    for at, by in enumerate((-2, -1, 1, 2)):
        source = me - by

        @pl.when((source >= 0) & (source < DEVICES))
        def _(at=at, source=source):
            atoms_ref[0:5, at * CAP : (at + 1) * CAP] = got_ref[pl.ds(source * PIECE, 5), :]

    copies[0].wait()
    copies[1].wait()
    atoms = atoms_ref[...]
    basis = basis_of(waves_of(freq, phase, flat), atoms)
    basis_ref[...] = basis
    both = poles(basis, atoms[3:4, :], cell_hot(atoms[4:5, :].astype(i32)))
    copies[2].wait()
    pole = stay[...] + both
    pole_ref[...] = pole
    outs = load(out_sems, (atoms_ref, atoms_hbm), (basis_ref, basis_hbm), (pole_ref, pole_hbm))
    ring[0:CELLS, :] = pole
    ring[CELLS:WRAP, :] = pole[0 : WRAP - CELLS, :]
    grouped = jnp.sum(pole.reshape(CELLS // 8, 8, LANES), axis=0)
    copies[3].wait()
    raised = up[...].reshape(COEF, OPS, COEF) * grouped[None, :, :COEF]
    turned[...] = jnp.zeros_like(turned)
    turned[0:COEF, 0:COEF] = jnp.sum(raised, axis=1)
    coarse = jnp.sum(turned[...].T, axis=0, keepdims=True)
    to_scalars.wait()

    def one(t, _):
        send_ref[pl.ds(t * BLOCK, SHORT), :] = ring[pl.ds(first_ref[0, t], SHORT), :]
        send_ref[pl.ds(t * BLOCK + SHORT, 1), :] = coarse
        return 0

    lax.fori_loop(0, DEVICES, one, 0, unroll=8)
    low_ref[...] = ring[pl.ds(first_ref[0, jnp.maximum(me - 1, 0)] + SHORT, EXTRA), :]
    high_ref[...] = ring[pl.ds(first_ref[0, jnp.minimum(me + 1, DEVICES - 1)] + SHORT, EXTRA), :]
    for copy in outs:
        copy.wait()


def load_ops(ops_ref, both):
    both[...] = jnp.zeros_like(both)
    for o in range(OPS):
        high, low = split(ops_ref[pl.ds(o, COEF, stride=OPS), :])
        for at, part in enumerate((high, high, low)):
            both[o * LANES : o * LANES + COEF, at * LANES : at * LANES + COEF] = part


def premultiply(rows, both, table, at, pitch):
    high, low = split(rows)
    out = lax.dot_general(jnp.concatenate([high, low, high], axis=1), both[...], NT, preferred_element_type=f32)
    for o in range(OPS):
        table[pl.ds(o * pitch + at, rows.shape[0]), :] = out[:, o * LANES : (o + 1) * LANES]


def index_of(index_ref, l, r, g):
    return index_ref.at[pl.ds(l * CELLS + r * LANES, LANES)][g]


def features(atoms_ref, left, right):
    def parts(value, count):
        out = []
        for _ in range(count):
            out.append(value.astype(bf16).astype(f32))
            value = value - out[-1]
        return out

    left[...] = jnp.zeros_like(left)
    right[...] = jnp.zeros_like(right)
    square = None
    for d in range(3):
        value = atoms_ref[d : d + 1, :]
        square = value * value if square is None else square + value * value
        for i, (a, b) in enumerate((a, b) for a in parts(value, 2) for b in parts(value, 2)):
            left[4 * d + i : 4 * d + i + 1, :] = a
            right[4 * d + i : 4 * d + i + 1, :] = -2.0 * b
    ones = jnp.ones_like(square)
    for i, part in enumerate(parts(square, 3)):
        left[12 + i : 13 + i, :] = part
        right[12 + i : 13 + i, :] = ones
    for i, part in enumerate(parts(square + 0.25, 3)):
        left[15 + i : 16 + i, :] = ones
        right[15 + i : 16 + i, :] = part


def pair_sums(atoms_ref, pair_ref, left, right, left_cols, right_low, charges, cells, back):
    features(atoms_ref, left, right)
    right_low[...] = right[...].astype(bf16)
    for lo in range(0, SLOTS, LANES):
        cut = slice(lo, lo + LANES)
        left_cols[cut, :] = left[:, cut].T.astype(bf16)
        charges[cut, :] = jnp.broadcast_to(atoms_ref[3:4, cut], (LANES, LANES)).T
        cells[cut, :] = jnp.broadcast_to(atoms_ref[4:5, cut], (LANES, LANES)).T
    back[...] = jnp.zeros_like(back)
    itself = atoms_ref[3:4, :] * lax.rsqrt(jnp.full((1, SLOTS), 0.25, f32))
    pair_ref[...] = -itself

    def near_ones(c, j):
        at, lo = pl.multiple_of(c * TALL, TALL), pl.multiple_of(j * WIDE, WIDE)
        far = lax.dot_general(
            left_cols[pl.ds(at, TALL), :], right_low[:, pl.ds(lo, WIDE)], NN, preferred_element_type=f32
        )
        its_cell = jnp.concatenate([cells[pl.ds(at, TALL), :]] * (WIDE // LANES), axis=1)
        its_charge = jnp.concatenate([charges[pl.ds(at, TALL), :]] * (WIDE // LANES), axis=1)
        near = jnp.where(its_cell == atoms_ref[4:5, pl.ds(lo, WIDE)], lax.rsqrt(far), 0.0)
        total = jnp.sum((near * its_charge).reshape(TALL // 8, 8, WIDE), axis=0)
        pair_ref[:, pl.ds(lo, WIDE)] += jnp.sum(total, axis=0, keepdims=True)
        return at, lo, near

    def row(c, _):
        diagonal = c // (WIDE // TALL)
        near_ones(c, diagonal)

        def block(j, _):
            at, lo, near = near_ones(c, j)
            near = near * atoms_ref[3:4, pl.ds(lo, WIDE)]
            total = near[:, 0:LANES]
            for k in range(1, WIDE // LANES):
                total = total + near[:, k * LANES : (k + 1) * LANES]
            back[pl.ds(at, TALL), :] += total
            return 0

        lax.fori_loop(diagonal + 1, SLOTS // WIDE, block, 0)
        return 0

    lax.fori_loop(0, SLOTS // TALL, row, 0)
    for lo in range(0, SLOTS, LANES):
        cut = slice(lo, lo + LANES)
        pair_ref[:, cut] += jnp.sum(back[cut, :].T, axis=0, keepdims=True)


def mid_kernel(
    own_ref, stay_hbm, new_hbm, pole_hbm, ops_hbm, sum_hbm, pair_hbm,
    table, both, ops, pole, atoms_ref, sum_ref, pair_ref, left, right, left_cols, right_low, charges, cells, back,
    sems, out_sems,
):
    copies = load(
        sems, (ops_hbm, ops), (pole_hbm, pole), (stay_hbm, atoms_ref.at[:, pl.ds(0, STAY)]),
        (new_hbm, atoms_ref.at[:, pl.ds(STAY, ARRIVE)]),
    )
    copies[0].wait()
    load_ops(ops, both)
    table[OPS * CELLS :, :] = jnp.zeros((8, LANES), f32)
    copies[1].wait()
    width = CELLS // 2
    for lo in range(0, CELLS, width):
        premultiply(pole[lo : lo + width, :], both, table, lo, CELLS)

    def gather(g, _):
        for r in range(8):
            total = None
            for l in range(LIST):
                row = table[pl.ds(index_of(own_ref, l, r, g), 1), :]
                total = row if total is None else total + row
            sum_ref[pl.ds(r * LANES + g, 1), :] = total
        return 0

    lax.fori_loop(0, LANES, gather, 0)
    sums_out = pltpu.make_async_copy(sum_ref, sum_hbm, out_sems.at[0])
    sums_out.start()
    copies[2].wait()
    copies[3].wait()
    pair_sums(atoms_ref, pair_ref, left, right, left_cols, right_low, charges, cells, back)
    pairs_out = pltpu.make_async_copy(pair_ref, pair_hbm, out_sems.at[1])
    pairs_out.start()
    sums_out.wait()
    pairs_out.wait()


def last_kernel(
    me_ref, index_ref, count_ref, far_ref, below_ref, above_ref, ops_hbm, sum_hbm, inner_hbm, outer_hbm, down_hbm,
    stay_hbm, new_hbm, stay_basis_hbm, new_basis_hbm, pair_hbm, local_ref, pot_ref,
    table, both, rows, coarse, ops, inner, outer, down, atoms_ref, basis_ref, pair, sems,
):
    copies = load(
        sems, (ops_hbm, ops), (sum_hbm, rows), (inner_hbm, inner), (outer_hbm, outer), (down_hbm, down),
        (stay_hbm, atoms_ref.at[:, pl.ds(0, STAY)]), (new_hbm, atoms_ref.at[:, pl.ds(STAY, ARRIVE)]),
        (stay_basis_hbm, basis_ref.at[:, pl.ds(0, STAY)]), (new_basis_hbm, basis_ref.at[:, pl.ds(STAY, ARRIVE)]),
        (pair_hbm, pair),
    )
    copies[0].wait()
    load_ops(ops, both)
    width = FAR_ROWS // 4
    for lo in range(0, FAR_ROWS, width):
        premultiply(far_ref[lo : lo + width, :], both, table, lo, REMOTE)
    premultiply(below_ref[...], both, table, FAR_ROWS, REMOTE)
    premultiply(above_ref[...], both, table, FAR_ROWS + EXTRA, REMOTE)
    table[OPS * REMOTE :, :] = jnp.zeros((8, LANES), f32)

    coarse[...] = far_ref[pl.ds(SHORT, DEVICES, stride=BLOCK), :]
    me = me_ref[0]
    group, member = me // MEMBERS, lax.rem(me, MEMBERS)
    who = lax.broadcasted_iota(i32, (40, DEVICES), 1)
    which = lax.broadcasted_iota(i32, (40, DEVICES), 0)
    its_group, its_member = who // MEMBERS, lax.rem(who, MEMBERS)
    near = (its_group == group) & (jnp.abs(its_member - member) - 1 == which) & (which < MEMBERS)
    away = (jnp.abs(its_group - group) - 1 == which - MEMBERS) & (which >= MEMBERS)
    chosen = jnp.where(near | away, 1.0, 0.0)
    sums = lax.dot_general(chosen, coarse[...], NN, precision=lax.Precision.HIGHEST, preferred_element_type=f32)
    for copy in copies[1:5]:
        copy.wait()
    field = jnp.sum(inner[...] * sums[None, 0 : MEMBERS - 1, 0:COEF], axis=1)
    for o in range(GROUPS - 1):
        field = field + outer[o] * sums[MEMBERS + o : MEMBERS + o + 1, 0:COEF]
    field = jnp.broadcast_to(jnp.sum(field, axis=1, keepdims=True), (COEF, LANES))
    child = lax.rem(lax.broadcasted_iota(i32, (COEF, LANES), 1), OPS)
    pattern = jnp.zeros((COEF, LANES), f32)
    for o in range(OPS):
        one = lax.dot_general(
            down[pl.ds(o, COEF, stride=OPS), :], field, NN,
            precision=lax.Precision.HIGHEST, preferred_element_type=f32,
        )
        pattern = jnp.where(child == o, one, pattern)

    def gather(g, _):
        def steps(count):
            totals = []
            for r in range(8):
                total = rows[pl.ds(r * LANES + g, 1), :]
                for l in range(count):
                    total = total + table[pl.ds(index_of(index_ref, l, r, g), 1), :]
                totals.append(total)
            return tuple(totals)

        used = count_ref[g]

        def tree(low, high):
            if low == high:
                return steps(2 * low)
            middle = (low + high) // 2
            return lax.cond(used <= 2 * middle, lambda: tree(low, middle), lambda: tree(middle + 1, high))

        totals = tree(1, LIST // 2)
        for r in range(8):
            rows[pl.ds(r * LANES + g, 1), :] = totals[r]
        return 0

    lax.fori_loop(0, LANES, gather, 0)

    for lo in range(0, CELLS, LANES):
        local_ref[:, lo : lo + LANES] = rows[lo : lo + LANES, :].T[0:COEF, :] + pattern
    local = local_ref[...]
    high, rest = split(local)
    high = jnp.concatenate([high, jnp.zeros((LANES - COEF, CELLS), bf16)], axis=0)
    rest = jnp.concatenate([rest, jnp.zeros((LANES - COEF, CELLS), bf16)], axis=0)
    stacked = jnp.concatenate([high, rest], axis=0)
    for copy in copies[5:]:
        copy.wait()
    wide = 512
    for lo in range(0, SLOTS, wide):
        cells, basis = atoms_ref[4:5, lo : lo + wide], basis_ref[:, lo : lo + wide]
        at = lax.dot_general(stacked, cell_hot(cells.astype(i32)), NN, preferred_element_type=f32)
        read = jnp.sum((at[:LANES] + at[LANES:]) * basis, axis=0, keepdims=True)
        read = read * COEF**-0.5 + pair[:, lo : lo + wide]
        for at in range(0, wide, LANES):
            i = (lo + at) // LANES
            pot_ref[i : i + 1, :] = read[:, at : at + LANES]


VM = pl.BlockSpec(memory_space=pltpu.VMEM)
SM = pl.BlockSpec(memory_space=pltpu.SMEM)
HB = pl.BlockSpec(memory_space=pltpu.HBM)


def call(kernel, name, ins, outs, scratch, copies, flops, *operands):
    cost = pl.CostEstimate(flops=flops, bytes_accessed=4 * MIB, transcendentals=0)
    return pl.pallas_call(
        kernel,
        name=name,
        in_specs=ins,
        out_specs=[spec for spec, _, _ in outs],
        out_shape=[jax.ShapeDtypeStruct(shape, kind) for _, shape, kind in outs],
        scratch_shapes=[pltpu.VMEM(shape, kind) if isinstance(shape, tuple) else shape for shape, kind in scratch]
        + [pltpu.SemaphoreType.DMA((count,)) for count in copies],
        cost_estimate=cost,
        compiler_params=pltpu.CompilerParams(vmem_limit_bytes=60 * MIB),
    )(*operands)


def on_device(
    atom_rows,
    atom_owner,
    atom_cell,
    need_cells,
    list_entry,
    list_class,
    basis_freq,
    basis_phase,
    near_ops,
    up_ops,
    far_in,
    far_out,
    down_ops,
):
    me = (lax.axis_index("group") * MEMBERS + lax.axis_index("dev")).reshape(1).astype(i32)
    freq, phase = basis_freq.T, basis_phase.reshape(1, COEF)
    waves = [((3, COEF), f32), ((1, COEF), f32)]
    owner_row, cell_row = atom_owner.reshape(1, STAY), atom_cell.reshape(1, STAY)
    by_row = [ops.transpose(1, 0, 2).reshape(COEF * OPS, COEF) for ops in (near_ops, up_ops, down_ops)]
    ops_shape = ((COEF * OPS, COEF), f32)
    mine = [((1, STAY), i32), ((4, STAY), f32), ((1, STAY), i32)]

    (outbound,) = call(
        pack_kernel, "pack", [SM, HB, HB, HB, HB], [(VM, (DEVICES * PIECE, LANES), f32)],
        [((8, LANES), i32), ((STAY // LANES, LANES), i32), *mine[1:], ((8, 512), f32)], [4], 10**6,
        me, need_cells.transpose(0, 2, 1), atom_owner.reshape(STAY // LANES, LANES), atom_rows, cell_row,
    )
    got = lax.all_to_all(outbound.reshape(DEVICES, 1, PIECE * LANES), AXES, split_axis=0, concat_axis=0, tiled=True)
    got = got.reshape(DEVICES * PIECE, LANES)

    shape3 = (LIST, CELLS // LANES, LANES)
    stay_outs = [((8, STAY), f32), ((LANES, STAY), f32), ((CELLS, LANES), f32), (shape3, i32), (shape3, i32), ((1, LANES), i32)]
    stay_atoms, stay_basis, stay_pole, own_index, far_index, counts = call(
        early_kernel, "early", [SM] + [HB] * 7, [(HB, *out) for out in stay_outs],
        [*mine, *waves, *[((LIST, CELLS), i32)] * 2, *[(shape3, i32)] * 2, ((8, LANES), f32), *stay_outs], [7, 6], 4 * 10**9,
        me, owner_row, atom_rows, cell_row, freq, phase, list_entry, list_class,
    )
    merge_outs = [((CELLS, LANES), f32), ((LANES, ARRIVE), f32), ((8, ARRIVE), f32)]
    send, low, high, pole, new_basis, new_atoms = call(
        merge_kernel, "merge", [SM, VM, HB, HB, HB, HB],
        [(VM, (FAR_ROWS, LANES), f32), (VM, (EXTRA, LANES), f32), (VM, (EXTRA, LANES), f32), *[(HB, *out) for out in merge_outs]],
        [*waves, ((CELLS, LANES), f32), ops_shape, ((8, LANES), f32), *merge_outs[::-1],
         ((WRAP, LANES), f32), ((LANES, LANES), f32), ((1, LANES), i32), (pltpu.SMEM((1, LANES), i32), None)],
        [5, 3], 2 * 10**9,
        me, got, freq, phase, stay_pole, by_row[1],
    )
    below, above = shift(high, 1), shift(low, -1)
    far_rows = lax.all_to_all(send.reshape(DEVICES, 1, BLOCK * LANES), AXES, split_axis=0, concat_axis=0, tiled=True)
    far_rows = far_rows.reshape(FAR_ROWS, LANES)
    mid_outs = [((CELLS, LANES), f32), ((1, SLOTS), f32)]
    own_sum, pair = call(
        mid_kernel, "mid", [SM, HB, HB, HB, HB], [(HB, *out) for out in mid_outs],
        [((OPS * CELLS + 8, LANES), f32), ((OPS * LANES, 3 * LANES), bf16), ops_shape, ((CELLS, LANES), f32), ((8, SLOTS), f32),
         *mid_outs, ((32, SLOTS), f32), ((32, SLOTS), f32), ((SLOTS, 32), bf16), ((32, SLOTS), bf16),
         *[((SLOTS, LANES), f32)] * 3],
        [4, 2], 20 * 10**9,
        own_index.reshape(-1), stay_atoms, new_atoms, pole, by_row[0],
    )
    local, pot = call(
        last_kernel, "last", [SM, SM, SM, VM, VM, VM] + [HB] * 10, [(VM, (COEF, CELLS), f32), (VM, (SLOTS // LANES, LANES), f32)],
        [((OPS * REMOTE + 8, LANES), f32), ((OPS * LANES, 3 * LANES), bf16), ((CELLS, LANES), f32), ((DEVICES, LANES), f32), ops_shape,
         ((COEF, MEMBERS - 1, COEF), f32), ((GROUPS - 1, COEF, COEF), f32), ops_shape, ((8, SLOTS), f32), ((LANES, SLOTS), f32),
         ((1, SLOTS), f32)],
        [10], 8 * 10**9,
        me, far_index.reshape(-1), counts.reshape(-1), far_rows, below, above, by_row[0], own_sum,
        far_in.transpose(1, 0, 2), far_out, by_row[2], stay_atoms, new_atoms, stay_basis, new_basis, pair,
    )
    return local, pot.reshape(SLOTS)


def solution(mesh):
    in_specs = (
        P(None, AXES),
        P(AXES),
        P(AXES),
        P(AXES, None, None),
        P(None, AXES),
        P(None, AXES),
        P(),
        P(),
        P(),
        P(),
        P(),
        P(),
        P(),
    )
    out_specs = (P(None, AXES), P(AXES))
    return jax.shard_map(on_device, mesh=mesh, in_specs=in_specs, out_specs=out_specs, check_vma=False)
```

```python
import math

import jax
import jax.numpy as jnp
from jax import lax
from jax.experimental import pallas as pl
from jax.experimental.pallas import tpu as pltpu
from jax.sharding import PartitionSpec as P

COEF = 121
LANES = 128
CELLS = 1024
STAY = 2048
CAP = 128
ARRIVE = 4 * CAP
SLOTS = STAY + ARRIVE
LIST = 16
OPS = 8
SLOT = 72
SHORT = 18
BLOCK = SHORT + 1
DEVICES = 128
MEMBERS = 32
GROUPS = 4
PIECE = 6
EXTRA = 56
FAR_ROWS = DEVICES * BLOCK
REMOTE = FAR_ROWS + 2 * EXTRA
WRAP = CELLS + 80
TALL, WIDE = 256, 512
AXES = ("group", "dev")
MIB = 2**20
f32, bf16, i32 = jnp.float32, jnp.bfloat16, jnp.int32
SIN = [(-1) ** n * (2 * math.pi) ** (2 * n + 1) / math.factorial(2 * n + 1) for n in range(6)]

NT = (((1,), (1,)), ((), ()))
NN = (((1,), (0,)), ((), ()))


def shift(value, by):
    pairs = [(i, i + by) for i in range(DEVICES) if 0 <= i + by < DEVICES]
    return lax.ppermute(value, AXES, pairs)


def split(value):
    high = value.astype(bf16)
    return high, (value - high.astype(f32)).astype(bf16)


def basis_of(waves, atoms):
    turns = waves[:, 3:4] + waves[:, 0:1] * atoms[0:1, :]
    turns = turns + waves[:, 1:2] * atoms[1:2, :]
    turns = turns + waves[:, 2:3] * atoms[2:3, :]
    turns = turns - jnp.floor(turns + 0.5)
    base = 0.25 - jnp.abs(turns)
    square = base * base
    total = jnp.full_like(square, SIN[5])
    for factor in SIN[4::-1]:
        total = total * square + factor
    return base * total


def cell_hot(cell_row):
    ids = lax.broadcasted_iota(i32, (CELLS, cell_row.shape[1]), 0) + 1
    return jnp.where(ids == cell_row, 1.0, 0.0).astype(bf16)


def poles(basis, charge, hot):
    high, low = split(basis * charge)
    both = lax.dot_general(hot, jnp.concatenate([high, low], axis=0), NT, preferred_element_type=f32)
    return both[:, :LANES] + both[:, LANES:]


def load(sems, *pairs):
    copies = [pltpu.make_async_copy(src, dst, sems.at[i]) for i, (src, dst) in enumerate(pairs)]
    for copy in copies:
        copy.start()
    return copies


def waves_of(freq_ref, phase_ref, flat):
    flat[...] = jnp.zeros_like(flat)
    flat[0:3, 0:COEF] = freq_ref[...] * (0.5 / math.pi)
    flat[3:4, 0:COEF] = phase_ref[...] * (0.5 / math.pi)
    return flat[...].T


def pack_kernel(me_ref, need_hbm, owner_hbm, rows_hbm, cell_hbm, out_ref, need, owner, rows, cell, buf, sems):
    copies = load(
        sems, (owner_hbm, owner), (rows_hbm, rows), (cell_hbm, cell), (need_hbm.at[0, pl.ds(0, 8), :], need)
    )
    out_ref[...] = jnp.zeros_like(out_ref)
    buf[...] = jnp.zeros_like(buf)
    for copy in copies:
        copy.wait()
    me = me_ref[0]
    gap = owner[...] - me

    def count(by):
        return jnp.sum(jnp.where(gap == by, 1.0, 0.0)).astype(i32)

    for at, lo in ((0, 0), (256, STAY - 256)):
        buf[0:4, at : at + 256] = rows[:, lo : lo + 256]
        buf[4:5, at : at + 256] = (cell[:, lo : lo + 256] + 1).astype(f32)
    lane = lax.broadcasted_iota(i32, (8, CAP), 1)
    low2, low1, up1, up2 = count(-2), count(-1), count(1), count(2)
    first = jnp.broadcast_to(need[0:1, :].astype(f32), (LANES, LANES)).T
    out_ref[pl.ds(5, DEVICES, stride=PIECE), :] = first
    ahead = pltpu.roll(buf[:, :256], lax.rem(256 - low2, 256), 1)
    behind = pltpu.roll(buf[:, 256:], lax.rem(up1 + up2, 256), 1)
    last = pltpu.roll(buf[:, 256:], lax.rem(up2, 256), 1)
    for by, count_by, piece in (
        (-2, low2, buf[:, :CAP]), (-1, low1, ahead[:, :CAP]), (1, up1, behind[:, :CAP]), (2, up2, last[:, :CAP])
    ):
        to = me + by

        @pl.when((to >= 0) & (to < DEVICES))
        def _(to=to, count_by=count_by, piece=piece):
            out_ref[pl.ds(to * PIECE, 5), :] = jnp.where(lane < count_by, piece, 0.0)[0:5, :]


def features(atoms_ref, left, right):
    def parts(value, count):
        out = []
        for _ in range(count):
            out.append(value.astype(bf16).astype(f32))
            value = value - out[-1]
        return out

    left[...] = jnp.zeros_like(left)
    right[...] = jnp.zeros_like(right)
    square = None
    for d in range(3):
        value = atoms_ref[d : d + 1, :]
        square = value * value if square is None else square + value * value
        for i, (a, b) in enumerate((a, b) for a in parts(value, 2) for b in parts(value, 2)):
            left[4 * d + i : 4 * d + i + 1, :] = a
            right[4 * d + i : 4 * d + i + 1, :] = -2.0 * b
    ones = jnp.ones_like(square)
    for i, part in enumerate(parts(square, 3)):
        left[12 + i : 13 + i, :] = part
        right[12 + i : 13 + i, :] = ones
    for i, part in enumerate(parts(square + 0.25, 3)):
        left[15 + i : 16 + i, :] = ones
        right[15 + i : 16 + i, :] = part


class Pairs:
    def __init__(self, atoms_ref, pair_ref, left, right, left_cols, right_low, charges, cells, back, start):
        self.atoms, self.pair, self.left_cols, self.right_low = atoms_ref, pair_ref, left_cols, right_low
        self.charges, self.cells, self.back, self.start = charges, cells, back, start
        features(atoms_ref, left, right)
        right_low[...] = right[...].astype(bf16)
        for at in range(0, left_cols.shape[0], LANES):
            cut, rows = slice(start + at, start + at + LANES), slice(at, at + LANES)
            left_cols[rows, :] = left[:, cut].T.astype(bf16)
            charges[rows, :] = jnp.broadcast_to(atoms_ref[3:4, cut], (LANES, LANES)).T
            cells[rows, :] = jnp.broadcast_to(atoms_ref[4:5, cut], (LANES, LANES)).T
        back[...] = jnp.zeros_like(back)

    def block(self, at, lo, both):
        far = lax.dot_general(
            self.left_cols[pl.ds(at, TALL), :], self.right_low[:, pl.ds(lo, WIDE)], NN, preferred_element_type=f32
        )
        its_cell = jnp.concatenate([self.cells[pl.ds(at, TALL), :]] * (WIDE // LANES), axis=1)
        its_charge = jnp.concatenate([self.charges[pl.ds(at, TALL), :]] * (WIDE // LANES), axis=1)
        near = jnp.where(its_cell == self.atoms[4:5, pl.ds(lo, WIDE)], lax.rsqrt(far), 0.0)
        total = jnp.sum((near * its_charge).reshape(TALL // 8, 8, WIDE), axis=0)
        self.pair[:, pl.ds(lo, WIDE)] += jnp.sum(total, axis=0, keepdims=True)
        if both:
            near = near * self.atoms[3:4, pl.ds(lo, WIDE)]
            total = near[:, 0:LANES]
            for k in range(1, WIDE // LANES):
                total = total + near[:, k * LANES : (k + 1) * LANES]
            self.back[pl.ds(at, TALL), :] += total

    def close(self):
        for at in range(0, self.back.shape[0], LANES):
            cut = slice(self.start + at, self.start + at + LANES)
            itself = self.atoms[3:4, cut] * lax.rsqrt(jnp.full((1, LANES), 0.25, f32))
            self.pair[:, cut] += jnp.sum(self.back[at : at + LANES, :].T, axis=0, keepdims=True) - itself


def pair_scratch(slots, rows):
    return [
        ((32, slots), f32), ((32, slots), f32), ((rows, 32), bf16), ((32, slots), bf16),
        *[((rows, LANES), f32)] * 3,
    ]


def sort_rows(keys):
    keys = list(keys)
    step = 1
    while step < LIST:
        gap = step
        while gap >= 1:
            for base in range(gap % step, LIST - gap, 2 * gap):
                for i in range(min(gap, LIST - base - gap)):
                    a, b = base + i, base + i + gap
                    if a // (2 * step) == b // (2 * step):
                        keys[a], keys[b] = jnp.maximum(keys[a], keys[b]), jnp.minimum(keys[a], keys[b])
            gap //= 2
        step *= 2
    return keys


def order(me, entry, kind, own_ref, far_ref, cell_ref, count_ref, lists):
    asked = jnp.maximum(entry - CELLS, 0)
    source = jnp.floor((asked.astype(f32) + 0.5) * (1.0 / SLOT)).astype(i32)
    slot = asked - source * SLOT
    side = jnp.where(source < me, FAR_ROWS, FAR_ROWS + EXTRA)
    row = jnp.where(slot < SHORT, source * BLOCK + slot, side + slot - SHORT)
    key = jnp.where(entry < CELLS, -1, kind * REMOTE + row)
    used = jnp.sum(jnp.where(key >= 0, 1, 0), axis=0)
    far = sort_rows(key[l] for l in range(LIST))
    key = jnp.where(entry < CELLS, kind * CELLS + entry, -1)
    own = sort_rows(key[l] for l in range(LIST))
    own = [jnp.where(one < 0, OPS * CELLS, one) for one in own]
    far = [jnp.where(one < 0, OPS * REMOTE, one) for one in far]

    def flat(value):
        return jnp.concatenate([value[r : r + 1, :] for r in range(CELLS // LANES)], axis=1)

    used_row = flat(used).astype(f32)
    rank_key = used_row * CELLS + lax.broadcasted_iota(i32, (1, CELLS), 1).astype(f32)
    rank = jnp.zeros((8, CELLS), f32)
    for lo in range(0, CELLS, LANES):
        column = jnp.broadcast_to(rank_key[:, lo : lo + LANES], (LANES, LANES)).T
        ahead = jnp.where(jnp.concatenate([column] * (CELLS // LANES), axis=1) > rank_key, 1.0, 0.0)
        rank = rank + jnp.sum(ahead.reshape(LANES // 8, 8, CELLS), axis=0)
    rank = jnp.sum(rank, axis=0, keepdims=True).astype(i32)
    place = (rank & 7) * LANES + (rank >> 3)
    moved = jnp.where(lax.broadcasted_iota(i32, (CELLS, CELLS), 0) == place, 1.0, 0.0).astype(bf16)
    lists[...] = jnp.zeros_like(lists)
    for l in range(LIST):
        for at, value in ((l, far[l] >> 8), (16 + l, far[l] & 255), (32 + l, own[l] >> 8), (48 + l, own[l] & 255)):
            for r in range(CELLS // LANES):
                lists[at : at + 1, r * LANES : (r + 1) * LANES] = value[r : r + 1, :].astype(f32)
    ids = lax.broadcasted_iota(i32, (1, CELLS), 1)
    lists[64:65, :] = (ids >> 8).astype(f32)
    lists[65:66, :] = (ids & 255).astype(f32)
    lists[66:67, :] = used_row
    sorted_lists = lax.dot_general(lists[...].astype(bf16), moved, NT, preferred_element_type=f32).astype(i32)
    far_rows = sorted_lists[0:16] * 256 + sorted_lists[16:32]
    own_rows = sorted_lists[32:48] * 256 + sorted_lists[48:64]
    cells = sorted_lists[64:65] * 256 + sorted_lists[65:66]
    for r in range(CELLS // LANES):
        cut = slice(r * LANES, (r + 1) * LANES)
        for l in range(LIST):
            far_ref[l, r : r + 1, :] = far_rows[l : l + 1, cut]
            own_ref[l, r : r + 1, :] = own_rows[l : l + 1, cut]
        cell_ref[r : r + 1, :] = cells[:, cut]
    count_ref[...] = jnp.zeros_like(count_ref)
    count_ref[0:1, :] = sorted_lists[66:67, 0:LANES]
    count_ref[1:2, :] = LIST - sorted_lists[66:67, CELLS - LANES : CELLS]


def early_kernel(
    me_ref, owner_hbm, rows_hbm, cell_hbm, freq_hbm, phase_hbm, entry_hbm, class_hbm,
    atoms_hbm, basis_hbm, pole_hbm, pair_hbm, own_hbm, far_hbm, place_hbm, count_hbm,
    owner, rows, cell, freq, phase, entry, kind, entry3, kind3, lists, flat,
    atoms_ref, basis_ref, pole_ref, pair_ref, own_ref, far_ref, place_ref, count_ref, *rest,
):
    *pair_buffers, sems, out_sems = rest
    copies = load(
        sems, (owner_hbm, owner), (rows_hbm, rows), (cell_hbm, cell), (freq_hbm, freq), (phase_hbm, phase),
        (entry_hbm, entry), (class_hbm, kind),
    )
    atoms_ref[...] = jnp.zeros_like(atoms_ref)
    for copy in copies[:5]:
        copy.wait()
    stays = owner[...] == me_ref[0]
    atoms_ref[0:4, :] = jnp.where(stays, rows[...], 0.0)
    atoms_ref[4:5, :] = jnp.where(stays, (cell[...] + 1).astype(f32), 0.0)
    waves = waves_of(freq, phase, flat)
    width = 512
    for lo in range(0, STAY, width):
        atoms = atoms_ref[:, lo : lo + width]
        basis = basis_of(waves, atoms)
        basis_ref[:, lo : lo + width] = basis
        part = poles(basis, atoms[3:4, :], cell_hot(atoms[4:5, :].astype(i32)))
        pole_ref[...] = part if lo == 0 else pole_ref[...] + part
    outs = load(out_sems, (atoms_ref, atoms_hbm), (basis_ref, basis_hbm), (pole_ref, pole_hbm))
    for copy in copies[5:]:
        copy.wait()
    for l in range(LIST):
        for r in range(CELLS // LANES):
            entry3[l, r : r + 1, :] = entry[l : l + 1, r * LANES : (r + 1) * LANES]
            kind3[l, r : r + 1, :] = kind[l : l + 1, r * LANES : (r + 1) * LANES]
    order(me_ref[0], entry3[...], kind3[...], own_ref, far_ref, place_ref, count_ref, lists)
    more = [(own_ref, own_hbm), (far_ref, far_hbm), (place_ref, place_hbm), (count_ref, count_hbm)]
    outs += load(out_sems.at[pl.ds(3, 4)], *more)

    pair_ref[...] = jnp.zeros_like(pair_ref)
    pairs = Pairs(atoms_ref, pair_ref, *pair_buffers, 0)
    blocks, strips = STAY // WIDE, WIDE // TALL

    def strip(c, reach):
        at, mine = pl.multiple_of(c * TALL, TALL), c // strips
        pairs.block(at, pl.multiple_of(mine * WIDE, WIDE), False)
        for by in range(1, reach + 1):
            pairs.block(at, pl.multiple_of(lax.rem(mine + by, blocks) * WIDE, WIDE), True)

    def wide_strip(c, _):
        strip(c, 2)
        return 0

    def short_strip(c, _):
        strip(c, 1)
        return 0

    half = blocks * strips // 2
    lax.fori_loop(0, half, wide_strip, 0)
    lax.fori_loop(half, 2 * half, short_strip, 0)
    pairs.close()
    last = pltpu.make_async_copy(pair_ref, pair_hbm, out_sems.at[7])
    last.start()
    for copy in outs:
        copy.wait()
    last.wait()


def merge_kernel(
    me_ref, got_hbm, freq_hbm, phase_hbm, stay_hbm, up_hbm,
    send_ref, low_ref, high_ref, pole_hbm, basis_hbm, atoms_hbm,
    got_ref, freq, phase, stay, up, flat, atoms_ref, basis_ref, pole_ref, ring, turned, ids, first_ref, sems, out_sems,
):
    copies = load(sems, (freq_hbm, freq), (phase_hbm, phase), (stay_hbm, stay), (up_hbm, up), (got_hbm, got_ref))
    copies[4].wait()
    me = me_ref[0]
    row = lax.broadcasted_iota(i32, (DEVICES, LANES), 0)
    lane = lax.broadcasted_iota(i32, (DEVICES, LANES), 1)
    asked = jnp.where(row == lane, got_ref[pl.ds(5, DEVICES, stride=PIECE), :], 0.0)
    ids[...] = jnp.maximum(jnp.sum(asked, axis=0, keepdims=True).astype(i32), 0)
    to_scalars = pltpu.make_async_copy(ids, first_ref, sems.at[5])
    to_scalars.start()
    atoms_ref[...] = jnp.zeros_like(atoms_ref)
    for at, by in enumerate((-2, -1, 1, 2)):
        source = me - by

        @pl.when((source >= 0) & (source < DEVICES))
        def _(at=at, source=source):
            atoms_ref[0:5, at * CAP : (at + 1) * CAP] = got_ref[pl.ds(source * PIECE, 5), :]

    copies[0].wait()
    copies[1].wait()
    atoms = atoms_ref[...]
    basis = basis_of(waves_of(freq, phase, flat), atoms)
    basis_ref[...] = basis
    both = poles(basis, atoms[3:4, :], cell_hot(atoms[4:5, :].astype(i32)))
    copies[2].wait()
    pole = stay[...] + both
    pole_ref[...] = pole
    outs = load(out_sems, (atoms_ref, atoms_hbm), (basis_ref, basis_hbm), (pole_ref, pole_hbm))
    ring[0:CELLS, :] = pole
    ring[CELLS:WRAP, :] = pole[0 : WRAP - CELLS, :]
    grouped = jnp.sum(pole.reshape(CELLS // 8, 8, LANES), axis=0)
    copies[3].wait()
    raised = up[...].reshape(COEF, OPS, COEF) * grouped[None, :, :COEF]
    turned[...] = jnp.zeros_like(turned)
    turned[0:COEF, 0:COEF] = jnp.sum(raised, axis=1)
    coarse = jnp.sum(turned[...].T, axis=0, keepdims=True)
    to_scalars.wait()

    def one(t, _):
        send_ref[pl.ds(t * BLOCK, SHORT), :] = ring[pl.ds(first_ref[0, t], SHORT), :]
        send_ref[pl.ds(t * BLOCK + SHORT, 1), :] = coarse
        return 0

    lax.fori_loop(0, DEVICES, one, 0, unroll=8)
    low_ref[...] = ring[pl.ds(first_ref[0, jnp.maximum(me - 1, 0)] + SHORT, EXTRA), :]
    high_ref[...] = ring[pl.ds(first_ref[0, jnp.minimum(me + 1, DEVICES - 1)] + SHORT, EXTRA), :]
    for copy in outs:
        copy.wait()


def load_ops(ops_ref, both):
    both[...] = jnp.zeros_like(both)
    for o in range(OPS):
        high, low = split(ops_ref[pl.ds(o, COEF, stride=OPS), :])
        for at, part in enumerate((high, high, low)):
            both[o * LANES : o * LANES + COEF, at * LANES : at * LANES + COEF] = part


def premultiply(rows, both, table, at, pitch):
    high, low = split(rows)
    parts = jnp.concatenate([high, low, high], axis=1)
    for o in range(0, OPS, 2):
        pair = both[o * LANES : (o + 2) * LANES, :]
        out = lax.dot_general(parts, pair, NT, preferred_element_type=f32)
        for k in range(2):
            table[pl.ds((o + k) * pitch + at, rows.shape[0]), :] = out[:, k * LANES : (k + 1) * LANES]


def index_of(index_ref, l, r, g):
    return index_ref.at[pl.ds(l * CELLS + r * LANES, LANES)][g]


def row_sums(index_ref, used, g, table, start):
    def steps(count):
        totals = []
        for r in range(8):
            total = None if start is None else start(r)
            for l in range(count):
                row = table[pl.ds(index_of(index_ref, l, r, g), 1), :]
                total = row if total is None else total + row
            totals.append(total)
        return tuple(totals)

    def tree(low, high):
        if low == high:
            return steps(2 * low)
        middle = (low + high) // 2
        return lax.cond(used <= 2 * middle, lambda: tree(low, middle), lambda: tree(middle + 1, high))

    return tree(1, LIST // 2)


def mid_kernel(
    own_ref, count_ref, stay_hbm, new_hbm, pole_hbm, ops_hbm, stay_pair_hbm, sum_hbm, pair_hbm,
    table, both, ops, pole, atoms_ref, sum_ref, pair_ref, *rest,
):
    *pair_buffers, sems, out_sems = rest
    copies = load(
        sems, (ops_hbm, ops), (pole_hbm, pole), (stay_hbm, atoms_ref.at[:, pl.ds(0, STAY)]),
        (new_hbm, atoms_ref.at[:, pl.ds(STAY, ARRIVE)]), (stay_pair_hbm, pair_ref.at[:, pl.ds(0, STAY)]),
    )
    pair_ref[:, STAY:] = jnp.zeros((1, ARRIVE), f32)
    copies[0].wait()
    load_ops(ops, both)
    table[OPS * CELLS :, :] = jnp.zeros((8, LANES), f32)
    copies[1].wait()
    width = CELLS // 2
    for lo in range(0, CELLS, width):
        premultiply(pole[lo : lo + width, :], both, table, lo, CELLS)

    def gather(g, _):
        totals = row_sums(own_ref, count_ref.at[pl.ds(LANES, LANES)][g], g, table, None)
        for r in range(8):
            sum_ref[pl.ds(r * LANES + g, 1), :] = totals[r]
        return 0

    lax.fori_loop(0, LANES, gather, 0)
    sums_out = pltpu.make_async_copy(sum_ref, sum_hbm, out_sems.at[0])
    sums_out.start()
    for copy in copies[2:]:
        copy.wait()
    pairs = Pairs(atoms_ref, pair_ref, *pair_buffers, STAY)

    def strip(c, _):
        at = pl.multiple_of(c * TALL, TALL)
        pairs.block(at, STAY, False)
        for lo in range(0, STAY, WIDE):
            pairs.block(at, lo, True)
        return 0

    lax.fori_loop(0, ARRIVE // TALL, strip, 0)
    pairs.close()
    pairs_out = pltpu.make_async_copy(pair_ref, pair_hbm, out_sems.at[1])
    pairs_out.start()
    sums_out.wait()
    pairs_out.wait()


def last_kernel(
    me_ref, index_ref, count_ref, place_ref, far_hbm, below_hbm, above_hbm, ops_hbm, sum_hbm, inner_hbm, outer_hbm,
    down_hbm, stay_hbm, new_hbm, stay_basis_hbm, new_basis_hbm, pair_hbm, local_ref, pot_ref,
    table, both, sums_ref, rows, coarse, ops, inner, outer, down, atoms_ref, basis_ref, pair, far_ref, below_ref, above_ref,
    sems,
):
    copies = load(
        sems, (ops_hbm, ops), (sum_hbm, sums_ref), (inner_hbm, inner), (outer_hbm, outer), (down_hbm, down),
        (stay_hbm, atoms_ref.at[:, pl.ds(0, STAY)]), (new_hbm, atoms_ref.at[:, pl.ds(STAY, ARRIVE)]),
        (stay_basis_hbm, basis_ref.at[:, pl.ds(0, STAY)]), (new_basis_hbm, basis_ref.at[:, pl.ds(STAY, ARRIVE)]),
        (pair_hbm, pair), (far_hbm, far_ref), (below_hbm, below_ref), (above_hbm, above_ref),
    )
    copies[0].wait()
    load_ops(ops, both)
    for copy in copies[10:]:
        copy.wait()
    width = FAR_ROWS // 4
    for lo in range(0, FAR_ROWS, width):
        premultiply(far_ref[lo : lo + width, :], both, table, lo, REMOTE)
    premultiply(below_ref[...], both, table, FAR_ROWS, REMOTE)
    premultiply(above_ref[...], both, table, FAR_ROWS + EXTRA, REMOTE)
    table[OPS * REMOTE :, :] = jnp.zeros((8, LANES), f32)

    coarse[...] = far_ref[pl.ds(SHORT, DEVICES, stride=BLOCK), :]
    me = me_ref[0]
    group, member = me // MEMBERS, lax.rem(me, MEMBERS)
    who = lax.broadcasted_iota(i32, (40, DEVICES), 1)
    which = lax.broadcasted_iota(i32, (40, DEVICES), 0)
    its_group, its_member = who // MEMBERS, lax.rem(who, MEMBERS)
    near = (its_group == group) & (jnp.abs(its_member - member) - 1 == which) & (which < MEMBERS)
    away = (jnp.abs(its_group - group) - 1 == which - MEMBERS) & (which >= MEMBERS)
    chosen = jnp.where(near | away, 1.0, 0.0)
    sums = lax.dot_general(chosen, coarse[...], NN, precision=lax.Precision.HIGHEST, preferred_element_type=f32)
    for copy in copies[1:5]:
        copy.wait()
    field = jnp.sum(inner[...] * sums[None, 0 : MEMBERS - 1, 0:COEF], axis=1)
    for o in range(GROUPS - 1):
        field = field + outer[o] * sums[MEMBERS + o : MEMBERS + o + 1, 0:COEF]
    field = jnp.broadcast_to(jnp.sum(field, axis=1, keepdims=True), (COEF, LANES))
    child = lax.rem(lax.broadcasted_iota(i32, (COEF, LANES), 1), OPS)
    pattern = jnp.zeros((COEF, LANES), f32)
    for o in range(OPS):
        one = lax.dot_general(
            down[pl.ds(o, COEF, stride=OPS), :], field, NN,
            precision=lax.Precision.HIGHEST, preferred_element_type=f32,
        )
        pattern = jnp.where(child == o, one, pattern)

    def gather(g, _):
        totals = row_sums(
            index_ref, count_ref.at[pl.ds(0, LANES)][g], g, table, lambda r: sums_ref[pl.ds(r * LANES + g, 1), :]
        )
        for r in range(8):
            rows[pl.ds(place_ref.at[pl.ds(r * LANES, LANES)][g], 1), :] = totals[r]
        return 0

    lax.fori_loop(0, LANES, gather, 0)

    for lo in range(0, CELLS, LANES):
        local_ref[:, lo : lo + LANES] = rows[lo : lo + LANES, :].T[0:COEF, :] + pattern
    local = local_ref[...]
    high, rest = split(local)
    high = jnp.concatenate([high, jnp.zeros((LANES - COEF, CELLS), bf16)], axis=0)
    rest = jnp.concatenate([rest, jnp.zeros((LANES - COEF, CELLS), bf16)], axis=0)
    stacked = jnp.concatenate([high, rest], axis=0)
    for copy in copies[5:10]:
        copy.wait()
    wide = 512
    for lo in range(0, SLOTS, wide):
        cells, basis = atoms_ref[4:5, lo : lo + wide], basis_ref[:, lo : lo + wide]
        at = lax.dot_general(stacked, cell_hot(cells.astype(i32)), NN, preferred_element_type=f32)
        read = jnp.sum((at[:LANES] + at[LANES:]) * basis, axis=0, keepdims=True)
        read = read * COEF**-0.5 + pair[:, lo : lo + wide]
        for at in range(0, wide, LANES):
            i = (lo + at) // LANES
            pot_ref[i : i + 1, :] = read[:, at : at + LANES]


VM = pl.BlockSpec(memory_space=pltpu.VMEM)
SM = pl.BlockSpec(memory_space=pltpu.SMEM)
HB = pl.BlockSpec(memory_space=pltpu.HBM)


def call(kernel, name, ins, outs, scratch, copies, flops, *operands):
    cost = pl.CostEstimate(flops=flops, bytes_accessed=4 * MIB, transcendentals=0)
    return pl.pallas_call(
        kernel,
        name=name,
        in_specs=ins,
        out_specs=[spec for spec, _, _ in outs],
        out_shape=[jax.ShapeDtypeStruct(shape, kind) for _, shape, kind in outs],
        scratch_shapes=[pltpu.VMEM(shape, kind) if isinstance(shape, tuple) else shape for shape, kind in scratch]
        + [pltpu.SemaphoreType.DMA((count,)) for count in copies],
        cost_estimate=cost,
        compiler_params=pltpu.CompilerParams(vmem_limit_bytes=60 * MIB),
    )(*operands)


def on_device(
    atom_rows,
    atom_owner,
    atom_cell,
    need_cells,
    list_entry,
    list_class,
    basis_freq,
    basis_phase,
    near_ops,
    up_ops,
    far_in,
    far_out,
    down_ops,
):
    me = (lax.axis_index("group") * MEMBERS + lax.axis_index("dev")).reshape(1).astype(i32)
    freq, phase = basis_freq.T, basis_phase.reshape(1, COEF)
    waves = [((3, COEF), f32), ((1, COEF), f32)]
    owner_row, cell_row = atom_owner.reshape(1, STAY), atom_cell.reshape(1, STAY)
    by_row = [ops.transpose(1, 0, 2).reshape(COEF * OPS, COEF) for ops in (near_ops, up_ops, down_ops)]
    ops_shape = ((COEF * OPS, COEF), f32)
    mine = [((1, STAY), i32), ((4, STAY), f32), ((1, STAY), i32)]

    (outbound,) = call(
        pack_kernel, "pack", [SM, HB, HB, HB, HB], [(VM, (DEVICES * PIECE, LANES), f32)],
        [((8, LANES), i32), ((STAY // LANES, LANES), i32), *mine[1:], ((8, 512), f32)], [4], 10**6,
        me, need_cells.transpose(0, 2, 1), atom_owner.reshape(STAY // LANES, LANES), atom_rows, cell_row,
    )
    got = lax.all_to_all(outbound.reshape(DEVICES, 1, PIECE * LANES), AXES, split_axis=0, concat_axis=0, tiled=True)
    got = got.reshape(DEVICES * PIECE, LANES)

    shape3, tile = (LIST, CELLS // LANES, LANES), (CELLS // LANES, LANES)
    early_outs = [
        ((8, STAY), f32), ((LANES, STAY), f32), ((CELLS, LANES), f32), ((1, STAY), f32),
        (shape3, i32), (shape3, i32), (tile, i32), (tile, i32),
    ]
    stay_atoms, stay_basis, stay_pole, stay_pair, own_index, far_index, place, counts = call(
        early_kernel, "early", [SM] + [HB] * 7, [(HB, *out) for out in early_outs],
        [*mine, *waves, *[((LIST, CELLS), i32)] * 2, *[(shape3, i32)] * 2, ((80, CELLS), f32), ((8, LANES), f32), *early_outs,
         *pair_scratch(STAY, STAY)], [7, 8], 12 * 10**9,
        me, owner_row, atom_rows, cell_row, freq, phase, list_entry, list_class,
    )
    own_index, far_index, place, counts = (one.reshape(-1) for one in (own_index, far_index, place, counts))
    merge_outs = [((CELLS, LANES), f32), ((LANES, ARRIVE), f32), ((8, ARRIVE), f32)]
    send, low, high, pole, new_basis, new_atoms = call(
        merge_kernel, "merge", [SM] + [HB] * 5,
        [(VM, (FAR_ROWS, LANES), f32), (VM, (EXTRA, LANES), f32), (VM, (EXTRA, LANES), f32), *[(HB, *out) for out in merge_outs]],
        [((DEVICES * PIECE, LANES), f32), *waves, ((CELLS, LANES), f32), ops_shape, ((8, LANES), f32), *merge_outs[::-1],
         ((WRAP, LANES), f32), ((LANES, LANES), f32), ((1, LANES), i32), (pltpu.SMEM((1, LANES), i32), None)],
        [6, 3], 2 * 10**9,
        me, got, freq, phase, stay_pole, by_row[1],
    )
    below, above = shift(high, 1), shift(low, -1)
    far_rows = lax.all_to_all(send.reshape(DEVICES, 1, BLOCK * LANES), AXES, split_axis=0, concat_axis=0, tiled=True)
    far_rows = far_rows.reshape(FAR_ROWS, LANES)
    mid_outs = [((CELLS, LANES), f32), ((1, SLOTS), f32)]
    own_sum, pair = call(
        mid_kernel, "mid", [SM, SM] + [HB] * 5, [(HB, *out) for out in mid_outs],
        [((OPS * CELLS + 8, LANES), f32), ((OPS * LANES, 3 * LANES), bf16), ops_shape, ((CELLS, LANES), f32), ((8, SLOTS), f32),
         *mid_outs, *pair_scratch(SLOTS, ARRIVE)],
        [5, 2], 20 * 10**9,
        own_index, counts, stay_atoms, new_atoms, pole, by_row[0], stay_pair,
    )
    local, pot = call(
        last_kernel, "last", [SM] * 4 + [HB] * 13, [(VM, (COEF, CELLS), f32), (VM, (SLOTS // LANES, LANES), f32)],
        [((OPS * REMOTE + 8, LANES), f32), ((OPS * LANES, 3 * LANES), bf16), *[((CELLS, LANES), f32)] * 2, ((DEVICES, LANES), f32),
         ops_shape, ((COEF, MEMBERS - 1, COEF), f32), ((GROUPS - 1, COEF, COEF), f32), ops_shape, ((8, SLOTS), f32),
         ((LANES, SLOTS), f32), ((1, SLOTS), f32), ((FAR_ROWS, LANES), f32), *[((EXTRA, LANES), f32)] * 2],
        [13], 8 * 10**9,
        me, far_index, counts, place, far_rows, below, above, by_row[0], own_sum,
        far_in.transpose(1, 0, 2), far_out, by_row[2], stay_atoms, new_atoms, stay_basis, new_basis, pair,
    )
    return local, pot.reshape(SLOTS)


def solution(mesh):
    in_specs = (
        P(None, AXES),
        P(AXES),
        P(AXES),
        P(AXES, None, None),
        P(None, AXES),
        P(None, AXES),
        P(),
        P(),
        P(),
        P(),
        P(),
        P(),
        P(),
    )
    out_specs = (P(None, AXES), P(AXES))
    return jax.shard_map(on_device, mesh=mesh, in_specs=in_specs, out_specs=out_specs, check_vma=False)
```

```python
import math

import jax
import jax.numpy as jnp
from jax import lax
from jax.experimental import pallas as pl
from jax.experimental.pallas import tpu as pltpu
from jax.sharding import PartitionSpec as P

COEF = 121
LANES = 128
CELLS = 1024
STAY = 2048
CAP = 128
ARRIVE = 4 * CAP
SLOTS = STAY + ARRIVE
LIST = 16
OPS = 8
SLOT = 72
SHORT = 18
BLOCK = SHORT + 1
DEVICES = 128
MEMBERS = 32
GROUPS = 4
PIECE = 6
EXTRA = 56
FAR_ROWS = DEVICES * BLOCK
REMOTE = FAR_ROWS + 2 * EXTRA
WRAP = CELLS + 80
TALL, WIDE = 256, 512
AXES = ("group", "dev")
MIB = 2**20
f32, bf16, i32 = jnp.float32, jnp.bfloat16, jnp.int32
SIN = [(-1) ** n * (2 * math.pi) ** (2 * n + 1) / math.factorial(2 * n + 1) for n in range(6)]

NT = (((1,), (1,)), ((), ()))
NN = (((1,), (0,)), ((), ()))


def shift(value, by):
    pairs = [(i, i + by) for i in range(DEVICES) if 0 <= i + by < DEVICES]
    return lax.ppermute(value, AXES, pairs)


def split(value):
    high = value.astype(bf16)
    return high, (value - high.astype(f32)).astype(bf16)


def basis_of(waves, atoms):
    turns = waves[:, 3:4] + waves[:, 0:1] * atoms[0:1, :]
    turns = turns + waves[:, 1:2] * atoms[1:2, :]
    turns = turns + waves[:, 2:3] * atoms[2:3, :]
    turns = turns - jnp.floor(turns + 0.5)
    base = 0.25 - jnp.abs(turns)
    square = base * base
    total = jnp.full_like(square, SIN[5])
    for factor in SIN[4::-1]:
        total = total * square + factor
    return base * total


def cell_hot(cell_row):
    ids = lax.broadcasted_iota(i32, (CELLS, cell_row.shape[1]), 0) + 1
    return jnp.where(ids == cell_row, 1.0, 0.0).astype(bf16)


def poles(basis, charge, hot):
    high, low = split(basis * charge)
    both = lax.dot_general(hot, jnp.concatenate([high, low], axis=0), NT, preferred_element_type=f32)
    return both[:, :LANES] + both[:, LANES:]


def load(sems, *pairs):
    copies = [pltpu.make_async_copy(src, dst, sems.at[i]) for i, (src, dst) in enumerate(pairs)]
    for copy in copies:
        copy.start()
    return copies


def waves_of(freq_ref, phase_ref, flat):
    flat[...] = jnp.zeros_like(flat)
    flat[0:3, 0:COEF] = freq_ref[...] * (0.5 / math.pi)
    flat[3:4, 0:COEF] = phase_ref[...] * (0.5 / math.pi)
    return flat[...].T


def pack_kernel(me_ref, need_hbm, owner_hbm, rows_hbm, cell_hbm, out_ref, need, owner, rows, cell, buf, sems):
    copies = load(
        sems, (owner_hbm, owner), (rows_hbm, rows), (cell_hbm, cell), (need_hbm.at[0, pl.ds(0, 8), :], need)
    )
    out_ref[...] = jnp.zeros_like(out_ref)
    buf[...] = jnp.zeros_like(buf)
    for copy in copies:
        copy.wait()
    me = me_ref[0]
    gap = owner[...] - me

    def count(by):
        return jnp.sum(jnp.where(gap == by, 1.0, 0.0)).astype(i32)

    for at, lo in ((0, 0), (256, STAY - 256)):
        buf[0:4, at : at + 256] = rows[:, lo : lo + 256]
        buf[4:5, at : at + 256] = (cell[:, lo : lo + 256] + 1).astype(f32)
    lane = lax.broadcasted_iota(i32, (8, CAP), 1)
    low2, low1, up1, up2 = count(-2), count(-1), count(1), count(2)
    first = jnp.broadcast_to(need[0:1, :].astype(f32), (LANES, LANES)).T
    out_ref[pl.ds(5, DEVICES, stride=PIECE), :] = first
    ahead = pltpu.roll(buf[:, :256], lax.rem(256 - low2, 256), 1)
    behind = pltpu.roll(buf[:, 256:], lax.rem(up1 + up2, 256), 1)
    last = pltpu.roll(buf[:, 256:], lax.rem(up2, 256), 1)
    for by, count_by, piece in (
        (-2, low2, buf[:, :CAP]), (-1, low1, ahead[:, :CAP]), (1, up1, behind[:, :CAP]), (2, up2, last[:, :CAP])
    ):
        to = me + by

        @pl.when((to >= 0) & (to < DEVICES))
        def _(to=to, count_by=count_by, piece=piece):
            out_ref[pl.ds(to * PIECE, 5), :] = jnp.where(lane < count_by, piece, 0.0)[0:5, :]


def features(atoms_ref, left, right):
    def parts(value, count):
        out = []
        for _ in range(count):
            out.append(value.astype(bf16).astype(f32))
            value = value - out[-1]
        return out

    left[...] = jnp.zeros_like(left)
    right[...] = jnp.zeros_like(right)
    square = None
    for d in range(3):
        value = atoms_ref[d : d + 1, :]
        square = value * value if square is None else square + value * value
        for i, (a, b) in enumerate((a, b) for a in parts(value, 2) for b in parts(value, 2)):
            left[4 * d + i : 4 * d + i + 1, :] = a
            right[4 * d + i : 4 * d + i + 1, :] = -2.0 * b
    ones = jnp.ones_like(square)
    for i, part in enumerate(parts(square, 3)):
        left[12 + i : 13 + i, :] = part
        right[12 + i : 13 + i, :] = ones
    for i, part in enumerate(parts(square + 0.25, 3)):
        left[15 + i : 16 + i, :] = ones
        right[15 + i : 16 + i, :] = part


class Pairs:
    def __init__(self, atoms_ref, pair_ref, left, right, left_cols, right_low, charges, cells, back, start):
        self.atoms, self.pair, self.left_cols, self.right_low = atoms_ref, pair_ref, left_cols, right_low
        self.charges, self.cells, self.back, self.start = charges, cells, back, start
        features(atoms_ref, left, right)
        right_low[...] = right[...].astype(bf16)
        for at in range(0, left_cols.shape[0], LANES):
            cut, rows = slice(start + at, start + at + LANES), slice(at, at + LANES)
            left_cols[rows, :] = left[:, cut].T.astype(bf16)
            charges[rows, :] = jnp.broadcast_to(atoms_ref[3:4, cut], (LANES, LANES)).T
            cells[rows, :] = jnp.broadcast_to(atoms_ref[4:5, cut], (LANES, LANES)).T
        back[...] = jnp.zeros_like(back)

    def block(self, at, lo, both):
        far = lax.dot_general(
            self.left_cols[pl.ds(at, TALL), :], self.right_low[:, pl.ds(lo, WIDE)], NN, preferred_element_type=f32
        )
        its_cell = jnp.concatenate([self.cells[pl.ds(at, TALL), :]] * (WIDE // LANES), axis=1)
        its_charge = jnp.concatenate([self.charges[pl.ds(at, TALL), :]] * (WIDE // LANES), axis=1)
        near = jnp.where(its_cell == self.atoms[4:5, pl.ds(lo, WIDE)], lax.rsqrt(far), 0.0)
        total = jnp.sum((near * its_charge).reshape(TALL // 8, 8, WIDE), axis=0)
        self.pair[:, pl.ds(lo, WIDE)] += jnp.sum(total, axis=0, keepdims=True)
        if both:
            near = near * self.atoms[3:4, pl.ds(lo, WIDE)]
            total = near[:, 0:LANES]
            for k in range(1, WIDE // LANES):
                total = total + near[:, k * LANES : (k + 1) * LANES]
            self.back[pl.ds(at, TALL), :] += total

    def close(self):
        for at in range(0, self.back.shape[0], LANES):
            cut = slice(self.start + at, self.start + at + LANES)
            itself = self.atoms[3:4, cut] * lax.rsqrt(jnp.full((1, LANES), 0.25, f32))
            self.pair[:, cut] += jnp.sum(self.back[at : at + LANES, :].T, axis=0, keepdims=True) - itself


def pair_scratch(slots, rows):
    return [
        ((32, slots), f32), ((32, slots), f32), ((rows, 32), bf16), ((32, slots), bf16),
        *[((rows, LANES), f32)] * 3,
    ]


def sort_rows(keys):
    keys = list(keys)
    step = 1
    while step < LIST:
        gap = step
        while gap >= 1:
            for base in range(gap % step, LIST - gap, 2 * gap):
                for i in range(min(gap, LIST - base - gap)):
                    a, b = base + i, base + i + gap
                    if a // (2 * step) == b // (2 * step):
                        keys[a], keys[b] = jnp.maximum(keys[a], keys[b]), jnp.minimum(keys[a], keys[b])
            gap //= 2
        step *= 2
    return keys


def order(me, entry, kind, own_ref, far_ref, cell_ref, count_ref, lists):
    asked = jnp.maximum(entry - CELLS, 0)
    source = jnp.floor((asked.astype(f32) + 0.5) * (1.0 / SLOT)).astype(i32)
    slot = asked - source * SLOT
    side = jnp.where(source < me, FAR_ROWS, FAR_ROWS + EXTRA)
    row = jnp.where(slot < SHORT, source * BLOCK + slot, side + slot - SHORT)
    key = jnp.where(entry < CELLS, -1, kind * REMOTE + row)
    used = jnp.sum(jnp.where(key >= 0, 1, 0), axis=0)
    far = sort_rows(key[l] for l in range(LIST))
    key = jnp.where(entry < CELLS, kind * CELLS + entry, -1)
    own = sort_rows(key[l] for l in range(LIST))
    own = [jnp.where(one < 0, OPS * CELLS, one) for one in own]
    far = [jnp.where(one < 0, OPS * REMOTE, one) for one in far]

    def flat(value):
        return jnp.concatenate([value[r : r + 1, :] for r in range(CELLS // LANES)], axis=1)

    used_row = flat(used).astype(f32)
    rank_key = used_row * CELLS + lax.broadcasted_iota(i32, (1, CELLS), 1).astype(f32)
    rank = jnp.zeros((8, CELLS), f32)
    for lo in range(0, CELLS, LANES):
        column = jnp.broadcast_to(rank_key[:, lo : lo + LANES], (LANES, LANES)).T
        ahead = jnp.where(jnp.concatenate([column] * (CELLS // LANES), axis=1) > rank_key, 1.0, 0.0)
        rank = rank + jnp.sum(ahead.reshape(LANES // 8, 8, CELLS), axis=0)
    rank = jnp.sum(rank, axis=0, keepdims=True).astype(i32)
    place = (rank & 7) * LANES + (rank >> 3)
    moved = jnp.where(lax.broadcasted_iota(i32, (CELLS, CELLS), 0) == place, 1.0, 0.0).astype(bf16)
    lists[...] = jnp.zeros_like(lists)
    for l in range(LIST):
        for at, value in ((l, far[l] >> 8), (16 + l, far[l] & 255), (32 + l, own[l] >> 8), (48 + l, own[l] & 255)):
            for r in range(CELLS // LANES):
                lists[at : at + 1, r * LANES : (r + 1) * LANES] = value[r : r + 1, :].astype(f32)
    ids = lax.broadcasted_iota(i32, (1, CELLS), 1)
    lists[64:65, :] = (ids >> 8).astype(f32)
    lists[65:66, :] = (ids & 255).astype(f32)
    lists[66:67, :] = used_row
    sorted_lists = lax.dot_general(lists[...].astype(bf16), moved, NT, preferred_element_type=f32).astype(i32)
    far_rows = sorted_lists[0:16] * 256 + sorted_lists[16:32]
    own_rows = sorted_lists[32:48] * 256 + sorted_lists[48:64]
    cells = sorted_lists[64:65] * 256 + sorted_lists[65:66]
    for r in range(CELLS // LANES):
        cut = slice(r * LANES, (r + 1) * LANES)
        for l in range(LIST):
            far_ref[l, r : r + 1, :] = far_rows[l : l + 1, cut]
            own_ref[l, r : r + 1, :] = own_rows[l : l + 1, cut]
        cell_ref[r : r + 1, :] = cells[:, cut]
    group = lax.broadcasted_iota(i32, (LANES, LANES), 0)
    number = lax.broadcasted_iota(i32, (LANES, LANES), 1)
    most = jnp.broadcast_to(sorted_lists[66:67, 0:LANES].astype(f32), (LANES, LANES)).T.astype(i32)
    least = jnp.broadcast_to(sorted_lists[66:67, CELLS - LANES : CELLS].astype(f32), (LANES, LANES)).T.astype(i32)
    count_ref[...] = jnp.zeros_like(count_ref)
    remote = jnp.where((most >= number) & ((group & 1) == 0), 1.0, 0.0)
    local = jnp.where((LIST - least <= number) & ((group & 1) == 1), 1.0, 0.0)
    count_ref[0:1, :] = jnp.sum(remote, axis=0, keepdims=True).astype(i32)
    count_ref[1:2, :] = jnp.sum(local, axis=0, keepdims=True).astype(i32)


def early_kernel(
    me_ref, owner_hbm, rows_hbm, cell_hbm, freq_hbm, phase_hbm, entry_hbm, class_hbm,
    atoms_hbm, basis_hbm, pole_hbm, pair_hbm, own_hbm, far_hbm, place_hbm, count_hbm,
    owner, rows, cell, freq, phase, entry, kind, entry3, kind3, lists, flat,
    atoms_ref, basis_ref, pole_ref, pair_ref, own_ref, far_ref, place_ref, count_ref, *rest,
):
    *pair_buffers, sems, out_sems = rest
    copies = load(
        sems, (owner_hbm, owner), (rows_hbm, rows), (cell_hbm, cell), (freq_hbm, freq), (phase_hbm, phase),
        (entry_hbm, entry), (class_hbm, kind),
    )
    atoms_ref[...] = jnp.zeros_like(atoms_ref)
    for copy in copies[:5]:
        copy.wait()
    stays = owner[...] == me_ref[0]
    atoms_ref[0:4, :] = jnp.where(stays, rows[...], 0.0)
    atoms_ref[4:5, :] = jnp.where(stays, (cell[...] + 1).astype(f32), 0.0)
    waves = waves_of(freq, phase, flat)
    width = 512
    for lo in range(0, STAY, width):
        atoms = atoms_ref[:, lo : lo + width]
        basis = basis_of(waves, atoms)
        basis_ref[:, lo : lo + width] = basis
        part = poles(basis, atoms[3:4, :], cell_hot(atoms[4:5, :].astype(i32)))
        pole_ref[...] = part if lo == 0 else pole_ref[...] + part
    outs = load(out_sems, (atoms_ref, atoms_hbm), (basis_ref, basis_hbm), (pole_ref, pole_hbm))
    for copy in copies[5:]:
        copy.wait()
    for l in range(LIST):
        for r in range(CELLS // LANES):
            entry3[l, r : r + 1, :] = entry[l : l + 1, r * LANES : (r + 1) * LANES]
            kind3[l, r : r + 1, :] = kind[l : l + 1, r * LANES : (r + 1) * LANES]
    order(me_ref[0], entry3[...], kind3[...], own_ref, far_ref, place_ref, count_ref, lists)
    more = [(own_ref, own_hbm), (far_ref, far_hbm), (place_ref, place_hbm), (count_ref, count_hbm)]
    outs += load(out_sems.at[pl.ds(3, 4)], *more)

    pair_ref[...] = jnp.zeros_like(pair_ref)
    pairs = Pairs(atoms_ref, pair_ref, *pair_buffers, 0)
    blocks, strips = STAY // WIDE, WIDE // TALL

    def strip(c, reach):
        at, mine = pl.multiple_of(c * TALL, TALL), c // strips
        pairs.block(at, pl.multiple_of(mine * WIDE, WIDE), False)
        for by in range(1, reach + 1):
            pairs.block(at, pl.multiple_of(lax.rem(mine + by, blocks) * WIDE, WIDE), True)

    def wide_strip(c, _):
        strip(c, 2)
        return 0

    def short_strip(c, _):
        strip(c, 1)
        return 0

    half = blocks * strips // 2
    lax.fori_loop(0, half, wide_strip, 0)
    lax.fori_loop(half, 2 * half, short_strip, 0)
    pairs.close()
    last = pltpu.make_async_copy(pair_ref, pair_hbm, out_sems.at[7])
    last.start()
    for copy in outs:
        copy.wait()
    last.wait()


def merge_kernel(
    me_ref, got_ref, freq_hbm, phase_hbm, stay_hbm, up_hbm,
    send_ref, low_ref, high_ref, pole_hbm, basis_hbm, atoms_hbm,
    freq, phase, stay, up, flat, atoms_ref, basis_ref, pole_ref, ring, turned, ids, first_ref, sems, out_sems,
):
    copies = load(sems, (freq_hbm, freq), (phase_hbm, phase), (stay_hbm, stay), (up_hbm, up))
    me = me_ref[0]
    row = lax.broadcasted_iota(i32, (DEVICES, LANES), 0)
    lane = lax.broadcasted_iota(i32, (DEVICES, LANES), 1)
    asked = jnp.where(row == lane, got_ref[pl.ds(5, DEVICES, stride=PIECE), :], 0.0)
    ids[...] = jnp.maximum(jnp.sum(asked, axis=0, keepdims=True).astype(i32), 0)
    to_scalars = pltpu.make_async_copy(ids, first_ref, sems.at[4])
    to_scalars.start()
    atoms_ref[...] = jnp.zeros_like(atoms_ref)
    for at, by in enumerate((-2, -1, 1, 2)):
        source = me - by

        @pl.when((source >= 0) & (source < DEVICES))
        def _(at=at, source=source):
            atoms_ref[0:5, at * CAP : (at + 1) * CAP] = got_ref[pl.ds(source * PIECE, 5), :]

    copies[0].wait()
    copies[1].wait()
    atoms = atoms_ref[...]
    basis = basis_of(waves_of(freq, phase, flat), atoms)
    basis_ref[...] = basis
    both = poles(basis, atoms[3:4, :], cell_hot(atoms[4:5, :].astype(i32)))
    copies[2].wait()
    pole = stay[...] + both
    pole_ref[...] = pole
    outs = load(out_sems, (atoms_ref, atoms_hbm), (basis_ref, basis_hbm), (pole_ref, pole_hbm))
    ring[0:CELLS, :] = pole
    ring[CELLS:WRAP, :] = pole[0 : WRAP - CELLS, :]
    grouped = jnp.sum(pole.reshape(CELLS // 8, 8, LANES), axis=0)
    copies[3].wait()
    raised = up[...].reshape(COEF, OPS, COEF) * grouped[None, :, :COEF]
    turned[...] = jnp.zeros_like(turned)
    turned[0:COEF, 0:COEF] = jnp.sum(raised, axis=1)
    coarse = jnp.sum(turned[...].T, axis=0, keepdims=True)
    to_scalars.wait()

    def one(t, _):
        send_ref[pl.ds(t * BLOCK, SHORT), :] = ring[pl.ds(first_ref[0, t], SHORT), :]
        send_ref[pl.ds(t * BLOCK + SHORT, 1), :] = coarse
        return 0

    lax.fori_loop(0, DEVICES, one, 0, unroll=8)
    low_ref[...] = ring[pl.ds(first_ref[0, jnp.maximum(me - 1, 0)] + SHORT, EXTRA), :]
    high_ref[...] = ring[pl.ds(first_ref[0, jnp.minimum(me + 1, DEVICES - 1)] + SHORT, EXTRA), :]
    for copy in outs:
        copy.wait()


def load_ops(ops_ref, both):
    both[...] = jnp.zeros_like(both)
    for o in range(OPS):
        high, low = split(ops_ref[pl.ds(o, COEF, stride=OPS), :])
        for at, part in enumerate((high, high, low)):
            both[o * LANES : o * LANES + COEF, at * LANES : at * LANES + COEF] = part


def premultiply(rows, both, table, at, pitch):
    high, low = split(rows)
    parts = jnp.concatenate([high, low, high], axis=1)
    for o in range(0, OPS, 2):
        pair = both[o * LANES : (o + 2) * LANES, :]
        out = lax.dot_general(parts, pair, NT, preferred_element_type=f32)
        for k in range(2):
            table[pl.ds((o + k) * pitch + at, rows.shape[0]), :] = out[:, k * LANES : (k + 1) * LANES]


def index_of(index_ref, l, r, g):
    return index_ref.at[pl.ds(l * CELLS + r * LANES, LANES)][g]


def row_sums(index_ref, table, count, first, last, start, store):
    def pair(p, _):
        for g in (2 * p, 2 * p + 1):
            for r in range(8):
                total = None if start is None else start(r, g)
                for l in range(count):
                    row = table[pl.ds(index_of(index_ref, l, r, g), 1), :]
                    total = row if total is None else total + row
                store(r, g, jnp.zeros((1, LANES), f32) if total is None else total)
        return 0

    lax.fori_loop(first, last, pair, 0)


def cross_kernel(
    low_hbm, high_hbm, stay_hbm, new_hbm, stay_pair_hbm, low_out, high_out, pair_hbm, low, high, atoms_ref, pair_ref, *rest
):
    *pair_buffers, sems, out_sems = rest
    copies = load(
        sems, (stay_hbm, atoms_ref.at[:, pl.ds(0, STAY)]), (new_hbm, atoms_ref.at[:, pl.ds(STAY, ARRIVE)]),
        (low_hbm, low), (high_hbm, high), (stay_pair_hbm, pair_ref.at[:, pl.ds(0, STAY)]),
    )
    pair_ref[:, STAY:] = jnp.zeros((1, ARRIVE), f32)
    for copy in copies:
        copy.wait()
    outs = load(out_sems, (low, low_out), (high, high_out))
    pairs = Pairs(atoms_ref, pair_ref, *pair_buffers, STAY)

    def strip(c, _):
        at = pl.multiple_of(c * TALL, TALL)
        pairs.block(at, STAY, False)
        for lo in range(0, STAY, WIDE):
            pairs.block(at, lo, True)
        return 0

    lax.fori_loop(0, ARRIVE // TALL, strip, 0)
    pairs.close()
    last = pltpu.make_async_copy(pair_ref, pair_hbm, out_sems.at[2])
    last.start()
    for copy in outs + [last]:
        copy.wait()


def mid_kernel(own_ref, count_ref, pole_hbm, ops_hbm, sum_hbm, table, both, ops, pole, sum_ref, sems):
    copies = load(sems, (ops_hbm, ops), (pole_hbm, pole))
    table[OPS * CELLS :, :] = jnp.zeros((8, LANES), f32)
    copies[0].wait()
    load_ops(ops, both)
    copies[1].wait()
    width = CELLS // 2
    for lo in range(0, CELLS, width):
        premultiply(pole[lo : lo + width, :], both, table, lo, CELLS)

    def store(r, g, total):
        sum_ref[pl.ds(r * LANES + g, 1), :] = total

    for n in range(LIST + 1):
        first = 0 if n == 0 else count_ref[LANES + n - 1]
        row_sums(own_ref, table, n, first, count_ref[LANES + n], None, store)
    out = pltpu.make_async_copy(sum_ref, sum_hbm, sems.at[2])
    out.start()
    out.wait()


def last_kernel(
    me_ref, index_ref, count_ref, place_ref, far_ref, below_ref, above_ref, ops_hbm, sum_hbm, inner_hbm, outer_hbm,
    down_hbm, stay_hbm, new_hbm, stay_basis_hbm, new_basis_hbm, pair_hbm, local_ref, pot_ref,
    table, both, sums_ref, rows, coarse, ops, inner, outer, down, atoms_ref, basis_ref, pair, sems,
):
    copies = load(
        sems, (ops_hbm, ops), (sum_hbm, sums_ref), (inner_hbm, inner), (outer_hbm, outer), (down_hbm, down),
        (stay_hbm, atoms_ref.at[:, pl.ds(0, STAY)]), (new_hbm, atoms_ref.at[:, pl.ds(STAY, ARRIVE)]),
        (stay_basis_hbm, basis_ref.at[:, pl.ds(0, STAY)]), (new_basis_hbm, basis_ref.at[:, pl.ds(STAY, ARRIVE)]),
        (pair_hbm, pair),
    )
    table[OPS * REMOTE :, :] = jnp.zeros((8, LANES), f32)
    copies[0].wait()
    load_ops(ops, both)
    width = FAR_ROWS // 4
    for lo in range(0, FAR_ROWS, width):
        premultiply(far_ref[lo : lo + width, :], both, table, lo, REMOTE)
    premultiply(below_ref[...], both, table, FAR_ROWS, REMOTE)
    premultiply(above_ref[...], both, table, FAR_ROWS + EXTRA, REMOTE)

    coarse[...] = far_ref[pl.ds(SHORT, DEVICES, stride=BLOCK), :]
    me = me_ref[0]
    group, member = me // MEMBERS, lax.rem(me, MEMBERS)
    who = lax.broadcasted_iota(i32, (40, DEVICES), 1)
    which = lax.broadcasted_iota(i32, (40, DEVICES), 0)
    its_group, its_member = who // MEMBERS, lax.rem(who, MEMBERS)
    near = (its_group == group) & (jnp.abs(its_member - member) - 1 == which) & (which < MEMBERS)
    away = (jnp.abs(its_group - group) - 1 == which - MEMBERS) & (which >= MEMBERS)
    chosen = jnp.where(near | away, 1.0, 0.0)
    sums = lax.dot_general(chosen, coarse[...], NN, precision=lax.Precision.HIGHEST, preferred_element_type=f32)
    for copy in copies[1:5]:
        copy.wait()
    field = jnp.sum(inner[...] * sums[None, 0 : MEMBERS - 1, 0:COEF], axis=1)
    for o in range(GROUPS - 1):
        field = field + outer[o] * sums[MEMBERS + o : MEMBERS + o + 1, 0:COEF]
    field = jnp.broadcast_to(jnp.sum(field, axis=1, keepdims=True), (COEF, LANES))
    child = lax.rem(lax.broadcasted_iota(i32, (COEF, LANES), 1), OPS)
    pattern = jnp.zeros((COEF, LANES), f32)
    for o in range(OPS):
        one = lax.dot_general(
            down[pl.ds(o, COEF, stride=OPS), :], field, NN,
            precision=lax.Precision.HIGHEST, preferred_element_type=f32,
        )
        pattern = jnp.where(child == o, one, pattern)

    def store(r, g, total):
        rows[pl.ds(place_ref.at[pl.ds(r * LANES, LANES)][g], 1), :] = total

    for n in range(LIST, -1, -1):
        row_sums(
            index_ref, table, n, count_ref[n + 1], count_ref[n], lambda r, g: sums_ref[pl.ds(r * LANES + g, 1), :], store
        )

    for lo in range(0, CELLS, LANES):
        local_ref[:, lo : lo + LANES] = rows[lo : lo + LANES, :].T[0:COEF, :] + pattern
    local = local_ref[...]
    high, rest = split(local)
    high = jnp.concatenate([high, jnp.zeros((LANES - COEF, CELLS), bf16)], axis=0)
    rest = jnp.concatenate([rest, jnp.zeros((LANES - COEF, CELLS), bf16)], axis=0)
    stacked = jnp.concatenate([high, rest], axis=0)
    for copy in copies[5:10]:
        copy.wait()
    wide = 512
    for lo in range(0, SLOTS, wide):
        cells, basis = atoms_ref[4:5, lo : lo + wide], basis_ref[:, lo : lo + wide]
        at = lax.dot_general(stacked, cell_hot(cells.astype(i32)), NN, preferred_element_type=f32)
        read = jnp.sum((at[:LANES] + at[LANES:]) * basis, axis=0, keepdims=True)
        read = read * COEF**-0.5 + pair[:, lo : lo + wide]
        for at in range(0, wide, LANES):
            i = (lo + at) // LANES
            pot_ref[i : i + 1, :] = read[:, at : at + LANES]


VM = pl.BlockSpec(memory_space=pltpu.VMEM)
SM = pl.BlockSpec(memory_space=pltpu.SMEM)
HB = pl.BlockSpec(memory_space=pltpu.HBM)


def call(kernel, name, ins, outs, scratch, copies, flops, *operands):
    cost = pl.CostEstimate(flops=1000, bytes_accessed=1000, transcendentals=0)
    return pl.pallas_call(
        kernel,
        name=name,
        in_specs=ins,
        out_specs=[spec for spec, _, _ in outs],
        out_shape=[jax.ShapeDtypeStruct(shape, kind) for _, shape, kind in outs],
        scratch_shapes=[pltpu.VMEM(shape, kind) if isinstance(shape, tuple) else shape for shape, kind in scratch]
        + [pltpu.SemaphoreType.DMA((count,)) for count in copies],
        cost_estimate=cost,
        compiler_params=pltpu.CompilerParams(vmem_limit_bytes=56 * MIB),
    )(*operands)


def on_device(
    atom_rows,
    atom_owner,
    atom_cell,
    need_cells,
    list_entry,
    list_class,
    basis_freq,
    basis_phase,
    near_ops,
    up_ops,
    far_in,
    far_out,
    down_ops,
):
    me = (lax.axis_index("group") * MEMBERS + lax.axis_index("dev")).reshape(1).astype(i32)
    freq, phase = basis_freq.T, basis_phase.reshape(1, COEF)
    waves = [((3, COEF), f32), ((1, COEF), f32)]
    owner_row, cell_row = atom_owner.reshape(1, STAY), atom_cell.reshape(1, STAY)
    by_row = [ops.transpose(1, 0, 2).reshape(COEF * OPS, COEF) for ops in (near_ops, up_ops, down_ops)]
    ops_shape = ((COEF * OPS, COEF), f32)
    mine = [((1, STAY), i32), ((4, STAY), f32), ((1, STAY), i32)]

    (outbound,) = call(
        pack_kernel, "pack", [SM, HB, HB, HB, HB], [(VM, (DEVICES * PIECE, LANES), f32)],
        [((8, LANES), i32), ((STAY // LANES, LANES), i32), *mine[1:], ((8, 512), f32)], [4], 10**6,
        me, need_cells.transpose(0, 2, 1), atom_owner.reshape(STAY // LANES, LANES), atom_rows, cell_row,
    )
    got = lax.all_to_all(outbound.reshape(DEVICES, 1, PIECE * LANES), AXES, split_axis=0, concat_axis=0, tiled=True)
    got = got.reshape(DEVICES * PIECE, LANES)

    shape3, tile = (LIST, CELLS // LANES, LANES), (CELLS // LANES, LANES)
    early_outs = [
        ((8, STAY), f32), ((LANES, STAY), f32), ((CELLS, LANES), f32), ((1, STAY), f32),
        (shape3, i32), (shape3, i32), (tile, i32), (tile, i32),
    ]
    stay_atoms, stay_basis, stay_pole, stay_pair, own_index, far_index, place, counts = call(
        early_kernel, "early", [SM] + [HB] * 7, [(HB, *out) for out in early_outs],
        [*mine, *waves, *[((LIST, CELLS), i32)] * 2, *[(shape3, i32)] * 2, ((80, CELLS), f32), ((8, LANES), f32), *early_outs,
         *pair_scratch(STAY, STAY)], [7, 8], 12 * 10**9,
        me, owner_row, atom_rows, cell_row, freq, phase, list_entry, list_class,
    )
    own_index, far_index, place, counts = (one.reshape(-1) for one in (own_index, far_index, place, counts))
    merge_outs = [((CELLS, LANES), f32), ((LANES, ARRIVE), f32), ((8, ARRIVE), f32)]
    send, low, high, pole, new_basis, new_atoms = call(
        merge_kernel, "merge", [SM, VM] + [HB] * 4,
        [(VM, (FAR_ROWS, LANES), f32), (VM, (EXTRA, LANES), f32), (VM, (EXTRA, LANES), f32), *[(HB, *out) for out in merge_outs]],
        [*waves, ((CELLS, LANES), f32), ops_shape, ((8, LANES), f32), *merge_outs[::-1],
         ((WRAP, LANES), f32), ((LANES, LANES), f32), ((1, LANES), i32), (pltpu.SMEM((1, LANES), i32), None)],
        [5, 3], 2 * 10**9,
        me, got, freq, phase, stay_pole, by_row[1],
    )
    far_rows = lax.all_to_all(send.reshape(DEVICES, 1, BLOCK * LANES), AXES, split_axis=0, concat_axis=0, tiled=True)
    far_rows = far_rows.reshape(FAR_ROWS, LANES)
    extra = ((EXTRA, LANES), f32)
    low, high, pair = call(
        cross_kernel, "cross", [HB] * 5, [(HB, *extra), (HB, *extra), (HB, (1, SLOTS), f32)],
        [extra, extra, ((8, SLOTS), f32), ((1, SLOTS), f32), *pair_scratch(SLOTS, ARRIVE)], [5, 3], 4 * 10**9,
        low, high, stay_atoms, new_atoms, stay_pair,
    )
    below, above = shift(high, 1), shift(low, -1)
    (own_sum,) = call(
        mid_kernel, "mid", [SM, SM, HB, HB], [(HB, (CELLS, LANES), f32)],
        [((OPS * CELLS + 8, LANES), f32), ((OPS * LANES, 3 * LANES), bf16), ops_shape, *[((CELLS, LANES), f32)] * 2],
        [3], 20 * 10**9,
        own_index, counts, pole, by_row[0],
    )
    local, pot = call(
        last_kernel, "last", [SM] * 4 + [VM] * 3 + [HB] * 10, [(VM, (COEF, CELLS), f32), (VM, (SLOTS // LANES, LANES), f32)],
        [((OPS * REMOTE + 8, LANES), f32), ((OPS * LANES, 3 * LANES), bf16), *[((CELLS, LANES), f32)] * 2, ((DEVICES, LANES), f32),
         ops_shape, ((COEF, MEMBERS - 1, COEF), f32), ((GROUPS - 1, COEF, COEF), f32), ops_shape, ((8, SLOTS), f32),
         ((LANES, SLOTS), f32), ((1, SLOTS), f32)],
        [10], 8 * 10**9,
        me, far_index, counts, place, far_rows, below, above, by_row[0], own_sum,
        far_in.transpose(1, 0, 2), far_out, by_row[2], stay_atoms, new_atoms, stay_basis, new_basis, pair,
    )
    return local, pot.reshape(SLOTS)


def solution(mesh):
    in_specs = (
        P(None, AXES),
        P(AXES),
        P(AXES),
        P(AXES, None, None),
        P(None, AXES),
        P(None, AXES),
        P(),
        P(),
        P(),
        P(),
        P(),
        P(),
        P(),
    )
    out_specs = (P(None, AXES), P(AXES))
    return jax.shard_map(on_device, mesh=mesh, in_specs=in_specs, out_specs=out_specs, check_vma=False)
```

```python
import math

import jax
import jax.numpy as jnp
from jax import lax
from jax.experimental import pallas as pl
from jax.experimental.pallas import tpu as pltpu
from jax.sharding import PartitionSpec as P

COEF = 121
LANES = 128
CELLS = 1024
STAY = 2048
CAP = 128
ARRIVE = 4 * CAP
SLOTS = STAY + ARRIVE
LIST = 16
OPS = 8
SLOT = 72
SHORT = 18
BLOCK = SHORT + 1
DEVICES = 128
MEMBERS = 32
GROUPS = 4
PIECE = 6
EXTRA = 56
FAR_ROWS = DEVICES * BLOCK
REMOTE = FAR_ROWS + 2 * EXTRA
WRAP = CELLS + 80
TALL, WIDE = 256, 512
AXES = ("group", "dev")
MIB = 2**20
f32, bf16, i32 = jnp.float32, jnp.bfloat16, jnp.int32
SIN = [(-1) ** n * (2 * math.pi) ** (2 * n + 1) / math.factorial(2 * n + 1) for n in range(6)]

NT = (((1,), (1,)), ((), ()))
NN = (((1,), (0,)), ((), ()))


def swap(value, first):
    pairs = [(i, i + 1) for i in range(first, DEVICES - 1, 2)]
    return lax.ppermute(value, AXES, pairs + [(j, i) for i, j in pairs])


def split(value):
    high = value.astype(bf16)
    return high, (value - high.astype(f32)).astype(bf16)


def basis_of(waves, atoms):
    turns = waves[:, 3:4] + waves[:, 0:1] * atoms[0:1, :]
    turns = turns + waves[:, 1:2] * atoms[1:2, :]
    turns = turns + waves[:, 2:3] * atoms[2:3, :]
    turns = turns - jnp.floor(turns + 0.5)
    base = 0.25 - jnp.abs(turns)
    square = base * base
    total = jnp.full_like(square, SIN[5])
    for factor in SIN[4::-1]:
        total = total * square + factor
    return base * total


def cell_hot(cell_row):
    ids = lax.broadcasted_iota(i32, (CELLS, cell_row.shape[1]), 0) + 1
    return jnp.where(ids == cell_row, 1.0, 0.0).astype(bf16)


def poles(basis, charge, hot):
    high, low = split(basis * charge)
    both = lax.dot_general(hot, jnp.concatenate([high, low], axis=0), NT, preferred_element_type=f32)
    return both[:, :LANES] + both[:, LANES:]


def load(sems, *pairs):
    copies = [pltpu.make_async_copy(src, dst, sems.at[i]) for i, (src, dst) in enumerate(pairs)]
    for copy in copies:
        copy.start()
    return copies


def waves_of(freq_ref, phase_ref, flat):
    flat[...] = jnp.zeros_like(flat)
    flat[0:3, 0:COEF] = freq_ref[...] * (0.5 / math.pi)
    flat[3:4, 0:COEF] = phase_ref[...] * (0.5 / math.pi)
    return flat[...].T


def pack_kernel(me_ref, need_hbm, owner_hbm, rows_hbm, cell_hbm, out_ref, need, owner, rows, cell, buf, sems):
    copies = load(
        sems, (owner_hbm, owner), (rows_hbm, rows), (cell_hbm, cell), (need_hbm.at[0, pl.ds(0, 8), :], need)
    )
    out_ref[...] = jnp.zeros_like(out_ref)
    buf[...] = jnp.zeros_like(buf)
    for copy in copies:
        copy.wait()
    me = me_ref[0]
    gap = owner[...] - me

    def count(by):
        return jnp.sum(jnp.where(gap == by, 1.0, 0.0)).astype(i32)

    for at, lo in ((0, 0), (256, STAY - 256)):
        buf[0:4, at : at + 256] = rows[:, lo : lo + 256]
        buf[4:5, at : at + 256] = (cell[:, lo : lo + 256] + 1).astype(f32)
    lane = lax.broadcasted_iota(i32, (8, CAP), 1)
    low2, low1, up1, up2 = count(-2), count(-1), count(1), count(2)
    first = jnp.broadcast_to(need[0:1, :].astype(f32), (LANES, LANES)).T
    out_ref[pl.ds(5, DEVICES, stride=PIECE), :] = first
    ahead = pltpu.roll(buf[:, :256], lax.rem(256 - low2, 256), 1)
    behind = pltpu.roll(buf[:, 256:], lax.rem(up1 + up2, 256), 1)
    last = pltpu.roll(buf[:, 256:], lax.rem(up2, 256), 1)
    for by, count_by, piece in (
        (-2, low2, buf[:, :CAP]), (-1, low1, ahead[:, :CAP]), (1, up1, behind[:, :CAP]), (2, up2, last[:, :CAP])
    ):
        to = me + by

        @pl.when((to >= 0) & (to < DEVICES))
        def _(to=to, count_by=count_by, piece=piece):
            out_ref[pl.ds(to * PIECE, 5), :] = jnp.where(lane < count_by, piece, 0.0)[0:5, :]


def features(atoms_ref, left, right):
    def parts(value, count):
        out = []
        for _ in range(count):
            out.append(value.astype(bf16).astype(f32))
            value = value - out[-1]
        return out

    left[...] = jnp.zeros_like(left)
    right[...] = jnp.zeros_like(right)
    square = None
    for d in range(3):
        value = atoms_ref[d : d + 1, :]
        square = value * value if square is None else square + value * value
        for i, (a, b) in enumerate((a, b) for a in parts(value, 2) for b in parts(value, 2)):
            left[4 * d + i : 4 * d + i + 1, :] = a
            right[4 * d + i : 4 * d + i + 1, :] = -2.0 * b
    ones = jnp.ones_like(square)
    for i, part in enumerate(parts(square, 3)):
        left[12 + i : 13 + i, :] = part
        right[12 + i : 13 + i, :] = ones
    for i, part in enumerate(parts(square + 0.25, 3)):
        left[15 + i : 16 + i, :] = ones
        right[15 + i : 16 + i, :] = part


class Pairs:
    def __init__(self, atoms_ref, pair_ref, left, right, left_cols, right_low, charges, cells, back, start):
        self.atoms, self.pair, self.left_cols, self.right_low = atoms_ref, pair_ref, left_cols, right_low
        self.charges, self.cells, self.back, self.start = charges, cells, back, start
        features(atoms_ref, left, right)
        right_low[...] = right[...].astype(bf16)
        for at in range(0, left_cols.shape[0], LANES):
            cut, rows = slice(start + at, start + at + LANES), slice(at, at + LANES)
            left_cols[rows, :] = left[:, cut].T.astype(bf16)
            charges[rows, :] = jnp.broadcast_to(atoms_ref[3:4, cut], (LANES, LANES)).T
            cells[rows, :] = jnp.broadcast_to(atoms_ref[4:5, cut], (LANES, LANES)).T
        back[...] = jnp.zeros_like(back)

    def block(self, at, lo, both):
        far = lax.dot_general(
            self.left_cols[pl.ds(at, TALL), :], self.right_low[:, pl.ds(lo, WIDE)], NN, preferred_element_type=f32
        )
        its_cell = jnp.concatenate([self.cells[pl.ds(at, TALL), :]] * (WIDE // LANES), axis=1)
        its_charge = jnp.concatenate([self.charges[pl.ds(at, TALL), :]] * (WIDE // LANES), axis=1)
        near = jnp.where(its_cell == self.atoms[4:5, pl.ds(lo, WIDE)], lax.rsqrt(far), 0.0)
        total = jnp.sum((near * its_charge).reshape(TALL // 8, 8, WIDE), axis=0)
        self.pair[:, pl.ds(lo, WIDE)] += jnp.sum(total, axis=0, keepdims=True)
        if both:
            near = near * self.atoms[3:4, pl.ds(lo, WIDE)]
            total = near[:, 0:LANES]
            for k in range(1, WIDE // LANES):
                total = total + near[:, k * LANES : (k + 1) * LANES]
            self.back[pl.ds(at, TALL), :] += total

    def close(self):
        for at in range(0, self.back.shape[0], LANES):
            cut = slice(self.start + at, self.start + at + LANES)
            itself = self.atoms[3:4, cut] * lax.rsqrt(jnp.full((1, LANES), 0.25, f32))
            self.pair[:, cut] += jnp.sum(self.back[at : at + LANES, :].T, axis=0, keepdims=True) - itself


def pair_scratch(slots, rows):
    return [
        ((32, slots), f32), ((32, slots), f32), ((rows, 32), bf16), ((32, slots), bf16),
        *[((rows, LANES), f32)] * 3,
    ]


def sort_rows(keys):
    keys = list(keys)
    step = 1
    while step < LIST:
        gap = step
        while gap >= 1:
            for base in range(gap % step, LIST - gap, 2 * gap):
                for i in range(min(gap, LIST - base - gap)):
                    a, b = base + i, base + i + gap
                    if a // (2 * step) == b // (2 * step):
                        keys[a], keys[b] = jnp.maximum(keys[a], keys[b]), jnp.minimum(keys[a], keys[b])
            gap //= 2
        step *= 2
    return keys


def order(me, entry, kind, own_ref, far_ref, cell_ref, count_ref, lists):
    asked = jnp.maximum(entry - CELLS, 0)
    source = jnp.floor((asked.astype(f32) + 0.5) * (1.0 / SLOT)).astype(i32)
    slot = asked - source * SLOT
    side = jnp.where((source | 1) == (me | 1), FAR_ROWS, FAR_ROWS + EXTRA)
    row = jnp.where(slot < SHORT, source * BLOCK + slot, side + slot - SHORT)
    key = jnp.where(entry < CELLS, -1, kind * REMOTE + row)
    used = jnp.sum(jnp.where(key >= 0, 1, 0), axis=0)
    far = sort_rows(key[l] for l in range(LIST))
    key = jnp.where(entry < CELLS, kind * CELLS + entry, -1)
    own = sort_rows(key[l] for l in range(LIST))
    own = [jnp.where(one < 0, OPS * CELLS, one) for one in own]
    far = [jnp.where(one < 0, OPS * REMOTE, one) for one in far]

    def flat(value):
        return jnp.concatenate([value[r : r + 1, :] for r in range(CELLS // LANES)], axis=1)

    used_row = flat(used).astype(f32)
    rank_key = used_row * CELLS + lax.broadcasted_iota(i32, (1, CELLS), 1).astype(f32)
    rank = jnp.zeros((8, CELLS), f32)
    for lo in range(0, CELLS, LANES):
        column = jnp.broadcast_to(rank_key[:, lo : lo + LANES], (LANES, LANES)).T
        ahead = jnp.where(jnp.concatenate([column] * (CELLS // LANES), axis=1) > rank_key, 1.0, 0.0)
        rank = rank + jnp.sum(ahead.reshape(LANES // 8, 8, CELLS), axis=0)
    rank = jnp.sum(rank, axis=0, keepdims=True).astype(i32)
    place = (rank & 7) * LANES + (rank >> 3)
    moved = jnp.where(lax.broadcasted_iota(i32, (CELLS, CELLS), 0) == place, 1.0, 0.0).astype(bf16)
    lists[...] = jnp.zeros_like(lists)
    for l in range(LIST):
        for at, value in ((l, far[l] >> 8), (16 + l, far[l] & 255), (32 + l, own[l] >> 8), (48 + l, own[l] & 255)):
            for r in range(CELLS // LANES):
                lists[at : at + 1, r * LANES : (r + 1) * LANES] = value[r : r + 1, :].astype(f32)
    ids = lax.broadcasted_iota(i32, (1, CELLS), 1)
    lists[64:65, :] = (ids >> 8).astype(f32)
    lists[65:66, :] = (ids & 255).astype(f32)
    lists[66:67, :] = used_row
    sorted_lists = lax.dot_general(lists[...].astype(bf16), moved, NT, preferred_element_type=f32).astype(i32)
    far_rows = sorted_lists[0:16] * 256 + sorted_lists[16:32]
    own_rows = sorted_lists[32:48] * 256 + sorted_lists[48:64]
    cells = sorted_lists[64:65] * 256 + sorted_lists[65:66]
    for r in range(CELLS // LANES):
        cut = slice(r * LANES, (r + 1) * LANES)
        for l in range(LIST):
            far_ref[l, r : r + 1, :] = far_rows[l : l + 1, cut]
            own_ref[l, r : r + 1, :] = own_rows[l : l + 1, cut]
        cell_ref[r : r + 1, :] = cells[:, cut]
    group = lax.broadcasted_iota(i32, (LANES, LANES), 0)
    number = lax.broadcasted_iota(i32, (LANES, LANES), 1)
    most = jnp.broadcast_to(sorted_lists[66:67, 0:LANES].astype(f32), (LANES, LANES)).T.astype(i32)
    least = jnp.broadcast_to(sorted_lists[66:67, CELLS - LANES : CELLS].astype(f32), (LANES, LANES)).T.astype(i32)
    count_ref[...] = jnp.zeros_like(count_ref)
    remote = jnp.where((most >= number) & ((group & 1) == 0), 1.0, 0.0)
    local = jnp.where((LIST - least <= number) & ((group & 1) == 1), 1.0, 0.0)
    count_ref[0:1, :] = jnp.sum(remote, axis=0, keepdims=True).astype(i32)
    count_ref[1:2, :] = jnp.sum(local, axis=0, keepdims=True).astype(i32)


def early_kernel(
    me_ref, owner_hbm, rows_hbm, cell_hbm, freq_hbm, phase_hbm, entry_hbm, class_hbm,
    atoms_hbm, basis_hbm, pole_hbm, pair_hbm, own_hbm, far_hbm, place_hbm, count_hbm,
    owner, rows, cell, freq, phase, entry, kind, entry3, kind3, lists, flat,
    atoms_ref, basis_ref, pole_ref, pair_ref, own_ref, far_ref, place_ref, count_ref, *rest,
):
    *pair_buffers, sems, out_sems = rest
    copies = load(
        sems, (owner_hbm, owner), (rows_hbm, rows), (cell_hbm, cell), (freq_hbm, freq), (phase_hbm, phase),
        (entry_hbm, entry), (class_hbm, kind),
    )
    atoms_ref[...] = jnp.zeros_like(atoms_ref)
    for copy in copies[:5]:
        copy.wait()
    stays = owner[...] == me_ref[0]
    atoms_ref[0:4, :] = jnp.where(stays, rows[...], 0.0)
    atoms_ref[4:5, :] = jnp.where(stays, (cell[...] + 1).astype(f32), 0.0)
    waves = waves_of(freq, phase, flat)
    width = 512
    for lo in range(0, STAY, width):
        atoms = atoms_ref[:, lo : lo + width]
        basis = basis_of(waves, atoms)
        basis_ref[:, lo : lo + width] = basis
        part = poles(basis, atoms[3:4, :], cell_hot(atoms[4:5, :].astype(i32)))
        pole_ref[...] = part if lo == 0 else pole_ref[...] + part
    outs = load(out_sems, (atoms_ref, atoms_hbm), (basis_ref, basis_hbm), (pole_ref, pole_hbm))
    for copy in copies[5:]:
        copy.wait()
    for l in range(LIST):
        for r in range(CELLS // LANES):
            entry3[l, r : r + 1, :] = entry[l : l + 1, r * LANES : (r + 1) * LANES]
            kind3[l, r : r + 1, :] = kind[l : l + 1, r * LANES : (r + 1) * LANES]
    order(me_ref[0], entry3[...], kind3[...], own_ref, far_ref, place_ref, count_ref, lists)
    more = [(own_ref, own_hbm), (far_ref, far_hbm), (place_ref, place_hbm), (count_ref, count_hbm)]
    outs += load(out_sems.at[pl.ds(3, 4)], *more)

    pair_ref[...] = jnp.zeros_like(pair_ref)
    pairs = Pairs(atoms_ref, pair_ref, *pair_buffers, 0)
    blocks, strips = STAY // WIDE, WIDE // TALL

    def strip(c, reach):
        at, mine = pl.multiple_of(c * TALL, TALL), c // strips
        pairs.block(at, pl.multiple_of(mine * WIDE, WIDE), False)
        for by in range(1, reach + 1):
            pairs.block(at, pl.multiple_of(lax.rem(mine + by, blocks) * WIDE, WIDE), True)

    def wide_strip(c, _):
        strip(c, 2)
        return 0

    def short_strip(c, _):
        strip(c, 1)
        return 0

    half = blocks * strips // 2
    lax.fori_loop(0, half, wide_strip, 0)
    lax.fori_loop(half, 2 * half, short_strip, 0)
    pairs.close()
    last = pltpu.make_async_copy(pair_ref, pair_hbm, out_sems.at[7])
    last.start()
    for copy in outs:
        copy.wait()
    last.wait()


def merge_kernel(
    me_ref, got_ref, freq_hbm, phase_hbm, stay_hbm, up_hbm,
    send_ref, mate_ref, other_ref, pole_hbm, basis_hbm, atoms_hbm,
    freq, phase, stay, up, flat, atoms_ref, basis_ref, pole_ref, ring, turned, ids, first_ref, sems, out_sems,
):
    copies = load(sems, (freq_hbm, freq), (phase_hbm, phase), (stay_hbm, stay), (up_hbm, up))
    me = me_ref[0]
    row = lax.broadcasted_iota(i32, (DEVICES, LANES), 0)
    lane = lax.broadcasted_iota(i32, (DEVICES, LANES), 1)
    asked = jnp.where(row == lane, got_ref[pl.ds(5, DEVICES, stride=PIECE), :], 0.0)
    ids[...] = jnp.maximum(jnp.sum(asked, axis=0, keepdims=True).astype(i32), 0)
    to_scalars = pltpu.make_async_copy(ids, first_ref, sems.at[4])
    to_scalars.start()
    atoms_ref[...] = jnp.zeros_like(atoms_ref)
    for at, by in enumerate((-2, -1, 1, 2)):
        source = me - by

        @pl.when((source >= 0) & (source < DEVICES))
        def _(at=at, source=source):
            atoms_ref[0:5, at * CAP : (at + 1) * CAP] = got_ref[pl.ds(source * PIECE, 5), :]

    copies[0].wait()
    copies[1].wait()
    atoms = atoms_ref[...]
    basis = basis_of(waves_of(freq, phase, flat), atoms)
    basis_ref[...] = basis
    both = poles(basis, atoms[3:4, :], cell_hot(atoms[4:5, :].astype(i32)))
    copies[2].wait()
    pole = stay[...] + both
    pole_ref[...] = pole
    outs = load(out_sems, (atoms_ref, atoms_hbm), (basis_ref, basis_hbm), (pole_ref, pole_hbm))
    ring[0:CELLS, :] = pole
    ring[CELLS:WRAP, :] = pole[0 : WRAP - CELLS, :]
    grouped = jnp.sum(pole.reshape(CELLS // 8, 8, LANES), axis=0)
    copies[3].wait()
    raised = up[...].reshape(COEF, OPS, COEF) * grouped[None, :, :COEF]
    turned[...] = jnp.zeros_like(turned)
    turned[0:COEF, 0:COEF] = jnp.sum(raised, axis=1)
    coarse = jnp.sum(turned[...].T, axis=0, keepdims=True)
    to_scalars.wait()

    def one(t, _):
        send_ref[pl.ds(t * BLOCK, SHORT), :] = ring[pl.ds(first_ref[0, t], SHORT), :]
        send_ref[pl.ds(t * BLOCK + SHORT, 1), :] = coarse
        return 0

    lax.fori_loop(0, DEVICES, one, 0, unroll=8)
    odd = lax.rem(me, 2)
    mate = me + 1 - 2 * odd
    other = jnp.clip(me - 1 + 2 * odd, 0, DEVICES - 1)
    mate_ref[...] = ring[pl.ds(first_ref[0, mate] + SHORT, EXTRA), :]
    other_ref[...] = ring[pl.ds(first_ref[0, other] + SHORT, EXTRA), :]
    for copy in outs:
        copy.wait()


def load_ops(ops_ref, both):
    both[...] = jnp.zeros_like(both)
    for o in range(OPS):
        high, low = split(ops_ref[pl.ds(o, COEF, stride=OPS), :])
        for at, part in enumerate((high, high, low)):
            both[o * LANES : o * LANES + COEF, at * LANES : at * LANES + COEF] = part


def premultiply(rows, both, table, at, pitch):
    high, low = split(rows)
    parts = jnp.concatenate([high, low, high], axis=1)
    for o in range(0, OPS, 2):
        pair = both[o * LANES : (o + 2) * LANES, :]
        out = lax.dot_general(parts, pair, NT, preferred_element_type=f32)
        for k in range(2):
            table[pl.ds((o + k) * pitch + at, rows.shape[0]), :] = out[:, k * LANES : (k + 1) * LANES]


def index_of(index_ref, l, r, g):
    return index_ref.at[pl.ds(l * CELLS + r * LANES, LANES)][g]


def row_sums(index_ref, table, count, first, last, start, store):
    def pair(p, _):
        for g in (2 * p, 2 * p + 1):
            for r in range(8):
                total = None if start is None else start(r, g)
                for l in range(count):
                    row = table[pl.ds(index_of(index_ref, l, r, g), 1), :]
                    total = row if total is None else total + row
                store(r, g, jnp.zeros((1, LANES), f32) if total is None else total)
        return 0

    lax.fori_loop(first, last, pair, 0)


def cross_kernel(stay_hbm, new_hbm, stay_pair_hbm, pair_hbm, atoms_ref, pair_ref, *rest):
    *pair_buffers, sems, out_sems = rest
    copies = load(
        sems, (stay_hbm, atoms_ref.at[:, pl.ds(0, STAY)]), (new_hbm, atoms_ref.at[:, pl.ds(STAY, ARRIVE)]),
        (stay_pair_hbm, pair_ref.at[:, pl.ds(0, STAY)]),
    )
    pair_ref[:, STAY:] = jnp.zeros((1, ARRIVE), f32)
    for copy in copies:
        copy.wait()
    pairs = Pairs(atoms_ref, pair_ref, *pair_buffers, STAY)

    def strip(c, _):
        at = pl.multiple_of(c * TALL, TALL)
        pairs.block(at, STAY, False)
        for lo in range(0, STAY, WIDE):
            pairs.block(at, lo, True)
        return 0

    lax.fori_loop(0, ARRIVE // TALL, strip, 0)
    pairs.close()
    (out,) = load(out_sems, (pair_ref, pair_hbm))
    out.wait()


def mid_kernel(own_hbm, count_ref, pole_hbm, ops_hbm, sum_hbm, own_ref, table, both, ops, pole, sum_ref, sems):
    copies = load(sems, (ops_hbm, ops), (pole_hbm, pole), (own_hbm, own_ref))
    table[OPS * CELLS :, :] = jnp.zeros((8, LANES), f32)
    copies[0].wait()
    load_ops(ops, both)
    copies[1].wait()
    width = CELLS // 2
    for lo in range(0, CELLS, width):
        premultiply(pole[lo : lo + width, :], both, table, lo, CELLS)
    copies[2].wait()

    def store(r, g, total):
        sum_ref[pl.ds(r * LANES + g, 1), :] = total

    for n in range(LIST + 1):
        first = 0 if n == 0 else count_ref[LANES + n - 1]
        row_sums(own_ref, table, n, first, count_ref[LANES + n], None, store)
    out = pltpu.make_async_copy(sum_ref, sum_hbm, sems.at[3])
    out.start()
    out.wait()


def last_kernel(
    me_ref, index_hbm, count_ref, place_ref, far_ref, near_ref, next_ref, ops_hbm, sum_hbm, inner_hbm, outer_hbm,
    down_hbm, stay_hbm, new_hbm, stay_basis_hbm, new_basis_hbm, pair_hbm, local_ref, pot_ref,
    index_ref, table, both, sums_ref, rows, coarse, ops, inner, outer, down, atoms_ref, basis_ref, pair, sems,
):
    copies = load(
        sems, (ops_hbm, ops), (sum_hbm, sums_ref), (inner_hbm, inner), (outer_hbm, outer), (down_hbm, down),
        (stay_hbm, atoms_ref.at[:, pl.ds(0, STAY)]), (new_hbm, atoms_ref.at[:, pl.ds(STAY, ARRIVE)]),
        (stay_basis_hbm, basis_ref.at[:, pl.ds(0, STAY)]), (new_basis_hbm, basis_ref.at[:, pl.ds(STAY, ARRIVE)]),
        (pair_hbm, pair), (index_hbm, index_ref),
    )
    table[OPS * REMOTE :, :] = jnp.zeros((8, LANES), f32)
    copies[0].wait()
    load_ops(ops, both)
    width = FAR_ROWS // 4
    for lo in range(0, FAR_ROWS, width):
        premultiply(far_ref[lo : lo + width, :], both, table, lo, REMOTE)
    premultiply(near_ref[...], both, table, FAR_ROWS, REMOTE)
    premultiply(next_ref[...], both, table, FAR_ROWS + EXTRA, REMOTE)

    coarse[...] = far_ref[pl.ds(SHORT, DEVICES, stride=BLOCK), :]
    me = me_ref[0]
    group, member = me // MEMBERS, lax.rem(me, MEMBERS)
    who = lax.broadcasted_iota(i32, (40, DEVICES), 1)
    which = lax.broadcasted_iota(i32, (40, DEVICES), 0)
    its_group, its_member = who // MEMBERS, lax.rem(who, MEMBERS)
    near = (its_group == group) & (jnp.abs(its_member - member) - 1 == which) & (which < MEMBERS)
    away = (jnp.abs(its_group - group) - 1 == which - MEMBERS) & (which >= MEMBERS)
    chosen = jnp.where(near | away, 1.0, 0.0)
    sums = lax.dot_general(chosen, coarse[...], NN, precision=lax.Precision.HIGHEST, preferred_element_type=f32)
    for copy in copies[1:5]:
        copy.wait()
    field = jnp.sum(inner[...] * sums[None, 0 : MEMBERS - 1, 0:COEF], axis=1)
    for o in range(GROUPS - 1):
        field = field + outer[o] * sums[MEMBERS + o : MEMBERS + o + 1, 0:COEF]
    field = jnp.broadcast_to(jnp.sum(field, axis=1, keepdims=True), (COEF, LANES))
    child = lax.rem(lax.broadcasted_iota(i32, (COEF, LANES), 1), OPS)
    pattern = jnp.zeros((COEF, LANES), f32)
    for o in range(OPS):
        one = lax.dot_general(
            down[pl.ds(o, COEF, stride=OPS), :], field, NN,
            precision=lax.Precision.HIGHEST, preferred_element_type=f32,
        )
        pattern = jnp.where(child == o, one, pattern)

    def store(r, g, total):
        rows[pl.ds(place_ref.at[pl.ds(r * LANES, LANES)][g], 1), :] = total

    copies[10].wait()
    for n in range(LIST, -1, -1):
        row_sums(
            index_ref, table, n, count_ref[n + 1], count_ref[n], lambda r, g: sums_ref[pl.ds(r * LANES + g, 1), :], store
        )

    for lo in range(0, CELLS, LANES):
        local_ref[:, lo : lo + LANES] = rows[lo : lo + LANES, :].T[0:COEF, :] + pattern
    local = local_ref[...]
    high, rest = split(local)
    high = jnp.concatenate([high, jnp.zeros((LANES - COEF, CELLS), bf16)], axis=0)
    rest = jnp.concatenate([rest, jnp.zeros((LANES - COEF, CELLS), bf16)], axis=0)
    stacked = jnp.concatenate([high, rest], axis=0)
    for copy in copies[5:10]:
        copy.wait()
    wide = 512
    for lo in range(0, SLOTS, wide):
        cells, basis = atoms_ref[4:5, lo : lo + wide], basis_ref[:, lo : lo + wide]
        at = lax.dot_general(stacked, cell_hot(cells.astype(i32)), NN, preferred_element_type=f32)
        read = jnp.sum((at[:LANES] + at[LANES:]) * basis, axis=0, keepdims=True)
        read = read * COEF**-0.5 + pair[:, lo : lo + wide]
        for at in range(0, wide, LANES):
            i = (lo + at) // LANES
            pot_ref[i : i + 1, :] = read[:, at : at + LANES]


VM = pl.BlockSpec(memory_space=pltpu.VMEM)
SM = pl.BlockSpec(memory_space=pltpu.SMEM)
HB = pl.BlockSpec(memory_space=pltpu.HBM)


def call(kernel, name, ins, outs, scratch, copies, *operands):
    cost = pl.CostEstimate(flops=1000, bytes_accessed=1000, transcendentals=0)
    return pl.pallas_call(
        kernel,
        name=name,
        in_specs=ins,
        out_specs=[spec for spec, _, _ in outs],
        out_shape=[jax.ShapeDtypeStruct(shape, kind) for _, shape, kind in outs],
        scratch_shapes=[pltpu.VMEM(shape, kind) if isinstance(shape, tuple) else shape for shape, kind in scratch]
        + [pltpu.SemaphoreType.DMA((count,)) for count in copies],
        cost_estimate=cost,
        compiler_params=pltpu.CompilerParams(vmem_limit_bytes=56 * MIB),
    )(*operands)


def on_device(
    atom_rows,
    atom_owner,
    atom_cell,
    need_cells,
    list_entry,
    list_class,
    basis_freq,
    basis_phase,
    near_ops,
    up_ops,
    far_in,
    far_out,
    down_ops,
):
    me = (lax.axis_index("group") * MEMBERS + lax.axis_index("dev")).reshape(1).astype(i32)
    freq, phase = basis_freq.T, basis_phase.reshape(1, COEF)
    waves = [((3, COEF), f32), ((1, COEF), f32)]
    owner_row, cell_row = atom_owner.reshape(1, STAY), atom_cell.reshape(1, STAY)
    by_row = [ops.transpose(1, 0, 2).reshape(COEF * OPS, COEF) for ops in (near_ops, up_ops, down_ops)]
    ops_shape = ((COEF * OPS, COEF), f32)
    mine = [((1, STAY), i32), ((4, STAY), f32), ((1, STAY), i32)]

    (outbound,) = call(
        pack_kernel, "pack", [SM, HB, HB, HB, HB], [(VM, (DEVICES * PIECE, LANES), f32)],
        [((8, LANES), i32), ((STAY // LANES, LANES), i32), *mine[1:], ((8, 512), f32)], [4],
        me, need_cells.transpose(0, 2, 1), atom_owner.reshape(STAY // LANES, LANES), atom_rows, cell_row,
    )
    got = lax.all_to_all(outbound.reshape(DEVICES, 1, PIECE * LANES), AXES, split_axis=0, concat_axis=0, tiled=True)
    got = got.reshape(DEVICES * PIECE, LANES)

    shape3, tile = (LIST, CELLS // LANES, LANES), (CELLS // LANES, LANES)
    early_outs = [
        ((8, STAY), f32), ((LANES, STAY), f32), ((CELLS, LANES), f32), ((1, STAY), f32),
        (shape3, i32), (shape3, i32), (tile, i32), (tile, i32),
    ]
    stay_atoms, stay_basis, stay_pole, stay_pair, own_index, far_index, place, counts = call(
        early_kernel, "early", [SM] + [HB] * 7, [(HB, *out) for out in early_outs],
        [*mine, *waves, *[((LIST, CELLS), i32)] * 2, *[(shape3, i32)] * 2, ((80, CELLS), f32), ((8, LANES), f32), *early_outs,
         *pair_scratch(STAY, STAY)], [7, 8],
        me, owner_row, atom_rows, cell_row, freq, phase, list_entry, list_class,
    )
    own_index, far_index, place, counts = (one.reshape(-1) for one in (own_index, far_index, place, counts))
    merge_outs = [((CELLS, LANES), f32), ((LANES, ARRIVE), f32), ((8, ARRIVE), f32)]
    send, mate_rows, other_rows, pole, new_basis, new_atoms = call(
        merge_kernel, "merge", [SM, VM] + [HB] * 4,
        [(VM, (FAR_ROWS, LANES), f32), (VM, (EXTRA, LANES), f32), (VM, (EXTRA, LANES), f32), *[(HB, *out) for out in merge_outs]],
        [*waves, ((CELLS, LANES), f32), ops_shape, ((8, LANES), f32), *merge_outs[::-1],
         ((WRAP, LANES), f32), ((LANES, LANES), f32), ((1, LANES), i32), (pltpu.SMEM((1, LANES), i32), None)],
        [5, 3],
        me, got, freq, phase, stay_pole, by_row[1],
    )
    far_rows = lax.all_to_all(send.reshape(DEVICES, 1, BLOCK * LANES), AXES, split_axis=0, concat_axis=0, tiled=True)
    far_rows = far_rows.reshape(FAR_ROWS, LANES)
    near_rows, next_rows = swap(mate_rows, 0), swap(other_rows, 1)
    (pair,) = call(
        cross_kernel, "cross", [HB] * 3, [(HB, (1, SLOTS), f32)],
        [((8, SLOTS), f32), ((1, SLOTS), f32), *pair_scratch(SLOTS, ARRIVE)], [3, 1],
        stay_atoms, new_atoms, stay_pair,
    )
    index_scratch = (pltpu.SMEM((LIST * CELLS,), i32), None)
    (own_sum,) = call(
        mid_kernel, "mid", [HB, SM, HB, HB], [(HB, (CELLS, LANES), f32)],
        [index_scratch, ((OPS * CELLS + 8, LANES), f32), ((OPS * LANES, 3 * LANES), bf16), ops_shape, *[((CELLS, LANES), f32)] * 2],
        [4],
        own_index, counts, pole, by_row[0],
    )
    local, pot = call(
        last_kernel, "last", [SM, HB, SM, SM] + [VM] * 3 + [HB] * 10, [(VM, (COEF, CELLS), f32), (VM, (SLOTS // LANES, LANES), f32)],
        [index_scratch, ((OPS * REMOTE + 8, LANES), f32), ((OPS * LANES, 3 * LANES), bf16), *[((CELLS, LANES), f32)] * 2, ((DEVICES, LANES), f32),
         ops_shape, ((COEF, MEMBERS - 1, COEF), f32), ((GROUPS - 1, COEF, COEF), f32), ops_shape, ((8, SLOTS), f32),
         ((LANES, SLOTS), f32), ((1, SLOTS), f32)],
        [11],
        me, far_index, counts, place, far_rows, near_rows, next_rows, by_row[0], own_sum,
        far_in.transpose(1, 0, 2), far_out, by_row[2], stay_atoms, new_atoms, stay_basis, new_basis, pair,
    )
    return local, pot.reshape(SLOTS)


def solution(mesh):
    in_specs = (
        P(None, AXES),
        P(AXES),
        P(AXES),
        P(AXES, None, None),
        P(None, AXES),
        P(None, AXES),
        P(),
        P(),
        P(),
        P(),
        P(),
        P(),
        P(),
    )
    out_specs = (P(None, AXES), P(AXES))
    return jax.shard_map(on_device, mesh=mesh, in_specs=in_specs, out_specs=out_specs, check_vma=False)
```

```python
import math

import jax
import jax.numpy as jnp
from jax import lax
from jax.experimental import pallas as pl
from jax.experimental.pallas import tpu as pltpu
from jax.sharding import PartitionSpec as P

COEF = 121
LANES = 128
CELLS = 1024
STAY = 2048
CAP = 128
ARRIVE = 4 * CAP
SLOTS = STAY + ARRIVE
LIST = 16
OPS = 8
SLOT = 72
SHORT = 18
BLOCK = SHORT + 1
DEVICES = 128
MEMBERS = 32
GROUPS = 4
PIECE = 6
EXTRA = 56
FAR_ROWS = DEVICES * BLOCK
REMOTE = FAR_ROWS + 2 * EXTRA
WRAP = CELLS + 80
TALL, WIDE = 256, 512
AXES = ("group", "dev")
LIMITS = {"pack": 56, "early": 56}
MIB = 2**20
f32, bf16, i32 = jnp.float32, jnp.bfloat16, jnp.int32
SIN = [(-1) ** n * (2 * math.pi) ** (2 * n + 1) / math.factorial(2 * n + 1) for n in range(6)]

NT = (((1,), (1,)), ((), ()))
NN = (((1,), (0,)), ((), ()))


def swap(value, first):
    pairs = [(i, i + 1) for i in range(first, DEVICES - 1, 2)]
    return lax.ppermute(value, AXES, pairs + [(j, i) for i, j in pairs])


def split(value):
    high = value.astype(bf16)
    return high, (value - high.astype(f32)).astype(bf16)


def basis_of(waves, atoms):
    turns = waves[:, 3:4] + waves[:, 0:1] * atoms[0:1, :]
    turns = turns + waves[:, 1:2] * atoms[1:2, :]
    turns = turns + waves[:, 2:3] * atoms[2:3, :]
    turns = turns - jnp.floor(turns + 0.5)
    base = 0.25 - jnp.abs(turns)
    square = base * base
    total = jnp.full_like(square, SIN[5])
    for factor in SIN[4::-1]:
        total = total * square + factor
    return base * total


def cell_hot(cell_row):
    ids = lax.broadcasted_iota(i32, (CELLS, cell_row.shape[1]), 0) + 1
    return jnp.where(ids == cell_row, 1.0, 0.0).astype(bf16)


def poles(basis, charge, hot):
    high, low = split(basis * charge)
    both = lax.dot_general(hot, jnp.concatenate([high, low], axis=0), NT, preferred_element_type=f32)
    return both[:, :LANES] + both[:, LANES:]


def load(sems, *pairs):
    copies = [pltpu.make_async_copy(src, dst, sems.at[i]) for i, (src, dst) in enumerate(pairs)]
    for copy in copies:
        copy.start()
    return copies


def waves_of(freq_ref, phase_ref, flat):
    flat[...] = jnp.zeros_like(flat)
    flat[0:3, 0:COEF] = freq_ref[...] * (0.5 / math.pi)
    flat[3:4, 0:COEF] = phase_ref[...] * (0.5 / math.pi)
    return flat[...].T


def pack_kernel(me_ref, need_hbm, owner_hbm, rows_hbm, cell_hbm, out_ref, need, owner, rows, cell, buf, sems):
    copies = load(
        sems, (owner_hbm, owner), (rows_hbm, rows), (cell_hbm, cell), (need_hbm.at[0, pl.ds(0, 8), :], need)
    )
    out_ref[...] = jnp.zeros_like(out_ref)
    buf[...] = jnp.zeros_like(buf)
    for copy in copies:
        copy.wait()
    me = me_ref[0]
    gap = owner[...] - me

    def count(by):
        return jnp.sum(jnp.where(gap == by, 1.0, 0.0)).astype(i32)

    for at, lo in ((0, 0), (256, STAY - 256)):
        buf[0:4, at : at + 256] = rows[:, lo : lo + 256]
        buf[4:5, at : at + 256] = (cell[:, lo : lo + 256] + 1).astype(f32)
    lane = lax.broadcasted_iota(i32, (8, CAP), 1)
    low2, low1, up1, up2 = count(-2), count(-1), count(1), count(2)
    first = jnp.broadcast_to(need[0:1, :].astype(f32), (LANES, LANES)).T
    out_ref[pl.ds(5, DEVICES, stride=PIECE), :] = first
    ahead = pltpu.roll(buf[:, :256], lax.rem(256 - low2, 256), 1)
    behind = pltpu.roll(buf[:, 256:], lax.rem(up1 + up2, 256), 1)
    last = pltpu.roll(buf[:, 256:], lax.rem(up2, 256), 1)
    for by, count_by, piece in (
        (-2, low2, buf[:, :CAP]), (-1, low1, ahead[:, :CAP]), (1, up1, behind[:, :CAP]), (2, up2, last[:, :CAP])
    ):
        to = me + by

        @pl.when((to >= 0) & (to < DEVICES))
        def _(to=to, count_by=count_by, piece=piece):
            out_ref[pl.ds(to * PIECE, 5), :] = jnp.where(lane < count_by, piece, 0.0)[0:5, :]


def features(atoms_ref, left, right):
    def parts(value, count):
        out = []
        for _ in range(count):
            out.append(value.astype(bf16).astype(f32))
            value = value - out[-1]
        return out

    left[...] = jnp.zeros_like(left)
    right[...] = jnp.zeros_like(right)
    square = None
    for d in range(3):
        value = atoms_ref[d : d + 1, :]
        square = value * value if square is None else square + value * value
        for i, (a, b) in enumerate((a, b) for a in parts(value, 2) for b in parts(value, 2)):
            left[4 * d + i : 4 * d + i + 1, :] = a
            right[4 * d + i : 4 * d + i + 1, :] = -2.0 * b
    ones = jnp.ones_like(square)
    for i, part in enumerate(parts(square, 3)):
        left[12 + i : 13 + i, :] = part
        right[12 + i : 13 + i, :] = ones
    for i, part in enumerate(parts(square + 0.25, 3)):
        left[15 + i : 16 + i, :] = ones
        right[15 + i : 16 + i, :] = part


class Pairs:
    def __init__(self, atoms_ref, pair_ref, left, right, left_cols, right_low, charges, cells, back, start):
        self.atoms, self.pair, self.left_cols, self.right_low = atoms_ref, pair_ref, left_cols, right_low
        self.charges, self.cells, self.back, self.start = charges, cells, back, start
        features(atoms_ref, left, right)
        right_low[...] = right[...].astype(bf16)
        for at in range(0, left_cols.shape[0], LANES):
            cut, rows = slice(start + at, start + at + LANES), slice(at, at + LANES)
            left_cols[rows, :] = left[:, cut].T.astype(bf16)
            charges[rows, :] = jnp.broadcast_to(atoms_ref[3:4, cut], (LANES, LANES)).T
            cells[rows, :] = jnp.broadcast_to(atoms_ref[4:5, cut], (LANES, LANES)).T
        back[...] = jnp.zeros_like(back)

    def block(self, at, lo, both):
        far = lax.dot_general(
            self.left_cols[pl.ds(at, TALL), :], self.right_low[:, pl.ds(lo, WIDE)], NN, preferred_element_type=f32
        )
        its_cell = jnp.concatenate([self.cells[pl.ds(at, TALL), :]] * (WIDE // LANES), axis=1)
        its_charge = jnp.concatenate([self.charges[pl.ds(at, TALL), :]] * (WIDE // LANES), axis=1)
        near = jnp.where(its_cell == self.atoms[4:5, pl.ds(lo, WIDE)], lax.rsqrt(far), 0.0)
        total = jnp.sum((near * its_charge).reshape(TALL // 8, 8, WIDE), axis=0)
        self.pair[:, pl.ds(lo, WIDE)] += jnp.sum(total, axis=0, keepdims=True)
        if both:
            near = near * self.atoms[3:4, pl.ds(lo, WIDE)]
            total = near[:, 0:LANES]
            for k in range(1, WIDE // LANES):
                total = total + near[:, k * LANES : (k + 1) * LANES]
            self.back[pl.ds(at, TALL), :] += total

    def close(self):
        for at in range(0, self.back.shape[0], LANES):
            cut = slice(self.start + at, self.start + at + LANES)
            itself = self.atoms[3:4, cut] * lax.rsqrt(jnp.full((1, LANES), 0.25, f32))
            self.pair[:, cut] += jnp.sum(self.back[at : at + LANES, :].T, axis=0, keepdims=True) - itself


def pair_scratch(slots, rows):
    return [
        ((32, slots), f32), ((32, slots), f32), ((rows, 32), bf16), ((32, slots), bf16),
        *[((rows, LANES), f32)] * 3,
    ]


def sort_rows(keys):
    keys = list(keys)
    step = 1
    while step < LIST:
        gap = step
        while gap >= 1:
            for base in range(gap % step, LIST - gap, 2 * gap):
                for i in range(min(gap, LIST - base - gap)):
                    a, b = base + i, base + i + gap
                    if a // (2 * step) == b // (2 * step):
                        keys[a], keys[b] = jnp.maximum(keys[a], keys[b]), jnp.minimum(keys[a], keys[b])
            gap //= 2
        step *= 2
    return keys


def order(me, entry, kind, own_ref, far_ref, cell_ref, count_ref, lists):
    asked = jnp.maximum(entry - CELLS, 0)
    source = jnp.floor((asked.astype(f32) + 0.5) * (1.0 / SLOT)).astype(i32)
    slot = asked - source * SLOT
    side = jnp.where((source | 1) == (me | 1), FAR_ROWS, FAR_ROWS + EXTRA)
    row = jnp.where(slot < SHORT, source * BLOCK + slot, side + slot - SHORT)
    key = jnp.where(entry < CELLS, -1, kind * REMOTE + row)
    used = jnp.sum(jnp.where(key >= 0, 1, 0), axis=0)
    far = sort_rows(key[l] for l in range(LIST))
    key = jnp.where(entry < CELLS, kind * CELLS + entry, -1)
    own = sort_rows(key[l] for l in range(LIST))
    own = [jnp.where(one < 0, OPS * CELLS, one) for one in own]
    far = [jnp.where(one < 0, OPS * REMOTE, one) for one in far]

    def flat(value):
        return jnp.concatenate([value[r : r + 1, :] for r in range(CELLS // LANES)], axis=1)

    used_row = flat(used).astype(f32)
    rank_key = used_row * CELLS + lax.broadcasted_iota(i32, (1, CELLS), 1).astype(f32)
    rank = jnp.zeros((8, CELLS), f32)
    for lo in range(0, CELLS, LANES):
        column = jnp.broadcast_to(rank_key[:, lo : lo + LANES], (LANES, LANES)).T
        ahead = jnp.where(jnp.concatenate([column] * (CELLS // LANES), axis=1) > rank_key, 1.0, 0.0)
        rank = rank + jnp.sum(ahead.reshape(LANES // 8, 8, CELLS), axis=0)
    rank = jnp.sum(rank, axis=0, keepdims=True).astype(i32)
    place = (rank & 7) * LANES + (rank >> 3)
    moved = jnp.where(lax.broadcasted_iota(i32, (CELLS, CELLS), 0) == place, 1.0, 0.0).astype(bf16)
    lists[...] = jnp.zeros_like(lists)
    for l in range(LIST):
        for at, value in ((l, far[l] >> 8), (16 + l, far[l] & 255), (32 + l, own[l] >> 8), (48 + l, own[l] & 255)):
            for r in range(CELLS // LANES):
                lists[at : at + 1, r * LANES : (r + 1) * LANES] = value[r : r + 1, :].astype(f32)
    ids = lax.broadcasted_iota(i32, (1, CELLS), 1)
    lists[64:65, :] = (ids >> 8).astype(f32)
    lists[65:66, :] = (ids & 255).astype(f32)
    lists[66:67, :] = used_row
    sorted_lists = lax.dot_general(lists[...].astype(bf16), moved, NT, preferred_element_type=f32).astype(i32)
    far_rows = sorted_lists[0:16] * 256 + sorted_lists[16:32]
    own_rows = sorted_lists[32:48] * 256 + sorted_lists[48:64]
    cells = sorted_lists[64:65] * 256 + sorted_lists[65:66]
    for r in range(CELLS // LANES):
        cut = slice(r * LANES, (r + 1) * LANES)
        for l in range(LIST):
            far_ref[l, r : r + 1, :] = far_rows[l : l + 1, cut]
            own_ref[l, r : r + 1, :] = own_rows[l : l + 1, cut]
        cell_ref[r : r + 1, :] = cells[:, cut]
    group = lax.broadcasted_iota(i32, (LANES, LANES), 0)
    number = lax.broadcasted_iota(i32, (LANES, LANES), 1)
    most = jnp.broadcast_to(sorted_lists[66:67, 0:LANES].astype(f32), (LANES, LANES)).T.astype(i32)
    least = jnp.broadcast_to(sorted_lists[66:67, CELLS - LANES : CELLS].astype(f32), (LANES, LANES)).T.astype(i32)
    count_ref[...] = jnp.zeros_like(count_ref)
    remote = jnp.where((most >= number) & ((group & 1) == 0), 1.0, 0.0)
    local = jnp.where((LIST - least <= number) & ((group & 1) == 1), 1.0, 0.0)
    count_ref[0:1, :] = jnp.sum(remote, axis=0, keepdims=True).astype(i32)
    count_ref[1:2, :] = jnp.sum(local, axis=0, keepdims=True).astype(i32)


def early_kernel(
    me_ref, owner_hbm, rows_hbm, cell_hbm, freq_hbm, phase_hbm, entry_hbm, class_hbm,
    atoms_hbm, basis_hbm, pole_hbm, pair_hbm, own_hbm, far_hbm, place_hbm, count_hbm,
    owner, rows, cell, freq, phase, entry, kind, entry3, kind3, lists, flat,
    atoms_ref, basis_ref, pole_ref, pair_ref, own_ref, far_ref, place_ref, count_ref, *rest,
):
    *pair_buffers, sems, out_sems = rest
    copies = load(
        sems, (owner_hbm, owner), (rows_hbm, rows), (cell_hbm, cell), (freq_hbm, freq), (phase_hbm, phase),
        (entry_hbm, entry), (class_hbm, kind),
    )
    atoms_ref[...] = jnp.zeros_like(atoms_ref)
    for copy in copies[:5]:
        copy.wait()
    stays = owner[...] == me_ref[0]
    atoms_ref[0:4, :] = jnp.where(stays, rows[...], 0.0)
    atoms_ref[4:5, :] = jnp.where(stays, (cell[...] + 1).astype(f32), 0.0)
    waves = waves_of(freq, phase, flat)
    width = 512
    for lo in range(0, STAY, width):
        atoms = atoms_ref[:, lo : lo + width]
        basis = basis_of(waves, atoms)
        basis_ref[:, lo : lo + width] = basis
        part = poles(basis, atoms[3:4, :], cell_hot(atoms[4:5, :].astype(i32)))
        pole_ref[...] = part if lo == 0 else pole_ref[...] + part
    outs = load(out_sems, (atoms_ref, atoms_hbm), (basis_ref, basis_hbm), (pole_ref, pole_hbm))
    for copy in copies[5:]:
        copy.wait()
    for l in range(LIST):
        for r in range(CELLS // LANES):
            entry3[l, r : r + 1, :] = entry[l : l + 1, r * LANES : (r + 1) * LANES]
            kind3[l, r : r + 1, :] = kind[l : l + 1, r * LANES : (r + 1) * LANES]
    order(me_ref[0], entry3[...], kind3[...], own_ref, far_ref, place_ref, count_ref, lists)
    more = [(own_ref, own_hbm), (far_ref, far_hbm), (place_ref, place_hbm), (count_ref, count_hbm)]
    outs += load(out_sems.at[pl.ds(3, 4)], *more)

    pair_ref[...] = jnp.zeros_like(pair_ref)
    pairs = Pairs(atoms_ref, pair_ref, *pair_buffers, 0)
    blocks, strips = STAY // WIDE, WIDE // TALL

    def strip(c, reach):
        at, mine = pl.multiple_of(c * TALL, TALL), c // strips
        pairs.block(at, pl.multiple_of(mine * WIDE, WIDE), False)
        for by in range(1, reach + 1):
            pairs.block(at, pl.multiple_of(lax.rem(mine + by, blocks) * WIDE, WIDE), True)

    def wide_strip(c, _):
        strip(c, 2)
        return 0

    def short_strip(c, _):
        strip(c, 1)
        return 0

    half = blocks * strips // 2
    lax.fori_loop(0, half, wide_strip, 0)
    lax.fori_loop(half, 2 * half, short_strip, 0)
    pairs.close()
    last = pltpu.make_async_copy(pair_ref, pair_hbm, out_sems.at[7])
    last.start()
    for copy in outs:
        copy.wait()
    last.wait()


def merge_kernel(
    me_ref, got_ref, freq_hbm, phase_hbm, stay_hbm, up_hbm,
    send_ref, mate_ref, other_ref, pole_hbm, basis_hbm, atoms_hbm,
    freq, phase, stay, up, flat, atoms_ref, basis_ref, pole_ref, ring, turned, ids, first_ref, sems, out_sems,
):
    copies = load(sems, (freq_hbm, freq), (phase_hbm, phase), (stay_hbm, stay), (up_hbm, up))
    me = me_ref[0]
    row = lax.broadcasted_iota(i32, (DEVICES, LANES), 0)
    lane = lax.broadcasted_iota(i32, (DEVICES, LANES), 1)
    asked = jnp.where(row == lane, got_ref[pl.ds(5, DEVICES, stride=PIECE), :], 0.0)
    ids[...] = jnp.maximum(jnp.sum(asked, axis=0, keepdims=True).astype(i32), 0)
    to_scalars = pltpu.make_async_copy(ids, first_ref, sems.at[4])
    to_scalars.start()
    atoms_ref[...] = jnp.zeros_like(atoms_ref)
    for at, by in enumerate((-2, -1, 1, 2)):
        source = me - by

        @pl.when((source >= 0) & (source < DEVICES))
        def _(at=at, source=source):
            atoms_ref[0:5, at * CAP : (at + 1) * CAP] = got_ref[pl.ds(source * PIECE, 5), :]

    copies[0].wait()
    copies[1].wait()
    atoms = atoms_ref[...]
    basis = basis_of(waves_of(freq, phase, flat), atoms)
    basis_ref[...] = basis
    both = poles(basis, atoms[3:4, :], cell_hot(atoms[4:5, :].astype(i32)))
    copies[2].wait()
    pole = stay[...] + both
    pole_ref[...] = pole
    outs = load(out_sems, (atoms_ref, atoms_hbm), (basis_ref, basis_hbm), (pole_ref, pole_hbm))
    ring[0:CELLS, :] = pole
    ring[CELLS:WRAP, :] = pole[0 : WRAP - CELLS, :]
    grouped = jnp.sum(pole.reshape(CELLS // 8, 8, LANES), axis=0)
    copies[3].wait()
    raised = up[...].reshape(COEF, OPS, COEF) * grouped[None, :, :COEF]
    turned[...] = jnp.zeros_like(turned)
    turned[0:COEF, 0:COEF] = jnp.sum(raised, axis=1)
    coarse = jnp.sum(turned[...].T, axis=0, keepdims=True)
    to_scalars.wait()

    def one(t, _):
        send_ref[pl.ds(t * BLOCK, SHORT), :] = ring[pl.ds(first_ref[0, t], SHORT), :]
        send_ref[pl.ds(t * BLOCK + SHORT, 1), :] = coarse
        return 0

    lax.fori_loop(0, DEVICES, one, 0, unroll=8)
    odd = lax.rem(me, 2)
    mate = me + 1 - 2 * odd
    other = jnp.clip(me - 1 + 2 * odd, 0, DEVICES - 1)
    mate_ref[...] = ring[pl.ds(first_ref[0, mate] + SHORT, EXTRA), :]
    other_ref[...] = ring[pl.ds(first_ref[0, other] + SHORT, EXTRA), :]
    for copy in outs:
        copy.wait()


def load_ops(ops_ref, both):
    both[...] = jnp.zeros_like(both)
    for o in range(OPS):
        high, low = split(ops_ref[pl.ds(o, COEF, stride=OPS), :])
        for at, part in enumerate((high, high, low)):
            both[o * LANES : o * LANES + COEF, at * LANES : at * LANES + COEF] = part


def premultiply(rows, both, table, at, pitch):
    high, low = split(rows)
    parts = jnp.concatenate([high, low, high], axis=1)
    for o in range(0, OPS, 2):
        pair = both[o * LANES : (o + 2) * LANES, :]
        out = lax.dot_general(parts, pair, NT, preferred_element_type=f32)
        for k in range(2):
            table[pl.ds((o + k) * pitch + at, rows.shape[0]), :] = out[:, k * LANES : (k + 1) * LANES]


def index_of(index_ref, l, r, g):
    return index_ref.at[pl.ds(l * CELLS + r * LANES, LANES)][g]


def row_sums(index_ref, table, count, first, last, start, store):
    def pair(p, _):
        for g in (2 * p, 2 * p + 1):
            for r in range(8):
                total = None if start is None else start(r, g)
                for l in range(count):
                    row = table[pl.ds(index_of(index_ref, l, r, g), 1), :]
                    total = row if total is None else total + row
                store(r, g, jnp.zeros((1, LANES), f32) if total is None else total)
        return 0

    lax.fori_loop(first, last, pair, 0)


def cross_kernel(stay_hbm, new_hbm, stay_pair_hbm, pair_hbm, atoms_ref, pair_ref, *rest):
    *pair_buffers, sems, out_sems = rest
    copies = load(
        sems, (stay_hbm, atoms_ref.at[:, pl.ds(0, STAY)]), (new_hbm, atoms_ref.at[:, pl.ds(STAY, ARRIVE)]),
        (stay_pair_hbm, pair_ref.at[:, pl.ds(0, STAY)]),
    )
    pair_ref[:, STAY:] = jnp.zeros((1, ARRIVE), f32)
    for copy in copies:
        copy.wait()
    pairs = Pairs(atoms_ref, pair_ref, *pair_buffers, STAY)

    def strip(c, _):
        at = pl.multiple_of(c * TALL, TALL)
        pairs.block(at, STAY, False)
        for lo in range(0, STAY, WIDE):
            pairs.block(at, lo, True)
        return 0

    lax.fori_loop(0, ARRIVE // TALL, strip, 0)
    pairs.close()
    (out,) = load(out_sems, (pair_ref, pair_hbm))
    out.wait()


def mid_kernel(own_hbm, count_ref, pole_hbm, ops_hbm, sum_hbm, own_ref, table, both, ops, pole, sum_ref, sems):
    copies = load(sems, (ops_hbm, ops), (pole_hbm, pole), (own_hbm, own_ref))
    table[OPS * CELLS :, :] = jnp.zeros((8, LANES), f32)
    copies[0].wait()
    load_ops(ops, both)
    copies[1].wait()
    width = CELLS // 2
    for lo in range(0, CELLS, width):
        premultiply(pole[lo : lo + width, :], both, table, lo, CELLS)
    copies[2].wait()

    def store(r, g, total):
        sum_ref[pl.ds(r * LANES + g, 1), :] = total

    for n in range(LIST + 1):
        first = 0 if n == 0 else count_ref[LANES + n - 1]
        row_sums(own_ref, table, n, first, count_ref[LANES + n], None, store)
    out = pltpu.make_async_copy(sum_ref, sum_hbm, sems.at[3])
    out.start()
    out.wait()


def last_kernel(
    me_ref, index_hbm, count_ref, place_ref, far_ref, near_ref, next_ref, ops_hbm, sum_hbm, inner_hbm, outer_hbm,
    down_hbm, stay_hbm, new_hbm, stay_basis_hbm, new_basis_hbm, pair_hbm, local_ref, pot_ref,
    index_ref, table, both, sums_ref, rows, coarse, ops, inner, outer, down, atoms_ref, basis_ref, pair, sems,
):
    copies = load(
        sems, (ops_hbm, ops), (sum_hbm, sums_ref), (inner_hbm, inner), (outer_hbm, outer), (down_hbm, down),
        (stay_hbm, atoms_ref.at[:, pl.ds(0, STAY)]), (new_hbm, atoms_ref.at[:, pl.ds(STAY, ARRIVE)]),
        (stay_basis_hbm, basis_ref.at[:, pl.ds(0, STAY)]), (new_basis_hbm, basis_ref.at[:, pl.ds(STAY, ARRIVE)]),
        (pair_hbm, pair), (index_hbm, index_ref),
    )
    table[OPS * REMOTE :, :] = jnp.zeros((8, LANES), f32)
    copies[0].wait()
    load_ops(ops, both)
    width = FAR_ROWS // 4
    for lo in range(0, FAR_ROWS, width):
        premultiply(far_ref[lo : lo + width, :], both, table, lo, REMOTE)
    premultiply(near_ref[...], both, table, FAR_ROWS, REMOTE)
    premultiply(next_ref[...], both, table, FAR_ROWS + EXTRA, REMOTE)

    coarse[...] = far_ref[pl.ds(SHORT, DEVICES, stride=BLOCK), :]
    me = me_ref[0]
    group, member = me // MEMBERS, lax.rem(me, MEMBERS)
    who = lax.broadcasted_iota(i32, (40, DEVICES), 1)
    which = lax.broadcasted_iota(i32, (40, DEVICES), 0)
    its_group, its_member = who // MEMBERS, lax.rem(who, MEMBERS)
    near = (its_group == group) & (jnp.abs(its_member - member) - 1 == which) & (which < MEMBERS)
    away = (jnp.abs(its_group - group) - 1 == which - MEMBERS) & (which >= MEMBERS)
    chosen = jnp.where(near | away, 1.0, 0.0)
    sums = lax.dot_general(chosen, coarse[...], NN, precision=lax.Precision.HIGHEST, preferred_element_type=f32)
    for copy in copies[1:5]:
        copy.wait()
    field = jnp.sum(inner[...] * sums[None, 0 : MEMBERS - 1, 0:COEF], axis=1)
    for o in range(GROUPS - 1):
        field = field + outer[o] * sums[MEMBERS + o : MEMBERS + o + 1, 0:COEF]
    field = jnp.broadcast_to(jnp.sum(field, axis=1, keepdims=True), (COEF, LANES))
    child = lax.rem(lax.broadcasted_iota(i32, (COEF, LANES), 1), OPS)
    pattern = jnp.zeros((COEF, LANES), f32)
    for o in range(OPS):
        one = lax.dot_general(
            down[pl.ds(o, COEF, stride=OPS), :], field, NN,
            precision=lax.Precision.HIGHEST, preferred_element_type=f32,
        )
        pattern = jnp.where(child == o, one, pattern)

    def store(r, g, total):
        rows[pl.ds(place_ref.at[pl.ds(r * LANES, LANES)][g], 1), :] = total

    copies[10].wait()
    for n in range(LIST, -1, -1):
        row_sums(
            index_ref, table, n, count_ref[n + 1], count_ref[n], lambda r, g: sums_ref[pl.ds(r * LANES + g, 1), :], store
        )

    for lo in range(0, CELLS, LANES):
        local_ref[:, lo : lo + LANES] = rows[lo : lo + LANES, :].T[0:COEF, :] + pattern
    local = local_ref[...]
    high, rest = split(local)
    high = jnp.concatenate([high, jnp.zeros((LANES - COEF, CELLS), bf16)], axis=0)
    rest = jnp.concatenate([rest, jnp.zeros((LANES - COEF, CELLS), bf16)], axis=0)
    stacked = jnp.concatenate([high, rest], axis=0)
    for copy in copies[5:10]:
        copy.wait()
    wide = 512
    for lo in range(0, SLOTS, wide):
        cells, basis = atoms_ref[4:5, lo : lo + wide], basis_ref[:, lo : lo + wide]
        at = lax.dot_general(stacked, cell_hot(cells.astype(i32)), NN, preferred_element_type=f32)
        read = jnp.sum((at[:LANES] + at[LANES:]) * basis, axis=0, keepdims=True)
        read = read * COEF**-0.5 + pair[:, lo : lo + wide]
        for at in range(0, wide, LANES):
            i = (lo + at) // LANES
            pot_ref[i : i + 1, :] = read[:, at : at + LANES]


VM = pl.BlockSpec(memory_space=pltpu.VMEM)
SM = pl.BlockSpec(memory_space=pltpu.SMEM)
HB = pl.BlockSpec(memory_space=pltpu.HBM)


def call(kernel, name, ins, outs, scratch, copies, *operands):
    cost = pl.CostEstimate(flops=1000, bytes_accessed=1000, transcendentals=0)
    return pl.pallas_call(
        kernel,
        name=name,
        in_specs=ins,
        out_specs=[spec for spec, _, _ in outs],
        out_shape=[jax.ShapeDtypeStruct(shape, kind) for _, shape, kind in outs],
        scratch_shapes=[pltpu.VMEM(shape, kind) if isinstance(shape, tuple) else shape for shape, kind in scratch]
        + [pltpu.SemaphoreType.DMA((count,)) for count in copies],
        cost_estimate=cost,
        compiler_params=pltpu.CompilerParams(vmem_limit_bytes=LIMITS.get(name, 52) * MIB),
    )(*operands)


def on_device(
    atom_rows,
    atom_owner,
    atom_cell,
    need_cells,
    list_entry,
    list_class,
    basis_freq,
    basis_phase,
    near_ops,
    up_ops,
    far_in,
    far_out,
    down_ops,
):
    me = (lax.axis_index("group") * MEMBERS + lax.axis_index("dev")).reshape(1).astype(i32)
    freq, phase = basis_freq.T, basis_phase.reshape(1, COEF)
    waves = [((3, COEF), f32), ((1, COEF), f32)]
    owner_row, cell_row = atom_owner.reshape(1, STAY), atom_cell.reshape(1, STAY)
    by_row = [ops.transpose(1, 0, 2).reshape(COEF * OPS, COEF) for ops in (near_ops, up_ops, down_ops)]
    ops_shape = ((COEF * OPS, COEF), f32)
    mine = [((1, STAY), i32), ((4, STAY), f32), ((1, STAY), i32)]

    (outbound,) = call(
        pack_kernel, "pack", [SM, HB, HB, HB, HB], [(VM, (DEVICES * PIECE, LANES), f32)],
        [((8, LANES), i32), ((STAY // LANES, LANES), i32), *mine[1:], ((8, 512), f32)], [4],
        me, need_cells.transpose(0, 2, 1), atom_owner.reshape(STAY // LANES, LANES), atom_rows, cell_row,
    )
    got = lax.all_to_all(outbound.reshape(DEVICES, 1, PIECE * LANES), AXES, split_axis=0, concat_axis=0, tiled=True)
    got = got.reshape(DEVICES * PIECE, LANES)

    shape3, tile = (LIST, CELLS // LANES, LANES), (CELLS // LANES, LANES)
    early_outs = [
        ((8, STAY), f32), ((LANES, STAY), f32), ((CELLS, LANES), f32), ((1, STAY), f32),
        (shape3, i32), (shape3, i32), (tile, i32), (tile, i32),
    ]
    stay_atoms, stay_basis, stay_pole, stay_pair, own_index, far_index, place, counts = call(
        early_kernel, "early", [SM] + [HB] * 7, [(HB, *out) for out in early_outs],
        [*mine, *waves, *[((LIST, CELLS), i32)] * 2, *[(shape3, i32)] * 2, ((80, CELLS), f32), ((8, LANES), f32), *early_outs,
         *pair_scratch(STAY, STAY)], [7, 8],
        me, owner_row, atom_rows, cell_row, freq, phase, list_entry, list_class,
    )
    own_index, far_index, place, counts = (one.reshape(-1) for one in (own_index, far_index, place, counts))
    merge_outs = [((CELLS, LANES), f32), ((LANES, ARRIVE), f32), ((8, ARRIVE), f32)]
    send, mate_rows, other_rows, pole, new_basis, new_atoms = call(
        merge_kernel, "merge", [SM, VM] + [HB] * 4,
        [(VM, (FAR_ROWS, LANES), f32), (VM, (EXTRA, LANES), f32), (VM, (EXTRA, LANES), f32), *[(HB, *out) for out in merge_outs]],
        [*waves, ((CELLS, LANES), f32), ops_shape, ((8, LANES), f32), *merge_outs[::-1],
         ((WRAP, LANES), f32), ((LANES, LANES), f32), ((1, LANES), i32), (pltpu.SMEM((1, LANES), i32), None)],
        [5, 3],
        me, got, freq, phase, stay_pole, by_row[1],
    )
    far_rows = lax.all_to_all(send.reshape(DEVICES, 1, BLOCK * LANES), AXES, split_axis=0, concat_axis=0, tiled=True)
    far_rows = far_rows.reshape(FAR_ROWS, LANES)
    near_rows, next_rows = swap(mate_rows, 0), swap(other_rows, 1)
    (pair,) = call(
        cross_kernel, "cross", [HB] * 3, [(HB, (1, SLOTS), f32)],
        [((8, SLOTS), f32), ((1, SLOTS), f32), *pair_scratch(SLOTS, ARRIVE)], [3, 1],
        stay_atoms, new_atoms, stay_pair,
    )
    index_scratch = (pltpu.SMEM((LIST * CELLS,), i32), None)
    (own_sum,) = call(
        mid_kernel, "mid", [HB, SM, HB, HB], [(HB, (CELLS, LANES), f32)],
        [index_scratch, ((OPS * CELLS + 8, LANES), f32), ((OPS * LANES, 3 * LANES), bf16), ops_shape, *[((CELLS, LANES), f32)] * 2],
        [4],
        own_index, counts, pole, by_row[0],
    )
    local, pot = call(
        last_kernel, "last", [SM, HB, SM, SM] + [VM] * 3 + [HB] * 10, [(VM, (COEF, CELLS), f32), (VM, (SLOTS // LANES, LANES), f32)],
        [index_scratch, ((OPS * REMOTE + 8, LANES), f32), ((OPS * LANES, 3 * LANES), bf16), *[((CELLS, LANES), f32)] * 2, ((DEVICES, LANES), f32),
         ops_shape, ((COEF, MEMBERS - 1, COEF), f32), ((GROUPS - 1, COEF, COEF), f32), ops_shape, ((8, SLOTS), f32),
         ((LANES, SLOTS), f32), ((1, SLOTS), f32)],
        [11],
        me, far_index, counts, place, far_rows, near_rows, next_rows, by_row[0], own_sum,
        far_in.transpose(1, 0, 2), far_out, by_row[2], stay_atoms, new_atoms, stay_basis, new_basis, pair,
    )
    return local, pot.reshape(SLOTS)


def solution(mesh):
    in_specs = (
        P(None, AXES),
        P(AXES),
        P(AXES),
        P(AXES, None, None),
        P(None, AXES),
        P(None, AXES),
        P(),
        P(),
        P(),
        P(),
        P(),
        P(),
        P(),
    )
    out_specs = (P(None, AXES), P(AXES))
    return jax.shard_map(on_device, mesh=mesh, in_specs=in_specs, out_specs=out_specs, check_vma=False)
```

```python
import math

import jax
import jax.numpy as jnp
from jax import lax
from jax.experimental import pallas as pl
from jax.experimental.pallas import tpu as pltpu
from jax.sharding import PartitionSpec as P

COEF = 121
LANES = 128
CELLS = 1024
STAY = 2048
CAP = 128
ARRIVE = 4 * CAP
SLOTS = STAY + ARRIVE
LIST = 16
OPS = 8
SLOT = 72
SHORT = 18
BLOCK = SHORT + 1
DEVICES = 128
MEMBERS = 32
GROUPS = 4
PIECE = 6
EXTRA = 56
FAR_ROWS = DEVICES * BLOCK
REMOTE = FAR_ROWS + 2 * EXTRA
WRAP = CELLS + 80
TALL, WIDE = 256, 512
AXES = ("group", "dev")
LIMITS = {"pack": 56, "early": 56}
MIB = 2**20
f32, bf16, i32 = jnp.float32, jnp.bfloat16, jnp.int32
SIN = [(-1) ** n * (2 * math.pi) ** (2 * n + 1) / math.factorial(2 * n + 1) for n in range(6)]

NT = (((1,), (1,)), ((), ()))
NN = (((1,), (0,)), ((), ()))


def swap(value, first):
    pairs = [(i, i + 1) for i in range(first, DEVICES - 1, 2)]
    return lax.ppermute(value, AXES, pairs + [(j, i) for i, j in pairs])


def split(value):
    high = value.astype(bf16)
    return high, (value - high.astype(f32)).astype(bf16)


def basis_of(waves, atoms):
    turns = waves[:, 3:4] + waves[:, 0:1] * atoms[0:1, :]
    turns = turns + waves[:, 1:2] * atoms[1:2, :]
    turns = turns + waves[:, 2:3] * atoms[2:3, :]
    turns = turns - jnp.floor(turns + 0.5)
    base = 0.25 - jnp.abs(turns)
    square = base * base
    total = jnp.full_like(square, SIN[5])
    for factor in SIN[4::-1]:
        total = total * square + factor
    return base * total


def cell_hot(cell_row):
    ids = lax.broadcasted_iota(i32, (CELLS, cell_row.shape[1]), 0) + 1
    return jnp.where(ids == cell_row, 1.0, 0.0).astype(bf16)


def poles(basis, charge, hot):
    high, low = split(basis * charge)
    both = lax.dot_general(hot, jnp.concatenate([high, low], axis=0), NT, preferred_element_type=f32)
    return both[:, :LANES] + both[:, LANES:]


def load(sems, *pairs):
    copies = [pltpu.make_async_copy(src, dst, sems.at[i]) for i, (src, dst) in enumerate(pairs)]
    for copy in copies:
        copy.start()
    return copies


def waves_of(freq_ref, phase_ref, flat):
    flat[...] = jnp.zeros_like(flat)
    flat[0:3, 0:COEF] = freq_ref[...] * (0.5 / math.pi)
    flat[3:4, 0:COEF] = phase_ref[...] * (0.5 / math.pi)
    return flat[...].T


def pack_kernel(me_ref, need_hbm, owner_hbm, rows_hbm, cell_hbm, out_ref, need, owner, rows, cell, buf, sems):
    copies = load(
        sems, (owner_hbm, owner), (rows_hbm, rows), (cell_hbm, cell), (need_hbm.at[0, pl.ds(0, 8), :], need)
    )
    out_ref[...] = jnp.zeros_like(out_ref)
    buf[...] = jnp.zeros_like(buf)
    for copy in copies:
        copy.wait()
    me = me_ref[0]
    gap = owner[...] - me

    def count(by):
        return jnp.sum(jnp.where(gap == by, 1.0, 0.0)).astype(i32)

    for at, lo in ((0, 0), (256, STAY - 256)):
        buf[0:4, at : at + 256] = rows[:, lo : lo + 256]
        buf[4:5, at : at + 256] = (cell[:, lo : lo + 256] + 1).astype(f32)
    lane = lax.broadcasted_iota(i32, (8, CAP), 1)
    low2, low1, up1, up2 = count(-2), count(-1), count(1), count(2)
    first = jnp.broadcast_to(need[0:1, :].astype(f32), (LANES, LANES)).T
    out_ref[pl.ds(5, DEVICES, stride=PIECE), :] = first
    ahead = pltpu.roll(buf[:, :256], lax.rem(256 - low2, 256), 1)
    behind = pltpu.roll(buf[:, 256:], lax.rem(up1 + up2, 256), 1)
    last = pltpu.roll(buf[:, 256:], lax.rem(up2, 256), 1)
    for by, count_by, piece in (
        (-2, low2, buf[:, :CAP]), (-1, low1, ahead[:, :CAP]), (1, up1, behind[:, :CAP]), (2, up2, last[:, :CAP])
    ):
        to = me + by

        @pl.when((to >= 0) & (to < DEVICES))
        def _(to=to, count_by=count_by, piece=piece):
            out_ref[pl.ds(to * PIECE, 5), :] = jnp.where(lane < count_by, piece, 0.0)[0:5, :]


def features(atoms_ref, left, right):
    def parts(value, count):
        out = []
        for _ in range(count):
            out.append(value.astype(bf16).astype(f32))
            value = value - out[-1]
        return out

    left[...] = jnp.zeros_like(left)
    right[...] = jnp.zeros_like(right)
    square = None
    for d in range(3):
        value = atoms_ref[d : d + 1, :]
        square = value * value if square is None else square + value * value
        for i, (a, b) in enumerate((a, b) for a in parts(value, 2) for b in parts(value, 2)):
            left[4 * d + i : 4 * d + i + 1, :] = a
            right[4 * d + i : 4 * d + i + 1, :] = -2.0 * b
    ones = jnp.ones_like(square)
    for i, part in enumerate(parts(square, 3)):
        left[12 + i : 13 + i, :] = part
        right[12 + i : 13 + i, :] = ones
    for i, part in enumerate(parts(square + 0.25, 3)):
        left[15 + i : 16 + i, :] = ones
        right[15 + i : 16 + i, :] = part


class Pairs:
    def __init__(self, atoms_ref, pair_ref, left, right, left_cols, right_low, charges, cells, back, start):
        self.atoms, self.pair, self.left_cols, self.right_low = atoms_ref, pair_ref, left_cols, right_low
        self.charges, self.cells, self.back, self.start = charges, cells, back, start
        features(atoms_ref, left, right)
        right_low[...] = right[...].astype(bf16)
        for at in range(0, left_cols.shape[0], LANES):
            cut, rows = slice(start + at, start + at + LANES), slice(at, at + LANES)
            left_cols[rows, :] = left[:, cut].T.astype(bf16)
            charges[rows, :] = jnp.broadcast_to(atoms_ref[3:4, cut], (LANES, LANES)).T
            cells[rows, :] = jnp.broadcast_to(atoms_ref[4:5, cut], (LANES, LANES)).T
        back[...] = jnp.zeros_like(back)

    def block(self, at, lo, both):
        far = lax.dot_general(
            self.left_cols[pl.ds(at, TALL), :], self.right_low[:, pl.ds(lo, WIDE)], NN, preferred_element_type=f32
        )
        its_cell = jnp.concatenate([self.cells[pl.ds(at, TALL), :]] * (WIDE // LANES), axis=1)
        its_charge = jnp.concatenate([self.charges[pl.ds(at, TALL), :]] * (WIDE // LANES), axis=1)
        near = jnp.where(its_cell == self.atoms[4:5, pl.ds(lo, WIDE)], lax.rsqrt(far), 0.0)
        total = jnp.sum((near * its_charge).reshape(TALL // 8, 8, WIDE), axis=0)
        self.pair[:, pl.ds(lo, WIDE)] += jnp.sum(total, axis=0, keepdims=True)
        if both:
            near = near * self.atoms[3:4, pl.ds(lo, WIDE)]
            total = near[:, 0:LANES]
            for k in range(1, WIDE // LANES):
                total = total + near[:, k * LANES : (k + 1) * LANES]
            self.back[pl.ds(at, TALL), :] += total

    def close(self):
        for at in range(0, self.back.shape[0], LANES):
            cut = slice(self.start + at, self.start + at + LANES)
            itself = self.atoms[3:4, cut] * lax.rsqrt(jnp.full((1, LANES), 0.25, f32))
            self.pair[:, cut] += jnp.sum(self.back[at : at + LANES, :].T, axis=0, keepdims=True) - itself


def pair_scratch(slots, rows):
    return [
        ((32, slots), f32), ((32, slots), f32), ((rows, 32), bf16), ((32, slots), bf16),
        *[((rows, LANES), f32)] * 3,
    ]


def sort_rows(keys):
    keys = list(keys)
    step = 1
    while step < LIST:
        gap = step
        while gap >= 1:
            for base in range(gap % step, LIST - gap, 2 * gap):
                for i in range(min(gap, LIST - base - gap)):
                    a, b = base + i, base + i + gap
                    if a // (2 * step) == b // (2 * step):
                        keys[a], keys[b] = jnp.maximum(keys[a], keys[b]), jnp.minimum(keys[a], keys[b])
            gap //= 2
        step *= 2
    return keys


def order(me, entry, kind, own_ref, far_ref, cell_ref, count_ref, lists):
    asked = jnp.maximum(entry - CELLS, 0)
    source = jnp.floor((asked.astype(f32) + 0.5) * (1.0 / SLOT)).astype(i32)
    slot = asked - source * SLOT
    side = jnp.where((source | 1) == (me | 1), FAR_ROWS, FAR_ROWS + EXTRA)
    row = jnp.where(slot < SHORT, source * BLOCK + slot, side + slot - SHORT)
    key = jnp.where(entry < CELLS, -1, kind * REMOTE + row)
    used = jnp.sum(jnp.where(key >= 0, 1, 0), axis=0)
    far = sort_rows(key[l] for l in range(LIST))
    key = jnp.where(entry < CELLS, kind * CELLS + entry, -1)
    own = sort_rows(key[l] for l in range(LIST))
    own = [jnp.where(one < 0, OPS * CELLS, one) for one in own]
    far = [jnp.where(one < 0, OPS * REMOTE, one) for one in far]

    def flat(value):
        return jnp.concatenate([value[r : r + 1, :] for r in range(CELLS // LANES)], axis=1)

    used_row = flat(used).astype(f32)
    rank_key = used_row * CELLS + lax.broadcasted_iota(i32, (1, CELLS), 1).astype(f32)
    rank = jnp.zeros((8, CELLS), f32)
    for lo in range(0, CELLS, LANES):
        column = jnp.broadcast_to(rank_key[:, lo : lo + LANES], (LANES, LANES)).T
        ahead = jnp.where(jnp.concatenate([column] * (CELLS // LANES), axis=1) > rank_key, 1.0, 0.0)
        rank = rank + jnp.sum(ahead.reshape(LANES // 8, 8, CELLS), axis=0)
    rank = jnp.sum(rank, axis=0, keepdims=True).astype(i32)
    place = (rank & 7) * LANES + (rank >> 3)
    moved = jnp.where(lax.broadcasted_iota(i32, (CELLS, CELLS), 0) == place, 1.0, 0.0).astype(bf16)
    lists[...] = jnp.zeros_like(lists)
    for l in range(LIST):
        for at, value in ((l, far[l] >> 8), (16 + l, far[l] & 255), (32 + l, own[l] >> 8), (48 + l, own[l] & 255)):
            for r in range(CELLS // LANES):
                lists[at : at + 1, r * LANES : (r + 1) * LANES] = value[r : r + 1, :].astype(f32)
    ids = lax.broadcasted_iota(i32, (1, CELLS), 1)
    lists[64:65, :] = (ids >> 8).astype(f32)
    lists[65:66, :] = (ids & 255).astype(f32)
    lists[66:67, :] = used_row
    sorted_lists = lax.dot_general(lists[...].astype(bf16), moved, NT, preferred_element_type=f32).astype(i32)
    far_rows = sorted_lists[0:16] * 256 + sorted_lists[16:32]
    own_rows = sorted_lists[32:48] * 256 + sorted_lists[48:64]
    cells = sorted_lists[64:65] * 256 + sorted_lists[65:66]
    for r in range(CELLS // LANES):
        cut = slice(r * LANES, (r + 1) * LANES)
        for l in range(LIST):
            far_ref[l, r : r + 1, :] = far_rows[l : l + 1, cut]
            own_ref[l, r : r + 1, :] = own_rows[l : l + 1, cut]
        cell_ref[r : r + 1, :] = cells[:, cut]
    group = lax.broadcasted_iota(i32, (LANES, LANES), 0)
    number = lax.broadcasted_iota(i32, (LANES, LANES), 1)
    most = jnp.broadcast_to(sorted_lists[66:67, 0:LANES].astype(f32), (LANES, LANES)).T.astype(i32)
    least = jnp.broadcast_to(sorted_lists[66:67, CELLS - LANES : CELLS].astype(f32), (LANES, LANES)).T.astype(i32)
    count_ref[...] = jnp.zeros_like(count_ref)
    remote = jnp.where((most >= number) & ((group & 1) == 0), 1.0, 0.0)
    local = jnp.where((LIST - least <= number) & ((group & 1) == 1), 1.0, 0.0)
    count_ref[0:1, :] = jnp.sum(remote, axis=0, keepdims=True).astype(i32)
    count_ref[1:2, :] = jnp.sum(local, axis=0, keepdims=True).astype(i32)


def early_kernel(
    me_ref, owner_hbm, rows_hbm, cell_hbm, freq_hbm, phase_hbm, entry_hbm, class_hbm,
    atoms_hbm, basis_hbm, pole_hbm, pair_hbm, own_hbm, far_hbm, place_hbm, count_hbm,
    owner, rows, cell, freq, phase, entry, kind, entry3, kind3, lists, flat,
    atoms_ref, basis_ref, pole_ref, pair_ref, own_ref, far_ref, place_ref, count_ref, *rest,
):
    *pair_buffers, sems, out_sems = rest
    copies = load(
        sems, (owner_hbm, owner), (rows_hbm, rows), (cell_hbm, cell), (freq_hbm, freq), (phase_hbm, phase),
        (entry_hbm, entry), (class_hbm, kind),
    )
    atoms_ref[...] = jnp.zeros_like(atoms_ref)
    for copy in copies[:5]:
        copy.wait()
    stays = owner[...] == me_ref[0]
    atoms_ref[0:4, :] = jnp.where(stays, rows[...], 0.0)
    atoms_ref[4:5, :] = jnp.where(stays, (cell[...] + 1).astype(f32), 0.0)
    waves = waves_of(freq, phase, flat)
    width = 512
    for lo in range(0, STAY, width):
        atoms = atoms_ref[:, lo : lo + width]
        basis = basis_of(waves, atoms)
        basis_ref[:, lo : lo + width] = basis
        part = poles(basis, atoms[3:4, :], cell_hot(atoms[4:5, :].astype(i32)))
        pole_ref[...] = part if lo == 0 else pole_ref[...] + part
    outs = load(out_sems, (atoms_ref, atoms_hbm), (basis_ref, basis_hbm), (pole_ref, pole_hbm))
    for copy in copies[5:]:
        copy.wait()
    for l in range(LIST):
        for r in range(CELLS // LANES):
            entry3[l, r : r + 1, :] = entry[l : l + 1, r * LANES : (r + 1) * LANES]
            kind3[l, r : r + 1, :] = kind[l : l + 1, r * LANES : (r + 1) * LANES]
    order(me_ref[0], entry3[...], kind3[...], own_ref, far_ref, place_ref, count_ref, lists)
    more = [(own_ref, own_hbm), (far_ref, far_hbm), (place_ref, place_hbm), (count_ref, count_hbm)]
    outs += load(out_sems.at[pl.ds(3, 4)], *more)

    pair_ref[...] = jnp.zeros_like(pair_ref)
    pairs = Pairs(atoms_ref, pair_ref, *pair_buffers, 0)
    blocks, strips = STAY // WIDE, WIDE // TALL

    def strip(c, reach):
        at, mine = pl.multiple_of(c * TALL, TALL), c // strips
        pairs.block(at, pl.multiple_of(mine * WIDE, WIDE), False)
        for by in range(1, reach + 1):
            pairs.block(at, pl.multiple_of(lax.rem(mine + by, blocks) * WIDE, WIDE), True)

    def wide_strip(c, _):
        strip(c, 2)
        return 0

    def short_strip(c, _):
        strip(c, 1)
        return 0

    half = blocks * strips // 2
    lax.fori_loop(0, half, wide_strip, 0)
    lax.fori_loop(half, 2 * half, short_strip, 0)
    pairs.close()
    last = pltpu.make_async_copy(pair_ref, pair_hbm, out_sems.at[7])
    last.start()
    for copy in outs:
        copy.wait()
    last.wait()


def merge_kernel(
    me_ref, got_ref, freq_hbm, phase_hbm, stay_hbm, up_hbm,
    send_ref, mate_ref, other_ref, pole_hbm, basis_hbm, atoms_hbm,
    freq, phase, stay, up, flat, atoms_ref, basis_ref, pole_ref, ring, turned, ids, first_ref, sems, out_sems,
):
    copies = load(sems, (freq_hbm, freq), (phase_hbm, phase), (stay_hbm, stay), (up_hbm, up))
    me = me_ref[0]
    row = lax.broadcasted_iota(i32, (DEVICES, LANES), 0)
    lane = lax.broadcasted_iota(i32, (DEVICES, LANES), 1)
    asked = jnp.where(row == lane, got_ref[pl.ds(5, DEVICES, stride=PIECE), :], 0.0)
    ids[...] = jnp.maximum(jnp.sum(asked, axis=0, keepdims=True).astype(i32), 0)
    to_scalars = pltpu.make_async_copy(ids, first_ref, sems.at[4])
    to_scalars.start()
    atoms_ref[...] = jnp.zeros_like(atoms_ref)
    for at, by in enumerate((-2, -1, 1, 2)):
        source = me - by

        @pl.when((source >= 0) & (source < DEVICES))
        def _(at=at, source=source):
            atoms_ref[0:5, at * CAP : (at + 1) * CAP] = got_ref[pl.ds(source * PIECE, 5), :]

    copies[0].wait()
    copies[1].wait()
    atoms = atoms_ref[...]
    basis = basis_of(waves_of(freq, phase, flat), atoms)
    basis_ref[...] = basis
    both = poles(basis, atoms[3:4, :], cell_hot(atoms[4:5, :].astype(i32)))
    copies[2].wait()
    pole = stay[...] + both
    pole_ref[...] = pole
    outs = load(out_sems, (atoms_ref, atoms_hbm), (basis_ref, basis_hbm), (pole_ref, pole_hbm))
    ring[0:CELLS, :] = pole
    ring[CELLS:WRAP, :] = pole[0 : WRAP - CELLS, :]
    grouped = jnp.sum(pole.reshape(CELLS // 8, 8, LANES), axis=0)
    copies[3].wait()
    raised = up[...].reshape(COEF, OPS, COEF) * grouped[None, :, :COEF]
    turned[...] = jnp.zeros_like(turned)
    turned[0:COEF, 0:COEF] = jnp.sum(raised, axis=1)
    coarse = jnp.sum(turned[...].T, axis=0, keepdims=True)
    to_scalars.wait()

    def one(t, _):
        send_ref[pl.ds(t * BLOCK, SHORT), :] = ring[pl.ds(first_ref[0, t], SHORT), :]
        send_ref[pl.ds(t * BLOCK + SHORT, 1), :] = coarse
        return 0

    lax.fori_loop(0, DEVICES, one, 0, unroll=8)
    odd = lax.rem(me, 2)
    mate = me + 1 - 2 * odd
    other = jnp.clip(me - 1 + 2 * odd, 0, DEVICES - 1)
    mate_ref[...] = ring[pl.ds(first_ref[0, mate] + SHORT, EXTRA), :]
    other_ref[...] = ring[pl.ds(first_ref[0, other] + SHORT, EXTRA), :]
    for copy in outs:
        copy.wait()


def load_ops(ops_ref, both):
    both[...] = jnp.zeros_like(both)
    for o in range(OPS):
        high, low = split(ops_ref[pl.ds(o, COEF, stride=OPS), :])
        for at, part in enumerate((high, high, low)):
            both[o * LANES : o * LANES + COEF, at * LANES : at * LANES + COEF] = part


def premultiply(rows, both, table, at, pitch):
    high, low = split(rows)
    parts = jnp.concatenate([high, low, high], axis=1)
    for o in range(0, OPS, 2):
        pair = both[o * LANES : (o + 2) * LANES, :]
        out = lax.dot_general(parts, pair, NT, preferred_element_type=f32)
        for k in range(2):
            table[pl.ds((o + k) * pitch + at, rows.shape[0]), :] = out[:, k * LANES : (k + 1) * LANES]


def index_of(index_ref, l, r, g):
    return index_ref.at[pl.ds(l * CELLS + r * LANES, LANES)][g]


def row_sums(index_ref, table, count, first, last, start, store):
    def pair(p, _):
        for g in (2 * p, 2 * p + 1):
            for r in range(8):
                total = None if start is None else start(r, g)
                for l in range(count):
                    row = table[pl.ds(index_of(index_ref, l, r, g), 1), :]
                    total = row if total is None else total + row
                store(r, g, jnp.zeros((1, LANES), f32) if total is None else total)
        return 0

    lax.fori_loop(first, last, pair, 0)


def cross_kernel(stay_hbm, new_hbm, stay_pair_hbm, pair_hbm, atoms_ref, pair_ref, *rest):
    *pair_buffers, sems, out_sems = rest
    copies = load(
        sems, (stay_hbm, atoms_ref.at[:, pl.ds(0, STAY)]), (new_hbm, atoms_ref.at[:, pl.ds(STAY, ARRIVE)]),
        (stay_pair_hbm, pair_ref.at[:, pl.ds(0, STAY)]),
    )
    pair_ref[:, STAY:] = jnp.zeros((1, ARRIVE), f32)
    for copy in copies:
        copy.wait()
    pairs = Pairs(atoms_ref, pair_ref, *pair_buffers, STAY)

    def strip(c, _):
        at = pl.multiple_of(c * TALL, TALL)
        pairs.block(at, STAY, False)
        for lo in range(0, STAY, WIDE):
            pairs.block(at, lo, True)
        return 0

    lax.fori_loop(0, ARRIVE // TALL, strip, 0)
    pairs.close()
    (out,) = load(out_sems, (pair_ref, pair_hbm))
    out.wait()


def mid_kernel(own_hbm, count_ref, pole_hbm, ops_hbm, sum_hbm, own_ref, table, both, ops, pole, sum_ref, sems):
    copies = load(sems, (ops_hbm, ops), (pole_hbm, pole), (own_hbm, own_ref))
    table[OPS * CELLS :, :] = jnp.zeros((8, LANES), f32)
    copies[0].wait()
    load_ops(ops, both)
    copies[1].wait()
    width = CELLS
    for lo in range(0, CELLS, width):
        premultiply(pole[lo : lo + width, :], both, table, lo, CELLS)
    copies[2].wait()

    def store(r, g, total):
        sum_ref[pl.ds(r * LANES + g, 1), :] = total

    for n in range(LIST + 1):
        first = 0 if n == 0 else count_ref[LANES + n - 1]
        row_sums(own_ref, table, n, first, count_ref[LANES + n], None, store)
    out = pltpu.make_async_copy(sum_ref, sum_hbm, sems.at[3])
    out.start()
    out.wait()


def last_kernel(
    me_ref, index_hbm, count_ref, place_ref, far_ref, near_ref, next_ref, ops, sum_hbm, inner_hbm, outer_hbm,
    down_hbm, stay_hbm, new_hbm, stay_basis_hbm, new_basis_hbm, pair_hbm, local_ref, pot_ref,
    index_ref, table, both, sums_ref, rows, coarse, inner, outer, down, atoms_ref, basis_ref, pair, sems,
):
    copies = load(
        sems, (sum_hbm, sums_ref), (inner_hbm, inner), (outer_hbm, outer), (down_hbm, down),
        (stay_hbm, atoms_ref.at[:, pl.ds(0, STAY)]), (new_hbm, atoms_ref.at[:, pl.ds(STAY, ARRIVE)]),
        (stay_basis_hbm, basis_ref.at[:, pl.ds(0, STAY)]), (new_basis_hbm, basis_ref.at[:, pl.ds(STAY, ARRIVE)]),
        (pair_hbm, pair), (index_hbm, index_ref),
    )
    table[OPS * REMOTE :, :] = jnp.zeros((8, LANES), f32)
    load_ops(ops, both)
    width = FAR_ROWS // 2
    for lo in range(0, FAR_ROWS, width):
        premultiply(far_ref[lo : lo + width, :], both, table, lo, REMOTE)
    premultiply(near_ref[...], both, table, FAR_ROWS, REMOTE)
    premultiply(next_ref[...], both, table, FAR_ROWS + EXTRA, REMOTE)

    coarse[...] = far_ref[pl.ds(SHORT, DEVICES, stride=BLOCK), :]
    me = me_ref[0]
    group, member = me // MEMBERS, lax.rem(me, MEMBERS)
    who = lax.broadcasted_iota(i32, (40, DEVICES), 1)
    which = lax.broadcasted_iota(i32, (40, DEVICES), 0)
    its_group, its_member = who // MEMBERS, lax.rem(who, MEMBERS)
    near = (its_group == group) & (jnp.abs(its_member - member) - 1 == which) & (which < MEMBERS)
    away = (jnp.abs(its_group - group) - 1 == which - MEMBERS) & (which >= MEMBERS)
    chosen = jnp.where(near | away, 1.0, 0.0)
    sums = lax.dot_general(chosen, coarse[...], NN, precision=lax.Precision.HIGHEST, preferred_element_type=f32)
    for copy in copies[0:4]:
        copy.wait()
    field = jnp.sum(inner[...] * sums[None, 0 : MEMBERS - 1, 0:COEF], axis=1)
    for o in range(GROUPS - 1):
        field = field + outer[o] * sums[MEMBERS + o : MEMBERS + o + 1, 0:COEF]
    field = jnp.broadcast_to(jnp.sum(field, axis=1, keepdims=True), (COEF, LANES))
    child = lax.rem(lax.broadcasted_iota(i32, (COEF, LANES), 1), OPS)
    pattern = jnp.zeros((COEF, LANES), f32)
    for o in range(OPS):
        one = lax.dot_general(
            down[pl.ds(o, COEF, stride=OPS), :], field, NN,
            precision=lax.Precision.HIGHEST, preferred_element_type=f32,
        )
        pattern = jnp.where(child == o, one, pattern)

    def store(r, g, total):
        rows[pl.ds(place_ref.at[pl.ds(r * LANES, LANES)][g], 1), :] = total

    copies[9].wait()
    for n in range(LIST, -1, -1):
        row_sums(
            index_ref, table, n, count_ref[n + 1], count_ref[n], lambda r, g: sums_ref[pl.ds(r * LANES + g, 1), :], store
        )

    for lo in range(0, CELLS, LANES):
        local_ref[:, lo : lo + LANES] = rows[lo : lo + LANES, :].T[0:COEF, :] + pattern
    local = local_ref[...]
    high, rest = split(local)
    high = jnp.concatenate([high, jnp.zeros((LANES - COEF, CELLS), bf16)], axis=0)
    rest = jnp.concatenate([rest, jnp.zeros((LANES - COEF, CELLS), bf16)], axis=0)
    stacked = jnp.concatenate([high, rest], axis=0)
    for copy in copies[4:9]:
        copy.wait()
    wide = 512
    for lo in range(0, SLOTS, wide):
        cells, basis = atoms_ref[4:5, lo : lo + wide], basis_ref[:, lo : lo + wide]
        at = lax.dot_general(stacked, cell_hot(cells.astype(i32)), NN, preferred_element_type=f32)
        read = jnp.sum((at[:LANES] + at[LANES:]) * basis, axis=0, keepdims=True)
        read = read * COEF**-0.5 + pair[:, lo : lo + wide]
        for at in range(0, wide, LANES):
            i = (lo + at) // LANES
            pot_ref[i : i + 1, :] = read[:, at : at + LANES]


VM = pl.BlockSpec(memory_space=pltpu.VMEM)
SM = pl.BlockSpec(memory_space=pltpu.SMEM)
HB = pl.BlockSpec(memory_space=pltpu.HBM)


def call(kernel, name, ins, outs, scratch, copies, *operands):
    cost = pl.CostEstimate(flops=1000, bytes_accessed=1000, transcendentals=0)
    return pl.pallas_call(
        kernel,
        name=name,
        in_specs=ins,
        out_specs=[spec for spec, _, _ in outs],
        out_shape=[jax.ShapeDtypeStruct(shape, kind) for _, shape, kind in outs],
        scratch_shapes=[pltpu.VMEM(shape, kind) if isinstance(shape, tuple) else shape for shape, kind in scratch]
        + [pltpu.SemaphoreType.DMA((count,)) for count in copies],
        cost_estimate=cost,
        compiler_params=pltpu.CompilerParams(vmem_limit_bytes=LIMITS.get(name, 52) * MIB),
    )(*operands)


def on_device(
    atom_rows,
    atom_owner,
    atom_cell,
    need_cells,
    list_entry,
    list_class,
    basis_freq,
    basis_phase,
    near_ops,
    up_ops,
    far_in,
    far_out,
    down_ops,
):
    me = (lax.axis_index("group") * MEMBERS + lax.axis_index("dev")).reshape(1).astype(i32)
    freq, phase = basis_freq.T, basis_phase.reshape(1, COEF)
    waves = [((3, COEF), f32), ((1, COEF), f32)]
    owner_row, cell_row = atom_owner.reshape(1, STAY), atom_cell.reshape(1, STAY)
    by_row = [ops.transpose(1, 0, 2).reshape(COEF * OPS, COEF) for ops in (near_ops, up_ops, down_ops)]
    ops_shape = ((COEF * OPS, COEF), f32)
    mine = [((1, STAY), i32), ((4, STAY), f32), ((1, STAY), i32)]

    (outbound,) = call(
        pack_kernel, "pack", [SM, HB, HB, HB, HB], [(VM, (DEVICES * PIECE, LANES), f32)],
        [((8, LANES), i32), ((STAY // LANES, LANES), i32), *mine[1:], ((8, 512), f32)], [4],
        me, need_cells.transpose(0, 2, 1), atom_owner.reshape(STAY // LANES, LANES), atom_rows, cell_row,
    )
    got = lax.all_to_all(outbound.reshape(DEVICES, 1, PIECE * LANES), AXES, split_axis=0, concat_axis=0, tiled=True)
    got = got.reshape(DEVICES * PIECE, LANES)

    shape3, tile = (LIST, CELLS // LANES, LANES), (CELLS // LANES, LANES)
    early_outs = [
        ((8, STAY), f32), ((LANES, STAY), f32), ((CELLS, LANES), f32), ((1, STAY), f32),
        (shape3, i32), (shape3, i32), (tile, i32), (tile, i32),
    ]
    stay_atoms, stay_basis, stay_pole, stay_pair, own_index, far_index, place, counts = call(
        early_kernel, "early", [SM] + [HB] * 7, [(HB, *out) for out in early_outs],
        [*mine, *waves, *[((LIST, CELLS), i32)] * 2, *[(shape3, i32)] * 2, ((80, CELLS), f32), ((8, LANES), f32), *early_outs,
         *pair_scratch(STAY, STAY)], [7, 8],
        me, owner_row, atom_rows, cell_row, freq, phase, list_entry, list_class,
    )
    own_index, far_index, place, counts = (one.reshape(-1) for one in (own_index, far_index, place, counts))
    merge_outs = [((CELLS, LANES), f32), ((LANES, ARRIVE), f32), ((8, ARRIVE), f32)]
    send, mate_rows, other_rows, pole, new_basis, new_atoms = call(
        merge_kernel, "merge", [SM, VM] + [HB] * 4,
        [(VM, (FAR_ROWS, LANES), f32), (VM, (EXTRA, LANES), f32), (VM, (EXTRA, LANES), f32), *[(HB, *out) for out in merge_outs]],
        [*waves, ((CELLS, LANES), f32), ops_shape, ((8, LANES), f32), *merge_outs[::-1],
         ((WRAP, LANES), f32), ((LANES, LANES), f32), ((1, LANES), i32), (pltpu.SMEM((1, LANES), i32), None)],
        [5, 3],
        me, got, freq, phase, stay_pole, by_row[1],
    )
    far_rows = lax.all_to_all(send.reshape(DEVICES, 1, BLOCK * LANES), AXES, split_axis=0, concat_axis=0, tiled=True)
    far_rows = far_rows.reshape(FAR_ROWS, LANES)
    near_rows, next_rows = swap(mate_rows, 0), swap(other_rows, 1)
    (pair,) = call(
        cross_kernel, "cross", [HB] * 3, [(HB, (1, SLOTS), f32)],
        [((8, SLOTS), f32), ((1, SLOTS), f32), *pair_scratch(SLOTS, ARRIVE)], [3, 1],
        stay_atoms, new_atoms, stay_pair,
    )
    index_scratch = (pltpu.SMEM((LIST * CELLS,), i32), None)
    (own_sum,) = call(
        mid_kernel, "mid", [HB, SM, HB, HB], [(HB, (CELLS, LANES), f32)],
        [index_scratch, ((OPS * CELLS + 8, LANES), f32), ((OPS * LANES, 3 * LANES), bf16), ops_shape, *[((CELLS, LANES), f32)] * 2],
        [4],
        own_index, counts, pole, by_row[0],
    )
    local, pot = call(
        last_kernel, "last", [SM, HB, SM, SM] + [VM] * 4 + [HB] * 9, [(VM, (COEF, CELLS), f32), (VM, (SLOTS // LANES, LANES), f32)],
        [index_scratch, ((OPS * REMOTE + 8, LANES), f32), ((OPS * LANES, 3 * LANES), bf16), *[((CELLS, LANES), f32)] * 2, ((DEVICES, LANES), f32),
         ((COEF, MEMBERS - 1, COEF), f32), ((GROUPS - 1, COEF, COEF), f32), ops_shape, ((8, SLOTS), f32),
         ((LANES, SLOTS), f32), ((1, SLOTS), f32)],
        [10],
        me, far_index, counts, place, far_rows, near_rows, next_rows, by_row[0], own_sum,
        far_in.transpose(1, 0, 2), far_out, by_row[2], stay_atoms, new_atoms, stay_basis, new_basis, pair,
    )
    return local, pot.reshape(SLOTS)


def solution(mesh):
    in_specs = (
        P(None, AXES),
        P(AXES),
        P(AXES),
        P(AXES, None, None),
        P(None, AXES),
        P(None, AXES),
        P(),
        P(),
        P(),
        P(),
        P(),
        P(),
        P(),
    )
    out_specs = (P(None, AXES), P(AXES))
    return jax.shard_map(on_device, mesh=mesh, in_specs=in_specs, out_specs=out_specs, check_vma=False)
```
